128 devices in a mesh: frame: 64 (over x_hi, y, z, core), video: 2 (over x_lo).
Axes of the slice: x: 4 (x_hi: 2, x_lo: 2; x = x_hi * 2 + x_lo), y: 4, z: 4, core: 2. Of those that a mesh axis runs over, the one named last changes fastest.
Arguments:
- tokens_in: bfloat16 [2, 256, 197, 768], P('video', 'frame'), may hold values from -6 to 6
- clip_ids: int32 [2, 256], P('video', 'frame'), may hold values from 0 to 7, as said below
- grad_out: bfloat16 [2, 256, 197, 768], P('video', 'frame'), may hold values from -6 to 6
- msg_fc_w: bfloat16 [768, 768], P('frame'), may hold values from -0.21875 to 0.21875
- msg_fc_b: bfloat16 [768], P('frame'), may hold values from -1.75 to 1.75
- msg_norm_gain: bfloat16 [768], P('frame'), may hold values from 0.5 to 1.5
- msg_norm_shift: bfloat16 [768], P('frame'), may hold values from -1.75 to 1.75
- msg_qkv_w: bfloat16 [768, 2304], P('frame'), may hold values from -0.21875 to 0.21875
- msg_qv_b: bfloat16 [1536], P('frame'), may hold values from -1.75 to 1.75
- msg_out_w: bfloat16 [768, 768], P('frame'), may hold values from -0.4375 to 0.4375
- msg_out_b: bfloat16 [768], P('frame'), may hold values from -1.75 to 1.75
- norm1_gain: bfloat16 [768], P('frame'), may hold values from 0.5 to 1.5
- norm1_shift: bfloat16 [768], P('frame'), may hold values from -1.75 to 1.75
- attn_qkv_w: bfloat16 [768, 2304], P('frame'), may hold values from -0.21875 to 0.21875
- attn_qv_b: bfloat16 [1536], P('frame'), may hold values from -1.75 to 1.75
- attn_out_w: bfloat16 [768, 768], P('frame'), may hold values from -0.625 to 0.625
- attn_out_b: bfloat16 [768], P('frame'), may hold values from -1.75 to 1.75
- norm2_gain: bfloat16 [768], P('frame'), may hold values from 0.5 to 1.5
- norm2_shift: bfloat16 [768], P('frame'), may hold values from -1.75 to 1.75
- mlp_in_w: bfloat16 [768, 3072], P('frame'), may hold values from -0.21875 to 0.21875
- mlp_in_b: bfloat16 [3072], P('frame'), may hold values from -1.75 to 1.75
- mlp_out_w: bfloat16 [3072, 768], P('frame'), may hold values from -0.109375 to 0.109375
- mlp_out_b: bfloat16 [768], P('frame'), may hold values from -1.75 to 1.75
Outputs:
- layer_out: bfloat16 [2, 256, 197, 768], P('video', 'frame')
- grad_tokens: float32 [2, 256, 197, 768], P('video', 'frame')
- grad_msg_fc_w: float32 [768, 768], P('frame')
- grad_msg_fc_b: float32 [768], P('frame')
- grad_msg_norm_gain: float32 [768], P('frame')
- grad_msg_norm_shift: float32 [768], P('frame')
- grad_msg_qkv_w: float32 [768, 2304], P('frame')
- grad_msg_qv_b: float32 [1536], P('frame')
- grad_msg_out_w: float32 [768, 768], P('frame')
- grad_msg_out_b: float32 [768], P('frame')
- grad_norm1_gain: float32 [768], P('frame')
- grad_norm1_shift: float32 [768], P('frame')
- grad_attn_qkv_w: float32 [768, 2304], P('frame')
- grad_attn_qv_b: float32 [1536], P('frame')
- grad_attn_out_w: float32 [768, 768], P('frame')
- grad_attn_out_b: float32 [768], P('frame')
- grad_norm2_gain: float32 [768], P('frame')
- grad_norm2_shift: float32 [768], P('frame')
- grad_mlp_in_w: float32 [768, 3072], P('frame')
- grad_mlp_in_b: float32 [3072], P('frame')
- grad_mlp_out_w: float32 [3072, 768], P('frame')
- grad_mlp_out_b: float32 [768], P('frame')
The draws below stay inside these ranges and needn't reach their ends.
Inputs may be any that keep to these rules, and one draw needn't show every extreme that they name: `clip_ids`: in every video, frame 0, frame 256 // 2 and the last frame share one clip group drawn from the seed.
All inputs are finite; a program needn't handle non-finite values.
Results may differ from the reference program's by a relative error of at most 0.03.
Values may be sent and summed in bfloat16 or wider, within the bound.
No kernel may reach another device: no remote copies, remote signals or barrier semaphores. Data moves between devices by JAX's collectives and lax.ppermute only.
A program may use at most 256 MiB of HBM per device.

```python
import jax
import jax.numpy as jnp
from jax import lax

D = 768
FF = 3072
TOK = 197
HEAD_DIM = 64
CLIPS = 8
FRAMES = 256
VIDEOS = 2


def draw_clip_ids(key, part):
    key = jax.random.fold_in(key, 7)
    first_key, second_key = jax.random.split(key)
    groups = jax.random.randint(first_key, (VIDEOS, FRAMES), 0, CLIPS)
    groups = groups.at[:, 1].set(CLIPS - 1).at[:, 2].set(0)
    spanning = jax.random.randint(second_key, (VIDEOS, 1), 0, CLIPS)
    middle = FRAMES // 2
    groups = groups.at[:, 0:1].set(spanning)
    groups = groups.at[:, middle:middle + 1].set(spanning)
    groups = groups.at[:, FRAMES - 1:FRAMES].set(spanning)
    return groups.astype(jnp.int32)


def shard_levels(stream_key, extent, cuts, least, largest):
    level = 1.0
    for position, shards_of in cuts:
        steps = jax.random.uniform(jax.random.fold_in(jax.random.fold_in(stream_key, 6), position), (shards_of,), jnp.float32, least / len(cuts), largest / len(cuts))
        level = level * jnp.repeat(jnp.exp(steps), extent[position] // shards_of).reshape((-1,) + (1,) * (len(extent) - 1 - position))
    return level


def gaussian(own_key, shape, deviation, limit, cuts=(), held_as=jnp.bfloat16):
    values = jax.random.normal(own_key, shape, jnp.float32) * deviation
    if len(cuts) > 0:
        values = shard_levels(own_key, shape, cuts, -0.22, 0.18) * values
    return jnp.clip(values, min=-limit, max=limit).astype(held_as)


def setup_inputs(seed: int = 0) -> dict:
    streams_of = jax.random.split(jax.random.key(seed), 24)
    return {
        "tokens_in": gaussian(streams_of[0], (VIDEOS, FRAMES, TOK, D), 1.0, 6.0, ((0, 2), (1, 64))),
        "clip_ids": draw_clip_ids(jax.random.fold_in(streams_of[23], 71), 0),
        "grad_out": gaussian(streams_of[2], (VIDEOS, FRAMES, TOK, D), 1.0, 6.0, ((0, 2), (1, 64))),
        "msg_fc_w": gaussian(streams_of[3], (D, D), D ** -0.5, 0.21875, ((0, 64),)),
        "msg_fc_b": gaussian(streams_of[4], (D,), 0.3, 1.75, ((0, 64),)),
        "msg_norm_gain": jnp.clip(1.0 + 0.1 * jax.random.normal(streams_of[5], (D,), jnp.float32), 0.5, 1.5).astype(jnp.bfloat16),
        "msg_norm_shift": gaussian(streams_of[6], (D,), 0.3, 1.75, ((0, 64),)),
        "msg_qkv_w": gaussian(streams_of[7], (D, 3 * D), D ** -0.5, 0.21875, ((0, 64),)),
        "msg_qv_b": gaussian(streams_of[8], (2 * D,), 0.3, 1.75, ((0, 64),)),
        "msg_out_w": gaussian(streams_of[9], (D, D), (D // 4) ** -0.5, 0.4375, ((0, 64),)),
        "msg_out_b": gaussian(streams_of[10], (D,), 0.3, 1.75, ((0, 64),)),
        "norm1_gain": jnp.clip(1.0 + 0.1 * jax.random.normal(streams_of[11], (D,), jnp.float32), 0.5, 1.5).astype(jnp.bfloat16),
        "norm1_shift": gaussian(streams_of[12], (D,), 0.3, 1.75, ((0, 64),)),
        "attn_qkv_w": gaussian(streams_of[13], (D, 3 * D), D ** -0.5, 0.21875, ((0, 64),)),
        "attn_qv_b": gaussian(streams_of[14], (2 * D,), 0.3, 1.75, ((0, 64),)),
        "attn_out_w": gaussian(streams_of[15], (D, D), (D // 8) ** -0.5, 0.625, ((0, 64),)),
        "attn_out_b": gaussian(streams_of[16], (D,), 0.3, 1.75, ((0, 64),)),
        "norm2_gain": jnp.clip(1.0 + 0.1 * jax.random.normal(streams_of[17], (D,), jnp.float32), 0.5, 1.5).astype(jnp.bfloat16),
        "norm2_shift": gaussian(streams_of[18], (D,), 0.3, 1.75, ((0, 64),)),
        "mlp_in_w": gaussian(streams_of[19], (D, FF), D ** -0.5, 0.21875, ((0, 64),)),
        "mlp_in_b": gaussian(streams_of[20], (FF,), 0.3, 1.75, ((0, 64),)),
        "mlp_out_w": gaussian(streams_of[21], (FF, D), FF ** -0.5, 0.109375, ((0, 64),)),
        "mlp_out_b": gaussian(streams_of[22], (D,), 0.3, 1.75, ((0, 64),)),
    }


HIGHEST = lax.Precision.HIGHEST

@jax.custom_vjp
def low(v):
    return lax.optimization_barrier(v.astype(jnp.bfloat16)).astype(jnp.float32)

@jax.custom_vjp
def low_back(v):
    return v

def low_keep(v):
    return (low(v), None)

def low_pass(kept, grad):
    return (grad,)

def back_keep(v):
    return (v, None)

def back_low(kept, grad):
    return (low(grad),)
low.defvjp(low_keep, low_pass)
low_back.defvjp(back_keep, back_low)

def both_round(value):
    return low_back(low(value))

def matmul_high(left, right):
    return jnp.matmul(left, right, precision=HIGHEST)

def layer_norm(value, gain, shift):
    center = value - lax.optimization_barrier(jnp.mean(value, -1, keepdims=True))
    inverse = lax.rsqrt(lax.optimization_barrier(jnp.mean(center * center, -1, keepdims=True)) + 1e-05)
    return center * inverse * gain + shift

def softmax_rows(scores):
    peak = lax.optimization_barrier(jnp.max(scores, -1, keepdims=True))
    raised = jnp.exp(scores - peak)
    return raised / lax.optimization_barrier(jnp.sum(raised, -1, keepdims=True))

def attend(normed, qkv_weight, qv_bias, model_width):
    row_count = normed.shape[0]
    head_count = model_width // HEAD_DIM
    project = matmul_high(normed, qkv_weight)
    queries = both_round(project[:, :model_width] + qv_bias[:model_width]).reshape(row_count, head_count, HEAD_DIM)
    key_rows = both_round(project[:, model_width:2 * model_width]).reshape(row_count, head_count, HEAD_DIM)
    value_rows = both_round(project[:, 2 * model_width:] + qv_bias[model_width:]).reshape(row_count, head_count, HEAD_DIM)
    scores = low_back(jnp.einsum('qhd,khd->hqk', queries, key_rows, precision=HIGHEST) * HEAD_DIM ** (-0.5))
    return (scores, value_rows)

def frame_block(frame_rows, weights):
    norm1_gain, norm1_shift, attn_qkv_w, attn_qv_b, attn_out_w, attn_out_b, norm2_gain, norm2_shift, mlp_in_w, mlp_in_b, mlp_out_w, mlp_out_b = weights
    model_width = frame_rows.shape[-1]
    row_count = frame_rows.shape[0]
    normed = low(layer_norm(frame_rows, norm1_gain, norm1_shift))
    scores, value_rows = attend(normed, attn_qkv_w, attn_qv_b, model_width)
    attn_probs = low(softmax_rows(scores))
    mixed_rows = both_round(jnp.einsum('hqk,khd->qhd', attn_probs, value_rows, precision=HIGHEST).reshape(row_count, model_width))
    branch = low_back(matmul_high(mixed_rows, attn_out_w) + attn_out_b)
    kept = (frame_rows + branch)[:TOK]
    normed_two = low(layer_norm(kept, norm2_gain, norm2_shift))
    hidden = low_back(matmul_high(normed_two, mlp_in_w) + mlp_in_b)
    active = both_round(hidden * jax.nn.sigmoid(1.702 * hidden))
    return kept + matmul_high(active, mlp_out_w) + mlp_out_b

def video_forward(tokens, groups, weights):
    msg_fc_w, msg_fc_b, msg_norm_gain, msg_norm_shift, msg_qkv_w, msg_qv_b, msg_out_w, msg_out_b = weights[:8]
    model_width = tokens.shape[-1]
    frame_count = tokens.shape[0]
    message = low_back(matmul_high(tokens[:, 0, :], msg_fc_w) + msg_fc_b)
    normed = low(layer_norm(message, msg_norm_gain, msg_norm_shift))
    scores, value_rows = attend(normed, msg_qkv_w, msg_qv_b, model_width)
    same_group = groups[:, None] == groups[None, :]
    scores = jnp.where(same_group[None], scores, -1000000000.0)
    attn_probs = low(softmax_rows(scores))
    mixed_rows = both_round(jnp.einsum('hqk,khd->qhd', attn_probs, value_rows, precision=HIGHEST).reshape(frame_count, model_width))
    message = message + low_back(matmul_high(mixed_rows, msg_out_w) + msg_out_b)
    joined = jnp.concatenate([tokens, message[:, None, :]], axis=1)
    frame_weights = weights[8:]
    block = jax.checkpoint(lambda frame_rows: frame_block(frame_rows, frame_weights))
    return lax.map(block, joined)

def reference(tokens_in, clip_ids, grad_out, msg_fc_w, msg_fc_b, msg_norm_gain, msg_norm_shift, msg_qkv_w, msg_qv_b, msg_out_w, msg_out_b, norm1_gain, norm1_shift, attn_qkv_w, attn_qv_b, attn_out_w, attn_out_b, norm2_gain, norm2_shift, mlp_in_w, mlp_in_b, mlp_out_w, mlp_out_b):
    weights = tuple((weight.astype(jnp.float32) for weight in (msg_fc_w, msg_fc_b, msg_norm_gain, msg_norm_shift, msg_qkv_w, msg_qv_b, msg_out_w, msg_out_b, norm1_gain, norm1_shift, attn_qkv_w, attn_qv_b, attn_out_w, attn_out_b, norm2_gain, norm2_shift, mlp_in_w, mlp_in_b, mlp_out_w, mlp_out_b)))
    totals = tuple((jnp.zeros_like(weight) for weight in weights))
    results = []
    input_grads = []
    for video in range(VIDEOS):
        groups = clip_ids[video]
        result, pullback = jax.vjp(lambda tokens, params: video_forward(tokens, groups, params), tokens_in[video].astype(jnp.float32), weights)
        grad_tok, grad_params = pullback(grad_out[video].astype(jnp.float32))
        results.append(result)
        input_grads.append(grad_tok)
        totals = tuple((total + part_grad for total, part_grad in zip(totals, grad_params)))
    layer_out = jnp.stack(results).astype(jnp.bfloat16)
    grad_tokens = jnp.stack(input_grads)
    return (layer_out, grad_tokens, totals[0], totals[1], totals[2], totals[3], totals[4], totals[5], totals[6], totals[7], totals[8], totals[9], totals[10], totals[11], totals[12], totals[13], totals[14], totals[15], totals[16], totals[17], totals[18], totals[19])
```

```python
import itertools

import jax
import jax.numpy as jnp
from jax import lax
from jax.sharding import PartitionSpec as P

HEAD_DIM = 64


def narrow(value):
    return value.astype(jnp.bfloat16)


def product(left, right):
    return jnp.dot(left, right, preferred_element_type=jnp.float32)


def product_left_t(left, right):
    return lax.dot_general(
        left, right, (((0,), (0,)), ((), ())), preferred_element_type=jnp.float32
    )


def product_right_t(left, right):
    return lax.dot_general(
        left, right, (((1,), (1,)), ((), ())), preferred_element_type=jnp.float32
    )


def norm_parts(value):
    center = value - jnp.mean(value, -1, keepdims=True)
    inverse = lax.rsqrt(jnp.mean(center * center, -1, keepdims=True) + 1e-05)
    return (center * inverse, inverse)


def norm_back(grad_normed, normed, inverse, gain):
    scaled = grad_normed * gain
    return inverse * (
        scaled
        - jnp.mean(scaled, -1, keepdims=True)
        - normed * jnp.mean(scaled * normed, -1, keepdims=True)
    )


def softmax_rows(scores):
    peak = jnp.max(scores, -1, keepdims=True)
    raised = jnp.exp(scores - peak)
    return raised / jnp.sum(raised, -1, keepdims=True)


def column_sums(value):
    return jnp.sum(value.astype(jnp.float32), 0)


def wide_of(value):
    return value.astype(jnp.float32)


def frame_of(x_hi, y, z, core):
    return ((x_hi * 4 + y) * 4 + z) * 2 + core


PLACES = list(itertools.product(range(2), range(4), range(4), range(2), range(2)))


def moves(to):
    return [(frame_of(*p[:4]) * 2 + p[4], frame_of(*to(*p)[:4]) * 2 + to(*p)[4]) for p in PLACES]


TO_CORE = moves(lambda x, y, z, c, v: (x, y, z, 1 - c, v))
TO_VIDEO = moves(lambda x, y, z, c, v: (x, y, z, c, 1 - v))
TO_HALF = moves(lambda x, y, z, c, v: (1 - x, y, z, c, v))
TO_BOTH = moves(lambda x, y, z, c, v: (1 - x, y, z, c, 1 - v))
ALONG_Z = [[frame_of(x, y, z, c) for z in range(4)] for x in range(2) for y in range(4) for c in range(2)]
ALONG_Y = [[frame_of(x, y, z, c) for y in range(4)] for x in range(2) for z in range(4) for c in range(2)]


def sent(x, pairs):
    return lax.ppermute(x, ("frame", "video"), pairs)


def ring_sum(x, groups):
    got = lax.all_to_all(x, "frame", 0, 0, axis_index_groups=groups, tiled=True)
    return narrow(jnp.sum(wide_of(got), 0))


def scattered(grad, z_first):
    place = lax.axis_index("frame")
    core, half = place % 2, place // 32
    r, n = grad.shape[0] // 64, grad.shape[1]
    parts = grad.reshape(2, 4, 4, 2, r, n)
    parts = parts.transpose((3, 2, 1, 0, 4, 5) if z_first else (3, 1, 2, 0, 4, 5))
    give = lax.dynamic_index_in_dim(parts, 1 - core, 0, keepdims=False)
    keep = lax.dynamic_index_in_dim(parts, core, 0, keepdims=False)
    part = narrow(wide_of(keep) + wide_of(sent(give, TO_CORE)))
    part = ring_sum(part, ALONG_Z if z_first else ALONG_Y)
    part = ring_sum(part, ALONG_Y if z_first else ALONG_Z)
    mine = lax.dynamic_index_in_dim(part, half, 0, keepdims=False)
    other = lax.dynamic_index_in_dim(part, 1 - half, 0, keepdims=False)
    return (
        wide_of(mine)
        + wide_of(sent(mine, TO_VIDEO))
        + wide_of(sent(other, TO_HALF))
        + wide_of(sent(other, TO_BOTH))
    )


def to_everyone(x):
    return lax.all_to_all(jnp.broadcast_to(x[None], (64, *x.shape)), "frame", 0, 0, tiled=True)

def shards(
    tokens_in,
    clip_ids,
    grad_out,
    msg_fc_w,
    msg_fc_b,
    msg_norm_gain,
    msg_norm_shift,
    msg_qkv_w,
    msg_qv_b,
    msg_out_w,
    msg_out_b,
    norm1_gain,
    norm1_shift,
    attn_qkv_w,
    attn_qv_b,
    attn_out_w,
    attn_out_b,
    norm2_gain,
    norm2_shift,
    mlp_in_w,
    mlp_in_b,
    mlp_out_w,
    mlp_out_b,
):
    place = lax.axis_index("frame")
    wide = jnp.float32
    model_width = tokens_in.shape[-1]
    head_count = model_width // HEAD_DIM
    frames_here = tokens_in.shape[1]
    token_count = tokens_in.shape[2]
    length = token_count + 1
    score_factor = HEAD_DIM ** (-0.5)
    inputs = tokens_in[0]
    small = jnp.concatenate(
        [
            inputs[:, 0, :].reshape(-1),
            msg_fc_b,
            msg_norm_gain,
            msg_norm_shift,
            msg_out_b,
            norm1_gain,
            norm1_shift,
            attn_out_b,
            norm2_gain,
            norm2_shift,
            mlp_out_b,
            msg_qv_b,
            attn_qv_b,
            mlp_in_b,
            clip_ids[0].astype(jnp.bfloat16),
        ]
    )
    small = jnp.pad(small, (0, 4096 - small.shape[0])).reshape(32, 128)
    small_all = to_everyone(small).reshape(64, 4096)
    msg_weights = lax.all_gather(
        jnp.concatenate([msg_fc_w, msg_qkv_w, msg_out_w], 1), "frame", axis=0, tiled=True
    )
    attn_weights = lax.all_gather(
        jnp.concatenate([attn_qkv_w, attn_out_w], 1), "frame", axis=0, tiled=True
    )
    up_weight = lax.all_gather(mlp_in_w, "frame", axis=0, tiled=True)
    down_weight = lax.all_gather(mlp_out_w, "frame", axis=0, tiled=True)
    class_all = small_all[:, :3072].reshape(256, model_width)
    at = 3072
    vectors = []
    for size in [12] * 10 + [24, 24, 48, 4]:
        vectors.append(small_all[:, at : at + size].reshape(-1))
        at += size
    (
        fc_bias,
        mnorm_gain,
        mnorm_shift,
        mout_bias,
        gain_one,
        shift_one,
        out_bias,
        gain_two,
        shift_two,
        down_bias,
        mqv_bias,
        qv_bias,
        up_bias,
        group_all,
    ) = vectors
    fc_weight, mqkv_weight, mout_weight = jnp.split(msg_weights, [768, 3072], 1)
    qkv_weight, out_weight = jnp.split(attn_weights, [2304], 1)
    message = product(class_all, fc_weight) + fc_bias.astype(wide)
    msg_normed, msg_inverse = norm_parts(message)
    msg_input = narrow(msg_normed * mnorm_gain.astype(wide) + mnorm_shift.astype(wide))
    msg_project = product(msg_input, mqkv_weight)
    msg_query = narrow(msg_project[:, :model_width] + mqv_bias[:model_width].astype(wide))
    msg_key = narrow(msg_project[:, model_width : 2 * model_width])
    msg_value = narrow(msg_project[:, 2 * model_width :] + mqv_bias[model_width:].astype(wide))
    frame_total = class_all.shape[0]
    query_heads = msg_query.reshape(frame_total, head_count, HEAD_DIM)
    key_heads = msg_key.reshape(frame_total, head_count, HEAD_DIM)
    value_heads = msg_value.reshape(frame_total, head_count, HEAD_DIM)
    same_group = (group_all[:, None] == group_all[None, :])[None]
    msg_scores = (
        jnp.einsum("qhd,khd->hqk", query_heads, key_heads, preferred_element_type=wide)
        * score_factor
    )
    msg_scores = jnp.where(same_group, msg_scores, -1000000000.0)
    msg_probs = softmax_rows(msg_scores)
    msg_probs_low = narrow(msg_probs)
    msg_mixed = narrow(
        jnp.einsum("hqk,khd->qhd", msg_probs_low, value_heads, preferred_element_type=wide).reshape(
            frame_total, model_width
        )
    )
    message_all = message + product(msg_mixed, mout_weight) + mout_bias.astype(wide)
    message_token = lax.dynamic_slice_in_dim(message_all, place * frames_here, frames_here)
    joined = jnp.concatenate([inputs.astype(wide), message_token[:, None, :]], axis=1)
    normed_one, inverse_one = norm_parts(joined)
    block_input = narrow(normed_one * gain_one.astype(wide) + shift_one.astype(wide)).reshape(
        frames_here * length, model_width
    )
    project = product(block_input, qkv_weight)
    head_shape = (frames_here, length, head_count, HEAD_DIM)
    queries = narrow(project[:, :model_width] + qv_bias[:model_width].astype(wide)).reshape(
        head_shape
    )
    key_rows = narrow(project[:, model_width : 2 * model_width]).reshape(head_shape)
    value_rows = narrow(project[:, 2 * model_width :] + qv_bias[model_width:].astype(wide)).reshape(
        head_shape
    )
    scores = (
        jnp.einsum("fqhd,fkhd->fhqk", queries, key_rows, preferred_element_type=wide) * score_factor
    )
    attn_probs = softmax_rows(scores)
    probs_low = narrow(attn_probs)
    mixed_rows = narrow(
        jnp.einsum("fhqk,fkhd->fqhd", probs_low, value_rows, preferred_element_type=wide).reshape(
            frames_here * length, model_width
        )
    )
    branch = product(mixed_rows, out_weight) + out_bias.astype(wide)
    residual = joined + branch.reshape(frames_here, length, model_width)
    kept = residual[:, :token_count]
    normed_two, inverse_two = norm_parts(kept)
    mlp_input = narrow(normed_two * gain_two.astype(wide) + shift_two.astype(wide)).reshape(
        frames_here * token_count, model_width
    )
    hidden = product(mlp_input, up_weight) + up_bias.astype(wide)
    sigmoid_part = jax.nn.sigmoid(1.702 * hidden)
    active = narrow(hidden * sigmoid_part)
    layer_out = kept + (product(active, down_weight) + down_bias.astype(wide)).reshape(
        frames_here, token_count, model_width
    )
    grad_low = grad_out[0].reshape(frames_here * token_count, model_width)
    grad_rows = grad_low.astype(wide)
    grad_down_weight = product_left_t(active, grad_low)
    grad_down_bias = jnp.sum(grad_rows, 0)
    grad_active = narrow(product_right_t(grad_low, down_weight)).astype(wide)
    grad_hidden = narrow(
        grad_active * (sigmoid_part + 1.702 * hidden * sigmoid_part * (1.0 - sigmoid_part))
    )
    grad_up_weight = product_left_t(mlp_input, grad_hidden)
    grad_up_bias = column_sums(grad_hidden)
    grad_mlp_in = product_right_t(grad_hidden, up_weight).reshape(
        frames_here, token_count, model_width
    )
    grad_gain_two = jnp.sum(grad_mlp_in * normed_two, (0, 1))
    grad_shift_two = jnp.sum(grad_mlp_in, (0, 1))
    grad_kept = grad_rows.reshape(frames_here, token_count, model_width) + norm_back(
        grad_mlp_in, normed_two, inverse_two, gain_two.astype(wide)
    )
    grad_resid = jnp.concatenate(
        [grad_kept, jnp.zeros((frames_here, 1, model_width), wide)], axis=1
    )
    grad_branch = narrow(grad_resid).reshape(frames_here * length, model_width)
    grad_out_weight = product_left_t(mixed_rows, grad_branch)
    grad_out_bias = column_sums(grad_branch)
    grad_mixed = narrow(product_right_t(grad_branch, out_weight)).reshape(head_shape)
    grad_probs = jnp.einsum("fqhd,fkhd->fhqk", grad_mixed, value_rows, preferred_element_type=wide)
    grad_values = narrow(
        jnp.einsum("fhqk,fqhd->fkhd", probs_low, grad_mixed, preferred_element_type=wide)
    )
    grad_scores = narrow(
        attn_probs * (grad_probs - jnp.sum(grad_probs * attn_probs, -1, keepdims=True))
    )
    grad_queries = narrow(
        jnp.einsum("fhqk,fkhd->fqhd", grad_scores, key_rows, preferred_element_type=wide)
        * score_factor
    )
    grad_keys = narrow(
        jnp.einsum("fhqk,fqhd->fkhd", grad_scores, queries, preferred_element_type=wide)
        * score_factor
    )
    flat_shape = (frames_here * length, model_width)
    grad_project = jnp.concatenate(
        [
            grad_queries.reshape(flat_shape),
            grad_keys.reshape(flat_shape),
            grad_values.reshape(flat_shape),
        ],
        axis=1,
    )
    grad_qkv_weight = product_left_t(block_input, grad_project)
    project_sums = column_sums(grad_project)
    grad_qv_bias = jnp.concatenate([project_sums[:model_width], project_sums[2 * model_width :]])
    grad_block_in = product_right_t(grad_project, qkv_weight).reshape(
        frames_here, length, model_width
    )
    grad_gain_one = jnp.sum(grad_block_in * normed_one, (0, 1))
    grad_shift_one = jnp.sum(grad_block_in, (0, 1))
    grad_joined = grad_resid + norm_back(
        grad_block_in, normed_one, inverse_one, gain_one.astype(wide)
    )
    grad_message = grad_joined[:, token_count]
    grad_message = wide_of(to_everyone(narrow(grad_message))).reshape(frame_total, model_width)
    grad_msg_branch = narrow(grad_message)
    mine = lambda x: lax.dynamic_slice_in_dim(x, place * 12, 12, 1)
    grad_mout_weight = product_left_t(mine(msg_mixed), grad_msg_branch)
    grad_mout_bias = column_sums(grad_msg_branch)
    grad_msg_mixed = narrow(product_right_t(grad_msg_branch, mout_weight)).reshape(
        frame_total, head_count, HEAD_DIM
    )
    grad_msg_probs = jnp.einsum(
        "qhd,khd->hqk", grad_msg_mixed, value_heads, preferred_element_type=wide
    )
    grad_msg_value = narrow(
        jnp.einsum("hqk,qhd->khd", msg_probs_low, grad_msg_mixed, preferred_element_type=wide)
    ).reshape(frame_total, model_width)
    grad_msg_scores = narrow(
        msg_probs * (grad_msg_probs - jnp.sum(grad_msg_probs * msg_probs, -1, keepdims=True))
    )
    grad_msg_query = narrow(
        jnp.einsum("hqk,khd->qhd", grad_msg_scores, key_heads, preferred_element_type=wide)
        * score_factor
    ).reshape(frame_total, model_width)
    grad_msg_key = narrow(
        jnp.einsum("hqk,qhd->khd", grad_msg_scores, query_heads, preferred_element_type=wide)
        * score_factor
    ).reshape(frame_total, model_width)
    grad_msg_project = jnp.concatenate([grad_msg_query, grad_msg_key, grad_msg_value], axis=1)
    grad_mqkv_weight = product_left_t(mine(msg_input), grad_msg_project)
    msg_sums = column_sums(grad_msg_project)
    grad_mqv_bias = jnp.concatenate([msg_sums[:model_width], msg_sums[2 * model_width :]])
    grad_msg_in = product_right_t(grad_msg_project, mqkv_weight)
    grad_mnorm_gain = jnp.sum(grad_msg_in * msg_normed, 0)
    grad_mnorm_shift = jnp.sum(grad_msg_in, 0)
    grad_fc = narrow(
        grad_message + norm_back(grad_msg_in, msg_normed, msg_inverse, mnorm_gain.astype(wide))
    )
    grad_fc_weight = product_left_t(mine(class_all), grad_fc)
    grad_fc_bias = column_sums(grad_fc)
    grad_fc_mine = lax.dynamic_slice_in_dim(grad_fc, place * frames_here, frames_here)
    grad_class = product_right_t(grad_fc_mine, fc_weight)
    grad_tokens = grad_joined[:, :token_count].at[:, 0, :].add(grad_class)
    up_rows = scattered(narrow(grad_up_weight), True)
    down_rows = scattered(narrow(grad_down_weight), False)
    attn_rows = scattered(narrow(jnp.concatenate([grad_qkv_weight, grad_out_weight], 1)), True)
    sums = [
        *(v.reshape(64, -1) for v in (grad_gain_one, grad_shift_one, grad_out_bias)),
        *(v.reshape(64, -1) for v in (grad_gain_two, grad_shift_two, grad_down_bias)),
        *(v.reshape(64, -1) for v in (grad_qv_bias, grad_up_bias)),
    ]
    sums = jnp.pad(jnp.concatenate(sums, 1), ((0, 0), (0, 256 - 144)))
    sums = jnp.sum(lax.all_to_all(sums, "frame", 0, 0, tiled=True), 0)
    own = [
        lax.dynamic_slice_in_dim(v, place * 12, 12)
        for v in (grad_fc_bias, grad_mnorm_gain, grad_mnorm_shift, grad_mout_bias)
    ]
    own.append(lax.dynamic_slice_in_dim(grad_mqv_bias, place * 24, 24))
    vector_sums = jnp.concatenate([sums[:144], *own])
    vector_sums = vector_sums + sent(vector_sums, TO_VIDEO)
    msg_rows = jnp.concatenate([grad_fc_weight, grad_mqkv_weight, grad_mout_weight], 1)
    msg_rows = msg_rows + wide_of(sent(narrow(msg_rows), TO_VIDEO))
    cuts = [12, 24, 36, 48, 60, 72, 96, 144, 156, 168, 180, 192]
    g1, s1, ob, g2, s2, db, qvb, ub, fb, mg, ms, mob, mqvb = jnp.split(vector_sums, cuts)
    return (
        narrow(layer_out)[None],
        grad_tokens[None],
        msg_rows[:, :768],
        fb,
        mg,
        ms,
        msg_rows[:, 768:3072],
        mqvb,
        msg_rows[:, 3072:],
        mob,
        g1,
        s1,
        attn_rows[:, :2304],
        qvb,
        attn_rows[:, 2304:],
        ob,
        g2,
        s2,
        up_rows,
        ub,
        down_rows,
        db,
    )


def solution(mesh):
    in_specs = (
        P("video", "frame", None, None),
        P("video", "frame"),
        P("video", "frame", None, None),
        P("frame", None),
        P("frame"),
        P("frame"),
        P("frame"),
        P("frame", None),
        P("frame"),
        P("frame", None),
        P("frame"),
        P("frame"),
        P("frame"),
        P("frame", None),
        P("frame"),
        P("frame", None),
        P("frame"),
        P("frame"),
        P("frame"),
        P("frame", None),
        P("frame"),
        P("frame", None),
        P("frame"),
    )
    out_specs = (
        P("video", "frame", None, None),
        P("video", "frame", None, None),
        P("frame", None),
        P("frame"),
        P("frame"),
        P("frame"),
        P("frame", None),
        P("frame"),
        P("frame", None),
        P("frame"),
        P("frame"),
        P("frame"),
        P("frame", None),
        P("frame"),
        P("frame", None),
        P("frame"),
        P("frame"),
        P("frame"),
        P("frame", None),
        P("frame"),
        P("frame", None),
        P("frame"),
    )
    return jax.shard_map(shards, mesh=mesh, in_specs=in_specs, out_specs=out_specs, check_vma=False)
```

```python
import itertools
import jax
import jax.numpy as jnp
from jax import lax
from jax.experimental import pallas as pl
from jax.experimental.pallas import tpu as pltpu
from jax.sharding import PartitionSpec as P

HEAD_DIM = 64
FRAMES = 4
TOK = 197
SPAN = 208
ROWS = FRAMES * SPAN
D = 768
FF = 3072
HEADS = 12
PAIRS = 6
WIDE = jnp.float32
LOW = jnp.bfloat16
SCALE = HEAD_DIM ** (-0.5)
FC_B, MSG_GAIN, MSG_SHIFT, MOUT_B, GAIN1, SHIFT1, OUT_B, GAIN2, SHIFT2, DOWN_B, MQ_B, MV_B, Q_B, V_B, UP_B = range(15)
VECTOR_ROWS = 24


def narrow(x):
    return x.astype(LOW)


def wide_of(x):
    return x.astype(WIDE)


def mm(a, b):
    return lax.dot_general(a, b, (((1,), (0,)), ((), ())), preferred_element_type=WIDE)


def mm_t(a, b):
    return lax.dot_general(a, b, (((1,), (1,)), ((), ())), preferred_element_type=WIDE)


def normed_of(x):
    center = x - jnp.mean(x, -1, keepdims=True)
    inverse = lax.rsqrt(jnp.mean(center * center, -1, keepdims=True) + 1e-05)
    return center * inverse, inverse


def norm_back(grad, normed, inverse, gain):
    scaled = grad * gain
    return inverse * (
        scaled
        - jnp.mean(scaled, -1, keepdims=True)
        - normed * jnp.mean(scaled * normed, -1, keepdims=True)
    )


def own_lanes(x, which):
    lane = lax.broadcasted_iota(jnp.int32, x.shape, 1)
    return jnp.where((lane < HEAD_DIM) == (which == 0), x, jnp.zeros_like(x))


def either(a, b):
    lane = lax.broadcasted_iota(jnp.int32, a.shape, 1)
    return jnp.where(lane < HEAD_DIM, a, b)


def vec(vec_ref, row):
    return vec_ref[row : row + 1, :]


def fill_joined(tok_ref, msg_ref, joined_ref):
    for f in range(FRAMES):
        joined_ref[f * SPAN : f * SPAN + TOK, :] = wide_of(tok_ref[f])
        joined_ref[f * SPAN + TOK : f * SPAN + TOK + 1, :] = msg_ref[f : f + 1, :]
        joined_ref[f * SPAN + TOK + 1 : (f + 1) * SPAN, :] = jnp.zeros((SPAN - TOK - 1, D), WIDE)


def attend_fwd(q, k, vt, valid, mask):
    out = []
    for h in range(2):
        s = mm_t(own_lanes(k, h), q) * SCALE
        s = mask(s)
        peak = jnp.max(s, 0, keepdims=True)
        e = jnp.exp(s - peak)
        total = jnp.sum(e, 0, keepdims=True)
        o = mm(vt[h * HEAD_DIM : (h + 1) * HEAD_DIM], narrow(e)) / total
        out.append((o, peak + jnp.log(total)))
    return out


def attend_bwd(q, k, v, kt, go, lse, dot, mask):
    dqt, dk, dv = [], [], []
    for h in range(2):
        s = mask(mm_t(own_lanes(k, h), q) * SCALE)
        p = jnp.exp(s - lse[h])
        dp = mm_t(own_lanes(v, h), go)
        ds = narrow(p * (dp - dot[h]))
        dv.append(mm(narrow(p), go))
        dk.append(mm(ds, q))
        dqt.append(mm(kt[h * HEAD_DIM : (h + 1) * HEAD_DIM], ds))
    return (
        narrow(jnp.concatenate(dqt, 0) * SCALE),
        narrow(either(*dk) * SCALE),
        narrow(either(*dv)),
    )


def frame_mask(s):
    key = lax.broadcasted_iota(jnp.int32, s.shape, 0)
    return jnp.where(key <= TOK, s, -1e30)


def attn_fwd_kernel(tok_ref, msg_ref, wqkv_ref, wout_ref, vec_ref,
                    qkv_ref, mixed_ref, kept_ref, lse_ref, blk_ref, vt_ref, ot_ref):
    fill_joined(tok_ref, msg_ref, kept_ref)
    for f in range(FRAMES):
        rows = pl.ds(f * SPAN, SPAN)
        normed, _ = normed_of(kept_ref[rows, :])
        blk_ref[rows, :] = narrow(normed * vec(vec_ref, GAIN1) + vec(vec_ref, SHIFT1))
    for n in range(9):
        cols = pl.ds(n * 256, 256)
        y = mm(blk_ref[...], wqkv_ref[:, cols])
        if n < 3:
            y = y + vec_ref[Q_B : Q_B + 1, n * 256 : (n + 1) * 256]
        if n >= 6:
            y = y + vec_ref[V_B : V_B + 1, (n - 6) * 256 : (n - 5) * 256]
        qkv_ref[:, cols] = narrow(y)
    lse_ref[...] = jnp.zeros_like(lse_ref)

    def frame(f, _):
        rows = pl.ds(pl.multiple_of(f * SPAN, SPAN), SPAN)
        vt_ref[...] = qkv_ref[rows, 2 * D :].T
        for p in range(PAIRS):
            q = qkv_ref[rows, p * 128 : (p + 1) * 128]
            k = qkv_ref[rows, D + p * 128 : D + (p + 1) * 128]
            vt = vt_ref[p * 128 : (p + 1) * 128, :]
            for h, (o, l) in enumerate(attend_fwd(q, k, vt, None, frame_mask)):
                at = p * 128 + h * HEAD_DIM
                ot_ref[at : at + HEAD_DIM, :] = narrow(o)
                lse_ref[f, 2 * p + h : 2 * p + h + 1, :] = l
        mixed_ref[rows, :] = ot_ref[...].T
        return 0

    lax.fori_loop(0, FRAMES, frame, 0)
    kept_ref[...] = kept_ref[...] + mm(mixed_ref[...], wout_ref[...]) + vec(vec_ref, OUT_B)


def whole(shape):
    return pl.BlockSpec(shape, lambda *_: (0,) * len(shape))


def shaped(*shape, dtype=LOW):
    return jax.ShapeDtypeStruct(shape, dtype)


def attn_fwd(tok, msg, wqkv, wout, vectors):
    return pl.pallas_call(
        attn_fwd_kernel,
        out_shape=(shaped(ROWS, 3 * D), shaped(ROWS, D), shaped(ROWS, D, dtype=WIDE),
                   shaped(FRAMES, 16, SPAN, dtype=WIDE), shaped(ROWS, D)),
        scratch_shapes=[pltpu.VMEM((D, SPAN), LOW), pltpu.VMEM((D, SPAN), LOW)],
        compiler_params=pltpu.CompilerParams(vmem_limit_bytes=48 << 20),
        name="frame_attention",
    )(tok, msg, wqkv, wout, vectors)


def valid_rows(shape, first=0):
    row = lax.broadcasted_iota(jnp.int32, shape, 0) + first
    return row % SPAN < TOK


CHUNK = 768
CHUNKS = FF // CHUNK


def mlp_kernel(core_ref, kept_ref, gout_ref, up_ref, down_ref, vec_ref, perm_ref,
               lay_ref, gk_ref, dup_keep_ref, dup_give_ref, down_keep_ref, down_give_ref, sums_ref, dub_ref,
               mlp_ref, mlpt_ref, g_ref, acc_ref, dacc_ref):
    j = pl.program_id(0)

    @pl.when(j == 0)
    def _():
        for f in range(FRAMES):
            rows = pl.ds(f * SPAN, SPAN)
            normed, _ = normed_of(kept_ref[rows, :])
            mlp_ref[rows, :] = narrow(normed * vec(vec_ref, GAIN2) + vec(vec_ref, SHIFT2))
            g = jnp.concatenate([wide_of(gout_ref[f]), jnp.zeros((SPAN - TOK, D), WIDE)], 0)
            g_ref[rows, :] = narrow(g)
        mlpt_ref[...] = narrow(mm_t(perm_ref[...], mlp_ref[...]))
        acc_ref[...] = kept_ref[...] + vec(vec_ref, DOWN_B)
        dacc_ref[...] = jnp.zeros_like(dacc_ref)

    mlp = mlp_ref[...]
    g = g_ref[...]
    up = up_ref[...]
    down = down_ref[...]
    hidden = mm(mlp, up) + vec_ref[pl.ds(UP_B + j, 1), :]
    sig = 1.0 / (1.0 + jnp.exp(-1.702 * hidden))
    act = narrow(hidden * sig)
    acc_ref[...] += mm(act, down)
    gact = wide_of(narrow(mm_t(g, down)))
    gh = narrow(gact * (sig + 1.702 * hidden * sig * (1.0 - sig)))
    dub_ref[0] = jnp.broadcast_to(jnp.sum(wide_of(gh), 0, keepdims=True), (8, CHUNK))
    dup = narrow(mm(mlpt_ref[...], gh))
    dup_keep_ref[...] = dup[: D // 2]
    dup_give_ref[...] = dup[D // 2 :]
    dacc_ref[...] += mm_t(gh, up)
    ddown = narrow(lax.dot_general(act, g, (((0,), (0,)), ((), ())), preferred_element_type=WIDE))
    for core in range(2):

        @pl.when(core_ref[0] == core)
        def _():
            for yl in range(2):
                for z in range(4):
                    at = (yl * 4 + z) * 2
                    down_keep_ref[yl, z, 0] = ddown[(at + core) * 48 : (at + core + 1) * 48]
                    down_give_ref[yl, z, 0] = ddown[(at + 1 - core) * 48 : (at + 2 - core) * 48]

    @pl.when(j == CHUNKS - 1)
    def _():
        for f in range(FRAMES):
            lay_ref[f] = narrow(acc_ref[f * SPAN : f * SPAN + TOK, :])
        dg = jnp.zeros((1, D), WIDE)
        dsh = jnp.zeros((1, D), WIDE)
        db = jnp.zeros((1, D), WIDE)
        for f in range(FRAMES):
            rows = pl.ds(f * SPAN, SPAN)
            normed, inverse = normed_of(kept_ref[rows, :])
            gm = dacc_ref[rows, :]
            gw = wide_of(g_ref[rows, :])
            dg += jnp.sum(gm * normed, 0, keepdims=True)
            dsh += jnp.sum(gm, 0, keepdims=True)
            db += jnp.sum(gw, 0, keepdims=True)
            gk = gw + norm_back(gm, normed, inverse, vec(vec_ref, GAIN2))
            gk_ref[rows, :] = jnp.where(valid_rows(gk.shape), gk, 0.0)
        sums_ref[...] = jnp.concatenate([dg, dsh, db, jnp.zeros((5, D), WIDE)], 0)


def mlp(kept, gout, up, down, vectors, perm, core):
    down_spec = pl.BlockSpec((2, 4, 1, 48, D), lambda j: (j % 2, 0, j // 2, 0, 0))
    up_spec = pl.BlockSpec((D // 2, CHUNK), lambda j: (0, j))
    return pl.pallas_call(
        mlp_kernel,
        grid=(CHUNKS,),
        in_specs=[pl.BlockSpec(memory_space=pltpu.SMEM), whole((ROWS, D)), whole((FRAMES, TOK, D)),
                  pl.BlockSpec((D, CHUNK), lambda j: (0, j)),
                  pl.BlockSpec((CHUNK, D), lambda j: (j, 0)),
                  whole((VECTOR_ROWS, D)), whole((D, D))],
        out_specs=[whole((FRAMES, TOK, D)), whole((ROWS, D)),
                   up_spec, up_spec, down_spec, down_spec,
                   whole((8, D)), pl.BlockSpec((1, 8, CHUNK), lambda j: (j, 0, 0))],
        out_shape=(shaped(FRAMES, TOK, D), shaped(ROWS, D, dtype=WIDE), shaped(D // 2, FF), shaped(D // 2, FF),
                   shaped(4, 4, 2, 48, D), shaped(4, 4, 2, 48, D), shaped(8, D, dtype=WIDE), shaped(CHUNKS, 8, CHUNK, dtype=WIDE)),
        scratch_shapes=[pltpu.VMEM((ROWS, D), LOW), pltpu.VMEM((D, ROWS), LOW), pltpu.VMEM((ROWS, D), LOW),
                        pltpu.VMEM((ROWS, D), WIDE), pltpu.VMEM((ROWS, D), WIDE)],
        compiler_params=pltpu.CompilerParams(vmem_limit_bytes=56 << 20),
        name="mlp_both_ways",
    )(core, kept, gout, up, down, vectors, perm)


def head_sums(go, o):
    t = wide_of(go) * wide_of(o)
    high = narrow(t)
    rest = narrow(t - wide_of(high))
    head = lax.broadcasted_iota(jnp.int32, (16, D), 0)
    lane = lax.broadcasted_iota(jnp.int32, (16, D), 1)
    pick = jnp.where((lane // HEAD_DIM) == head, 1.0, 0.0).astype(LOW)
    return mm_t(pick, high) + mm_t(pick, rest)


def attn_bwd_kernel(gk_ref, mixed_ref, qkv_ref, lse_ref, msg_ref, wqkv_ref, wout_ref, vec_ref, perm_ref,
                    dqkv_ref, dout_ref, sums_ref, gmsg_ref,
                    gb_ref, gmix_ref, kt_ref, dqt_ref, rows_ref):
    gb_ref[...] = narrow(gk_ref[...])
    gb = gb_ref[...]
    gmix_ref[...] = narrow(mm_t(gb, wout_ref[...]))
    turned = narrow(mm_t(perm_ref[...], mixed_ref[...]))
    dout_ref[...] = narrow(mm(turned, gb))

    def frame(f, _):
        rows = pl.ds(pl.multiple_of(f * SPAN, SPAN), SPAN)
        kt_ref[...] = qkv_ref[rows, D : 2 * D].T
        dots = head_sums(gmix_ref[rows, :], mixed_ref[rows, :])
        for p in range(PAIRS):
            cols = lambda part: slice(part * D + p * 128, part * D + (p + 1) * 128)
            q, k, v = (qkv_ref[rows, cols(i)] for i in range(3))
            go = gmix_ref[rows, cols(0)]
            lse = [lse_ref[f, 2 * p + h : 2 * p + h + 1, :] for h in range(2)]
            dot = [dots[2 * p + h : 2 * p + h + 1, :] for h in range(2)]
            dqt, dk, dv = attend_bwd(q, k, v, kt_ref[cols(0), :], go, lse, dot, frame_mask)
            dqt_ref[cols(0), :] = dqt
            dqkv_ref[rows, cols(1)] = dk
            dqkv_ref[rows, cols(2)] = dv
        dqkv_ref[rows, :D] = dqt_ref[...].T
        return 0

    lax.fori_loop(0, FRAMES, frame, 0)
    dqb = jnp.zeros((1, D), WIDE)
    dvb = jnp.zeros((1, D), WIDE)
    db = jnp.zeros((1, D), WIDE)
    for f in range(FRAMES):
        rows = pl.ds(f * SPAN, SPAN)
        dqb += jnp.sum(wide_of(dqkv_ref[rows, :D]), 0, keepdims=True)
        dvb += jnp.sum(wide_of(dqkv_ref[rows, 2 * D :]), 0, keepdims=True)
        db += jnp.sum(wide_of(gb_ref[rows, :]), 0, keepdims=True)
        tile = wide_of(dqkv_ref[f * SPAN + 192 : f * SPAN + 208, :])
        rows_ref[f : f + 1, :] = tile[TOK - 192 : TOK - 191, :]
    rows_ref[FRAMES:, :] = jnp.zeros((8 - FRAMES, 3 * D), WIDE)
    sums_ref[...] = jnp.concatenate([db, dqb, dvb, jnp.zeros((5, D), WIDE)], 0)
    back = mm_t(narrow(rows_ref[...]), wqkv_ref[...])
    normed, inverse = normed_of(msg_ref[...])
    gmsg_ref[...] = norm_back(back[:FRAMES], normed, inverse, vec(vec_ref, GAIN1))


def attn_bwd(gk, mixed, qkv, lse, msg, wqkv, wout, vectors, perm):
    return pl.pallas_call(
        attn_bwd_kernel,
        out_shape=(shaped(ROWS, 3 * D), shaped(D, D), shaped(8, D, dtype=WIDE), shaped(FRAMES, D, dtype=WIDE)),
        scratch_shapes=[pltpu.VMEM((ROWS, D), LOW), pltpu.VMEM((ROWS, D), LOW), pltpu.VMEM((D, SPAN), LOW),
                        pltpu.VMEM((D, SPAN), LOW), pltpu.VMEM((8, 3 * D), WIDE)],
        compiler_params=pltpu.CompilerParams(vmem_limit_bytes=56 << 20),
        name="frame_attention_back",
    )(gk, mixed, qkv, lse, msg, wqkv, wout, vectors, perm)


def qkv_weight_kernel(blk_ref, dqkv_ref, perm_ref, out_ref, turned_ref):
    @pl.when(pl.program_id(0) == 0)
    def _():
        turned_ref[...] = narrow(mm_t(perm_ref[...], blk_ref[...]))

    out_ref[...] = narrow(mm(turned_ref[...], dqkv_ref[...]))


def qkv_weight(blk, dqkv, perm):
    return pl.pallas_call(
        qkv_weight_kernel,
        grid=(3,),
        in_specs=[whole((ROWS, D)), pl.BlockSpec((ROWS, D), lambda j: (0, j)), whole((D, D))],
        out_specs=pl.BlockSpec((D, D), lambda j: (0, j)),
        out_shape=shaped(D, 3 * D),
        scratch_shapes=[pltpu.VMEM((D, ROWS), LOW)],
        compiler_params=pltpu.CompilerParams(vmem_limit_bytes=48 << 20),
        name="qkv_weight_gradient",
    )(blk, dqkv, perm)


def tokens_back_kernel(dqkv_ref, wqkv_ref, gk_ref, tok_ref, msg_ref, gcls_ref, vec_ref,
                       out_ref, sums_ref, joined_ref):
    fill_joined(tok_ref, msg_ref, joined_ref)
    dg = jnp.zeros((1, D), WIDE)
    dsh = jnp.zeros((1, D), WIDE)
    joined_ref2 = joined_ref
    back_all = mm_t(dqkv_ref[...], wqkv_ref[...])
    for f in range(FRAMES):
        rows = pl.ds(f * SPAN, SPAN)
        back = back_all[f * SPAN : (f + 1) * SPAN]
        normed, inverse = normed_of(joined_ref2[rows, :])
        dg += jnp.sum(back * normed, 0, keepdims=True)
        dsh += jnp.sum(back, 0, keepdims=True)
        full = gk_ref[rows, :] + norm_back(back, normed, inverse, vec(vec_ref, GAIN1))
        out_ref[f] = full[:TOK]
        out_ref[f, 0:1, :] = full[0:1] + gcls_ref[f : f + 1, :]
    sums_ref[...] = jnp.concatenate([dg, dsh, jnp.zeros((6, D), WIDE)], 0)


def tokens_back(dqkv, wqkv, gk, tok, msg, gcls, vectors):
    return pl.pallas_call(
        tokens_back_kernel,
        out_shape=(shaped(FRAMES, TOK, D, dtype=WIDE), shaped(8, D, dtype=WIDE)),
        scratch_shapes=[pltpu.VMEM((ROWS, D), WIDE)],
        compiler_params=pltpu.CompilerParams(vmem_limit_bytes=56 << 20),
        name="tokens_back",
    )(dqkv, wqkv, gk, tok, msg, gcls, vectors)


ALL = 256


def group_mask(grow_ref, gcol_ref):
    same = gcol_ref[:, 0:1] == grow_ref[0:1, :]

    def mask(s):
        return jnp.where(same, s, -1000000000.0)

    return mask


def msg_fwd_kernel(cls_ref, w_ref, vec_ref, grow_ref, gcol_ref,
                   message_ref, token_ref, min_ref, qkv_ref, mixed_ref, lse_ref, vt_ref, ot_ref):
    message = mm(cls_ref[...], w_ref[:, :D]) + vec(vec_ref, FC_B)
    message_ref[...] = message
    normed, _ = normed_of(message)
    min_ref[...] = narrow(normed * vec(vec_ref, MSG_GAIN) + vec(vec_ref, MSG_SHIFT))
    for n in range(9):
        y = mm(min_ref[...], w_ref[:, D + n * 256 : D + (n + 1) * 256])
        if n < 3:
            y = y + vec_ref[MQ_B : MQ_B + 1, n * 256 : (n + 1) * 256]
        if n >= 6:
            y = y + vec_ref[MV_B : MV_B + 1, (n - 6) * 256 : (n - 5) * 256]
        qkv_ref[:, n * 256 : (n + 1) * 256] = narrow(y)
    vt_ref[...] = qkv_ref[:, 2 * D :].T
    mask = group_mask(grow_ref, gcol_ref)
    lse_ref[...] = jnp.zeros_like(lse_ref)
    for p in range(PAIRS):
        q = qkv_ref[:, p * 128 : (p + 1) * 128]
        k = qkv_ref[:, D + p * 128 : D + (p + 1) * 128]
        vt = vt_ref[p * 128 : (p + 1) * 128, :]
        for h, (o, l) in enumerate(attend_fwd(q, k, vt, None, mask)):
            at = p * 128 + h * HEAD_DIM
            ot_ref[at : at + HEAD_DIM, :] = narrow(o)
            lse_ref[2 * p + h : 2 * p + h + 1, :] = l
    mixed_ref[...] = ot_ref[...].T
    token_ref[...] = message + mm(mixed_ref[...], w_ref[:, 4 * D :]) + vec(vec_ref, MOUT_B)


def msg_fwd(cls, w, vectors, grow, gcol):
    return pl.pallas_call(
        msg_fwd_kernel,
        out_shape=(shaped(ALL, D, dtype=WIDE), shaped(ALL, D, dtype=WIDE), shaped(ALL, D), shaped(ALL, 3 * D),
                   shaped(ALL, D), shaped(16, ALL, dtype=WIDE)),
        scratch_shapes=[pltpu.VMEM((D, ALL), LOW), pltpu.VMEM((D, ALL), LOW)],
        compiler_params=pltpu.CompilerParams(vmem_limit_bytes=48 << 20),
        name="message_forward",
    )(cls, w, vectors, grow, gcol)


def msg_bwd_kernel(gm_ref, cls_ref, message_ref, min_ref, qkv_ref, mixed_ref, lse_ref, w_ref, vec_ref,
                   grow_ref, gcol_ref, pick_ref,
                   gcls_ref, dw_ref, sums_ref,
                   gmix_ref, kt_ref, dqt_ref, dqkv_ref):
    gb = gm_ref[...]
    pick = pick_ref[...]
    turned = lambda x: narrow(mm_t(pick, x))
    gmix_ref[...] = narrow(mm_t(gb, w_ref[:, 4 * D :]))
    dw_ref[:, 4 * D :] = mm(turned(mixed_ref[...]), gb)
    kt_ref[...] = qkv_ref[:, D : 2 * D].T
    mask = group_mask(grow_ref, gcol_ref)
    dots = head_sums(gmix_ref[...], mixed_ref[...])
    for p in range(PAIRS):
        cols = lambda part: slice(part * D + p * 128, part * D + (p + 1) * 128)
        q, k, v = (qkv_ref[:, cols(i)] for i in range(3))
        go = gmix_ref[:, cols(0)]
        lse = [lse_ref[2 * p + h : 2 * p + h + 1, :] for h in range(2)]
        dot = [dots[2 * p + h : 2 * p + h + 1, :] for h in range(2)]
        dqt, dk, dv = attend_bwd(q, k, v, kt_ref[cols(0), :], go, lse, dot, mask)
        dqt_ref[cols(0), :] = dqt
        dqkv_ref[:, cols(1)] = dk
        dqkv_ref[:, cols(2)] = dv
    dqkv_ref[:, :D] = dqt_ref[...].T
    dqkv = dqkv_ref[...]
    dw_ref[:, D : 4 * D] = mm(turned(min_ref[...]), dqkv)
    back = mm_t(dqkv, w_ref[:, D : 4 * D])
    normed, inverse = normed_of(message_ref[...])
    gfc = narrow(wide_of(gb) + norm_back(back, normed, inverse, vec(vec_ref, MSG_GAIN)))
    dw_ref[:, :D] = mm(turned(cls_ref[...]), gfc)
    gcls_ref[...] = mm_t(gfc, w_ref[:, :D])
    col = lambda x: jnp.sum(wide_of(x), 0, keepdims=True)
    sums_ref[...] = jnp.concatenate(
        [col(gfc), col(back * normed), col(back), col(gb), col(dqkv[:, :D]), col(dqkv[:, 2 * D :]),
         jnp.zeros((2, D), WIDE)], 0)


def msg_bwd(gm, cls, message, mins, qkv, mixed, lse, w, vectors, grow, gcol, pick):
    return pl.pallas_call(
        msg_bwd_kernel,
        out_shape=(shaped(ALL, D, dtype=WIDE), shaped(16, 5 * D, dtype=WIDE), shaped(8, D, dtype=WIDE)),
        scratch_shapes=[pltpu.VMEM((ALL, D), LOW), pltpu.VMEM((D, ALL), LOW), pltpu.VMEM((D, ALL), LOW),
                        pltpu.VMEM((ALL, 3 * D), LOW)],
        compiler_params=pltpu.CompilerParams(vmem_limit_bytes=48 << 20),
        name="message_back",
    )(gm, cls, message, mins, qkv, mixed, lse, w, vectors, grow, gcol, pick)


def frame_of(x_hi, y, z, core):
    return ((x_hi * 4 + y) * 4 + z) * 2 + core


PLACES = list(itertools.product(range(2), range(4), range(4), range(2), range(2)))


def moves(to):
    return [(frame_of(*p[:4]) * 2 + p[4], frame_of(*to(*p)[:4]) * 2 + to(*p)[4]) for p in PLACES]


TO_CORE = moves(lambda x, y, z, c, v: (x, y, z, 1 - c, v))
TO_VIDEO = moves(lambda x, y, z, c, v: (x, y, z, c, 1 - v))
TO_HALF = moves(lambda x, y, z, c, v: (1 - x, y, z, c, v))
TO_BOTH = moves(lambda x, y, z, c, v: (1 - x, y, z, c, 1 - v))
TO_Y = [moves(lambda x, y, z, c, v, k=k: (x, (y + k) % 4, z, c, v)) for k in range(4)]
TO_Z = [moves(lambda x, y, z, c, v, k=k: (x, y, (z + k) % 4, c, v)) for k in range(4)]
PLANE = [[frame_of(x, y, z, c) for y in range(4) for z in range(4)] for x in range(2) for c in range(2)]
ATTN_HALF = 1536
MSG_HALF = 1920


def sent(x, pairs):
    return lax.ppermute(x, ("frame", "video"), pairs)


def to_everyone(x):
    return lax.all_to_all(jnp.broadcast_to(x[None], (64, *x.shape)), "frame", 0, 0, tiled=True)


def assemble_kernel(place_ref, *refs):
    pieces, (attn_ref, msg_ref, sems) = refs[:12], refs[12:]
    place = place_ref[0]
    core = lax.rem(place, 2)
    y = lax.rem(lax.div(place, 8), 4)
    x = lax.div(place, 32)
    copies = []

    def copy(src, dst_ref, x_at, y_at, col, width):
        row = pl.multiple_of((x_at * 4 + y_at) * 96, 96)
        dst = dst_ref.at[pl.ds(row, 96), pl.ds(pl.multiple_of(col, 128), width)]
        done = pltpu.make_async_copy(src, dst, sems.at[len(copies)])
        done.start()
        copies.append(done)

    for who in range(2):
        owner = core if who == 0 else 1 - core
        for k in range(4):
            for h in range(2):
                copy(pieces[who * 4 + k].at[h], attn_ref, x if h == 0 else 1 - x,
                     lax.rem(y + 4 - k, 4), owner * ATTN_HALF, ATTN_HALF)
        for h in range(2):
            for k in range(4):
                copy(pieces[8 + who * 2 + h].at[k], msg_ref, x if h == 0 else 1 - x,
                     lax.rem(y + 4 - k, 4), owner * MSG_HALF, MSG_HALF)
    for done in copies:
        done.wait()


def assemble(place, pieces):
    anywhere = pl.BlockSpec(memory_space=pl.ANY)
    return pl.pallas_call(
        assemble_kernel,
        in_specs=[pl.BlockSpec(memory_space=pltpu.SMEM)] + [anywhere] * 12,
        out_specs=(anywhere, anywhere),
        out_shape=(shaped(D, 2 * ATTN_HALF), shaped(D, 2 * MSG_HALF)),
        scratch_shapes=[pltpu.SemaphoreType.DMA((32,))],
        name="assemble_weights",
    )(place, *pieces)


def gathered(place, attn, msg):
    core = place % 2
    z = place // 2 % 4
    cols = lambda w, half, which: lax.dynamic_slice_in_dim(w, which * half, half, 1)
    mine = jnp.concatenate([cols(attn, ATTN_HALF, core), cols(msg, MSG_HALF, core)], 1)
    give = jnp.concatenate([cols(attn, ATTN_HALF, 1 - core), cols(msg, MSG_HALF, 1 - core)], 1)
    got = sent(give, TO_CORE)
    pair = jnp.where(core == 0, jnp.concatenate([mine, got], 0), jnp.concatenate([got, mine], 0))
    ring = [pair, *(sent(pair, TO_Z[k]) for k in range(1, 4))]
    ring = jnp.stack([ring[-t % 4] for t in range(7)])
    slab = lax.dynamic_slice_in_dim(ring, (4 - z) % 4, 4, 0).reshape(96, -1)
    part_a, part_b = slab[:, :ATTN_HALF], slab[:, ATTN_HALF:]
    side_a = jnp.stack([part_a, sent(part_a, TO_HALF)])
    side_b = jnp.stack([part_b, *(sent(part_b, TO_Y[k]) for k in range(1, 4))])
    all_a = [side_a, *(sent(side_a, TO_Y[k]) for k in range(1, 4))]
    all_b = [side_b, sent(side_b, TO_HALF)]
    pieces = [*all_a, *(sent(a, TO_CORE) for a in all_a), *all_b, *(sent(b, TO_CORE) for b in all_b)]
    return assemble(place.reshape(1), pieces)


def row_order(place):
    row = jnp.arange(D, dtype=jnp.int32)
    r, x, z, y, c = row % 12, row // 12 % 2, row // 24 % 4, row // 96 % 4, row // 384
    natural = ((((x * 4 + y) * 4 + z) * 2) + jnp.where(c == 0, place % 2, 1 - place % 2)) * 12 + r
    return (natural[:, None] == row[None, :]).astype(LOW)


def add_pack_kernel(keep_up, got_up, keep_down, got_down, out_ref):
    up = wide_of(keep_up[...]) + wide_of(got_up[...])
    down = wide_of(keep_down[0]) + wide_of(got_down[0])
    for i in range(2):
        out_ref[i, :, :FF] = narrow(up[24 * i : 24 * i + 24])
        slab = jnp.concatenate([down[i, 0], down[i, 1]], 0)
        for q in range(4):
            out_ref[i, :, FF + q * D : FF + (q + 1) * D] = narrow(slab[24 * q : 24 * q + 24])


def add_pack(keep_up, got_up, keep_down, got_down):
    down_spec = pl.BlockSpec((1, 2, 2, 48, D), lambda i: (i // 2, i % 2, 0, 0, 0))
    up_spec = pl.BlockSpec((48, FF), lambda i: (i, 0))
    return pl.pallas_call(
        add_pack_kernel,
        grid=(8,),
        in_specs=[up_spec, up_spec, down_spec, down_spec],
        out_specs=pl.BlockSpec((2, 24, 2 * FF), lambda i: (i, 0, 0)),
        out_shape=shaped(16, 24, 2 * FF),
        compiler_params=pltpu.CompilerParams(vmem_limit_bytes=32 << 20),
        name="add_mlp_gradients",
    )(keep_up, got_up, keep_down, got_down)


def plane_sum(parts):
    got = lax.all_to_all(parts, "frame", 0, 0, axis_index_groups=PLANE, tiled=True)
    return narrow(jnp.sum(wide_of(got), 0))


def last_sum(mine, other):
    return wide_of(mine) + wide_of(sent(mine, TO_VIDEO)) + wide_of(sent(other, TO_HALF)) + wide_of(sent(other, TO_BOTH))


def shards(
    tokens_in,
    clip_ids,
    grad_out,
    msg_fc_w,
    msg_fc_b,
    msg_norm_gain,
    msg_norm_shift,
    msg_qkv_w,
    msg_qv_b,
    msg_out_w,
    msg_out_b,
    norm1_gain,
    norm1_shift,
    attn_qkv_w,
    attn_qv_b,
    attn_out_w,
    attn_out_b,
    norm2_gain,
    norm2_shift,
    mlp_in_w,
    mlp_in_b,
    mlp_out_w,
    mlp_out_b,
):
    place = lax.axis_index("frame").astype(jnp.int32)
    core, half = place % 2, place // 32
    tok = tokens_in[0]
    small = jnp.concatenate(
        [
            tok[:, 0, :].reshape(-1),
            msg_fc_b,
            msg_norm_gain,
            msg_norm_shift,
            msg_out_b,
            norm1_gain,
            norm1_shift,
            attn_out_b,
            norm2_gain,
            norm2_shift,
            mlp_out_b,
            msg_qv_b,
            attn_qv_b,
            mlp_in_b,
            clip_ids[0].astype(LOW),
        ]
    )
    small = jnp.pad(small, (0, 4096 - small.shape[0])).reshape(32, 128)
    small_all = to_everyone(small).reshape(64, 4096)
    up_rows = mlp_in_w.reshape(12, 4, D).transpose(1, 0, 2).reshape(48, D)
    mlp_all = lax.all_gather(jnp.concatenate([up_rows, mlp_out_w], 1), "frame", axis=0, tiled=True)
    w_attn, w_msg = gathered(
        place,
        jnp.concatenate([attn_qkv_w, attn_out_w], 1),
        jnp.concatenate([msg_fc_w, msg_qkv_w, msg_out_w], 1),
    )
    up = mlp_all[:, :D].reshape(64, 4, 12, D).transpose(0, 2, 1, 3).reshape(D, FF)
    down = mlp_all[:, D:]
    cls = small_all[:, :3072].reshape(ALL, D)
    vectors = []
    at = 3072
    for size in [12] * 10 + [24, 24, 48]:
        vectors.append(small_all[:, at : at + size].reshape(-1, D))
        at += size
    vectors = jnp.concatenate(vectors, 0).astype(WIDE)
    vectors = jnp.pad(vectors, ((0, VECTOR_ROWS - vectors.shape[0]), (0, 0)))
    groups = wide_of(small_all[:, at : at + 4].reshape(ALL))
    grow = jnp.broadcast_to(groups[None], (8, ALL))
    gcol = jnp.broadcast_to(groups[:, None], (ALL, 128))
    order = row_order(place)
    pick_row = jnp.arange(16, dtype=jnp.int32)[:, None]
    pick_col = jnp.arange(D, dtype=jnp.int32)[None, :]
    pick = ((pick_row < 12) & (pick_col == place * 12 + pick_row)).astype(LOW)
    w_qkv, w_out = w_attn[:, : 3 * D], w_attn[:, 3 * D :]

    message, token, mins, mqkv, mmixed, mlse = msg_fwd(cls, w_msg, vectors, grow, gcol)
    msg = lax.dynamic_slice_in_dim(token, place * FRAMES, FRAMES)
    qkv, mixed, kept, lse, blk = attn_fwd(tok, msg, w_qkv, w_out, vectors)
    lay, gk, dup_keep, dup_give, down_keep, down_give, sums_mlp, dub = mlp(
        kept, grad_out[0], up, down, vectors, order, core.reshape(1)
    )
    dup_got, down_got = sent(dup_give, TO_CORE), sent(down_give, TO_CORE)
    mlp_sum = plane_sum(add_pack(dup_keep, dup_got, down_keep, down_got))
    dqkv, dout, sums_attn, gmsg = attn_bwd(gk, mixed, qkv, lse, msg, w_qkv, w_out, vectors, order)
    gmsg_all = to_everyone(narrow(gmsg)).reshape(ALL, D)
    dwqkv = qkv_weight(blk, dqkv, order)
    attn_part = jnp.concatenate([dwqkv, dout], 1)
    attn_got = sent(attn_part[384:], TO_CORE)
    attn_sum = narrow(wide_of(attn_part[:384]) + wide_of(attn_got)).reshape(16, 24, FF)
    attn_sum = plane_sum(attn_sum)
    gcls, dw_msg, sums_msg = msg_bwd(gmsg_all, cls, message, mins, mqkv, mmixed, mlse, w_msg, vectors, grow, gcol, pick)
    gcls = lax.dynamic_slice_in_dim(gcls, place * FRAMES, FRAMES)
    grad_tokens, sums_tok = tokens_back(dqkv, w_qkv, gk, tok, msg, gcls, vectors)

    rows = jnp.concatenate([mlp_sum[:, :FF], attn_sum], 1).reshape(2, 12, 2 * FF)
    down_rows = mlp_sum[:, FF:].reshape(24, 4, D).transpose(1, 0, 2).reshape(2, 48, D)
    pick_half = lambda x, which: lax.dynamic_index_in_dim(x, which, 0, keepdims=False)
    rows = last_sum(pick_half(rows, half), pick_half(rows, 1 - half))
    down_rows = last_sum(pick_half(down_rows, half), pick_half(down_rows, 1 - half))
    msg_rows = dw_msg[:12]
    msg_rows = msg_rows + wide_of(sent(narrow(msg_rows), TO_VIDEO))
    sums = jnp.concatenate(
        [sums_tok[:2], sums_attn[:1], sums_mlp[:3]], 0
    ).reshape(6, 64, 12).transpose(1, 0, 2).reshape(64, 72)
    sums = jnp.concatenate(
        [sums, sums_attn[1:3].reshape(64, 24), dub[:, 0].reshape(64, 48), jnp.zeros((64, 112), WIDE)], 1
    )
    sums = jnp.sum(lax.all_to_all(sums, "frame", 0, 0, tiled=True), 0)[:144]
    own = lax.dynamic_slice_in_dim(sums_msg[:4], place * 12, 12, 1).reshape(-1)
    own_qv = lax.dynamic_slice_in_dim(sums_msg[4:6].reshape(-1), place * 24, 24)
    sums = jnp.concatenate([sums, own, own_qv])
    sums = sums + sent(sums, TO_VIDEO)
    cuts = [12, 24, 36, 48, 60, 72, 96, 144, 156, 168, 180, 192]
    g1, s1, ob, g2, s2, db, qvb, ub, fb, mg, ms, mob, mqvb = jnp.split(sums, cuts)
    return (
        lay[None],
        grad_tokens[None],
        msg_rows[:, :D],
        fb,
        mg,
        ms,
        msg_rows[:, D : 4 * D],
        mqvb,
        msg_rows[:, 4 * D :],
        mob,
        g1,
        s1,
        rows[:, FF : FF + 3 * D],
        qvb,
        rows[:, FF + 3 * D :],
        ob,
        g2,
        s2,
        rows[:, :FF],
        ub,
        down_rows,
        db,
    )


def solution(mesh):
    in_specs = (
        P("video", "frame", None, None),
        P("video", "frame"),
        P("video", "frame", None, None),
        P("frame", None),
        P("frame"),
        P("frame"),
        P("frame"),
        P("frame", None),
        P("frame"),
        P("frame", None),
        P("frame"),
        P("frame"),
        P("frame"),
        P("frame", None),
        P("frame"),
        P("frame", None),
        P("frame"),
        P("frame"),
        P("frame"),
        P("frame", None),
        P("frame"),
        P("frame", None),
        P("frame"),
    )
    out_specs = (
        P("video", "frame", None, None),
        P("video", "frame", None, None),
        P("frame", None),
        P("frame"),
        P("frame"),
        P("frame"),
        P("frame", None),
        P("frame"),
        P("frame", None),
        P("frame"),
        P("frame"),
        P("frame"),
        P("frame", None),
        P("frame"),
        P("frame", None),
        P("frame"),
        P("frame"),
        P("frame"),
        P("frame", None),
        P("frame"),
        P("frame", None),
        P("frame"),
    )
    return jax.shard_map(shards, mesh=mesh, in_specs=in_specs, out_specs=out_specs, check_vma=False)
```

```python
import functools
import itertools
import jax
import jax.numpy as jnp
from jax import lax
from jax.experimental import pallas as pl
from jax.experimental.pallas import tpu as pltpu
from jax.sharding import PartitionSpec as P

HEAD_DIM = 64
FRAMES = 4
TOK = 197
SPAN = 208
ROWS = FRAMES * SPAN
D = 768
FF = 3072
HEADS = 12
PAIRS = 6
WIDE = jnp.float32
LOW = jnp.bfloat16
SCALE = HEAD_DIM ** (-0.5)
FC_B, MSG_GAIN, MSG_SHIFT, MOUT_B, GAIN1, SHIFT1, OUT_B, GAIN2, SHIFT2, DOWN_B, MQ_B, MV_B, Q_B, V_B, UP_B = range(15)
VECTOR_ROWS = 24


def narrow(x):
    return x.astype(LOW)


def wide_of(x):
    return x.astype(WIDE)


def mm(a, b):
    return lax.dot_general(a, b, (((1,), (0,)), ((), ())), preferred_element_type=WIDE)


def mm_t(a, b):
    return lax.dot_general(a, b, (((1,), (1,)), ((), ())), preferred_element_type=WIDE)


def normed_of(x):
    center = x - jnp.mean(x, -1, keepdims=True)
    inverse = lax.rsqrt(jnp.mean(center * center, -1, keepdims=True) + 1e-05)
    return center * inverse, inverse


def norm_back(grad, normed, inverse, gain):
    scaled = grad * gain
    return inverse * (
        scaled
        - jnp.mean(scaled, -1, keepdims=True)
        - normed * jnp.mean(scaled * normed, -1, keepdims=True)
    )


def own_lanes(x, which):
    lane = lax.broadcasted_iota(jnp.int32, x.shape, 1)
    return jnp.where((lane < HEAD_DIM) == (which == 0), x, jnp.zeros_like(x))


def either(a, b):
    lane = lax.broadcasted_iota(jnp.int32, a.shape, 1)
    return jnp.where(lane < HEAD_DIM, a, b)


def vec(vec_ref, row):
    return vec_ref[row : row + 1, :]


def fill_joined(tok_ref, msg_ref, joined_ref):
    for f in range(FRAMES):
        joined_ref[f * SPAN : f * SPAN + TOK, :] = wide_of(tok_ref[f])
        joined_ref[f * SPAN + TOK : f * SPAN + TOK + 1, :] = msg_ref[f : f + 1, :]
        joined_ref[f * SPAN + TOK + 1 : (f + 1) * SPAN, :] = jnp.zeros((SPAN - TOK - 1, D), WIDE)


def attend_fwd(q, k, vt, valid, mask):
    out = []
    for h in range(2):
        s = mm_t(own_lanes(k, h), q) * SCALE
        s = mask(s)
        peak = jnp.max(s, 0, keepdims=True)
        e = jnp.exp(s - peak)
        total = jnp.sum(e, 0, keepdims=True)
        o = mm(vt[h * HEAD_DIM : (h + 1) * HEAD_DIM], narrow(e)) / total
        out.append((o, peak + jnp.log(total)))
    return out


def attend_bwd(q, k, v, kt, go, lse, dot, mask):
    dqt, dk, dv = [], [], []
    for h in range(2):
        s = mask(mm_t(own_lanes(k, h), q) * SCALE)
        p = jnp.exp(s - lse[h])
        dp = mm_t(own_lanes(v, h), go)
        ds = narrow(p * (dp - dot[h]))
        dv.append(mm(narrow(p), go))
        dk.append(mm(ds, q))
        dqt.append(mm(kt[h * HEAD_DIM : (h + 1) * HEAD_DIM], ds))
    return (
        narrow(jnp.concatenate(dqt, 0) * SCALE),
        narrow(either(*dk) * SCALE),
        narrow(either(*dv)),
    )


def frame_mask(s):
    key = lax.broadcasted_iota(jnp.int32, s.shape, 0)
    return jnp.where(key <= TOK, s, -1e30)


def attn_fwd_kernel(tok_ref, msg_ref, wqkv_ref, wout_ref, vec_ref,
                    qkv_ref, mixed_ref, kept_ref, lse_ref, blk_ref, vt_ref, ot_ref):
    fill_joined(tok_ref, msg_ref, kept_ref)
    for f in range(FRAMES):
        rows = pl.ds(f * SPAN, SPAN)
        normed, _ = normed_of(kept_ref[rows, :])
        blk_ref[rows, :] = narrow(normed * vec(vec_ref, GAIN1) + vec(vec_ref, SHIFT1))
    for n in range(9):
        cols = pl.ds(n * 256, 256)
        y = mm(blk_ref[...], wqkv_ref[:, cols])
        if n < 3:
            y = y + vec_ref[Q_B : Q_B + 1, n * 256 : (n + 1) * 256]
        if n >= 6:
            y = y + vec_ref[V_B : V_B + 1, (n - 6) * 256 : (n - 5) * 256]
        qkv_ref[:, cols] = narrow(y)
    lse_ref[...] = jnp.zeros_like(lse_ref)

    def frame(f, _):
        rows = pl.ds(pl.multiple_of(f * SPAN, SPAN), SPAN)
        vt_ref[...] = qkv_ref[rows, 2 * D :].T
        for p in range(PAIRS):
            q = qkv_ref[rows, p * 128 : (p + 1) * 128]
            k = qkv_ref[rows, D + p * 128 : D + (p + 1) * 128]
            vt = vt_ref[p * 128 : (p + 1) * 128, :]
            for h, (o, l) in enumerate(attend_fwd(q, k, vt, None, frame_mask)):
                at = p * 128 + h * HEAD_DIM
                ot_ref[at : at + HEAD_DIM, :] = narrow(o)
                lse_ref[f, 2 * p + h : 2 * p + h + 1, :] = l
        mixed_ref[rows, :] = ot_ref[...].T
        return 0

    lax.fori_loop(0, FRAMES, frame, 0)
    kept_ref[...] = kept_ref[...] + mm(mixed_ref[...], wout_ref[...]) + vec(vec_ref, OUT_B)


def cost(us):
    return pl.CostEstimate(flops=int(us * 1.15e9), bytes_accessed=int(us * 1e6), transcendentals=0)


def qkv_out_specs():
    return [pl.BlockSpec((D, 3 * D), lambda *_: (0, 0)), pl.BlockSpec((D, D), lambda *_: (0, 3))]


def whole(shape):
    return pl.BlockSpec(shape, lambda *_: (0,) * len(shape))


def shaped(*shape, dtype=LOW):
    return jax.ShapeDtypeStruct(shape, dtype)


def attn_fwd(tok, msg, w_attn, vectors):
    return pl.pallas_call(
        attn_fwd_kernel,
        grid=(1,),
        in_specs=[whole(tok.shape), whole(msg.shape), *qkv_out_specs(), whole(vectors.shape)],
        out_specs=(whole((ROWS, 3 * D)), whole((ROWS, D)), whole((ROWS, D)), whole((FRAMES, 16, SPAN)), whole((ROWS, D))),
        out_shape=(shaped(ROWS, 3 * D), shaped(ROWS, D), shaped(ROWS, D, dtype=WIDE),
                   shaped(FRAMES, 16, SPAN, dtype=WIDE), shaped(ROWS, D)),
        scratch_shapes=[pltpu.VMEM((D, SPAN), LOW), pltpu.VMEM((D, SPAN), LOW)],
        compiler_params=pltpu.CompilerParams(vmem_limit_bytes=48 << 20),
        cost_estimate=cost(1),
        name="frame_attention",
    )(tok, msg, w_attn, w_attn, vectors)


def valid_rows(shape, first=0):
    row = lax.broadcasted_iota(jnp.int32, shape, 0) + first
    return row % SPAN < TOK


def place_parts(place):
    return lax.div(place, 32), lax.rem(lax.div(place, 8), 4), lax.rem(lax.div(place, 2), 4), lax.rem(place, 2)


CHUNK = 768
CHUNKS = FF // CHUNK


def assemble_up(place_ref, held_ref, out_ref, j):
    x, y, _, _ = place_parts(place_ref[0])
    cols = pl.ds(pl.multiple_of(j * CHUNK, CHUNK), CHUNK)
    for k in range(4):
        slabs = [wide_of(held_ref[z, 48 * k : 48 * k + 48, cols]) for z in range(4)]
        for h in range(2):
            row = pl.multiple_of(((x if h == 0 else 1 - x) * 4 + lax.rem(y + 4 - k, 4)) * 96, 96)
            out_ref[pl.ds(row, 96), :] = narrow(jnp.concatenate([v[24 * h : 24 * h + 24] for v in slabs], 0))


def assemble_down(place_ref, held_ref, out_ref, j):
    x, y, _, core = place_parts(place_ref[0])
    side = lax.rem(lax.div(j, 2) + x, 2)
    for who in range(2):
        col = pl.multiple_of((core if who == 0 else 1 - core) * (D // 2), 128)
        for yl in range(2):
            piece = who * 4 + lax.rem(y + 4 - (lax.rem(j, 2) * 2 + yl), 4)
            for pair in range(2):
                slab = wide_of(held_ref[piece, side, 48 * pair : 48 * pair + 48, :])
                parts = [slab[24 * z : 24 * z + 24, q * (D // 2) : (q + 1) * (D // 2)] for z in range(2) for q in range(4)]
                at = yl * 384 + pair * 192
                out_ref[at : at + 192, pl.ds(col, D // 2)] = narrow(jnp.concatenate(parts, 0))


def mlp_kernel(place_ref, kept_ref, gout_ref, vec_ref, perm_ref, *refs):
    up_pieces, down_pieces = refs[:2], refs[2:10]
    lay_ref, gk_ref, dup_keep_ref, dup_give_ref, down_keep_ref, down_give_ref, sums_ref, dub_ref = refs[10:18]
    mlp_ref, mlpt_ref, g_ref, acc_ref, dacc_ref, held_up_ref, held_down_ref, up_ref, down_ref, sems = refs[18:]
    j = pl.program_id(0)
    core_at = lax.rem(place_ref[0], 2)

    def copies():
        for who in range(2):
            col = pl.multiple_of((core_at if who == 0 else 1 - core_at) * (FF // 2), 128)
            yield pltpu.make_async_copy(up_pieces[who], held_up_ref.at[:, :, pl.ds(col, FF // 2)], sems.at[who])
        for n in range(8):
            yield pltpu.make_async_copy(down_pieces[n], held_down_ref.at[n], sems.at[2 + n])

    @pl.when(j == 0)
    def _():
        for copy in copies():
            copy.start()

    @pl.when(j == 0)
    def _():
        for f in range(FRAMES):
            rows = pl.ds(f * SPAN, SPAN)
            normed, _ = normed_of(kept_ref[rows, :])
            mlp_ref[rows, :] = narrow(normed * vec(vec_ref, GAIN2) + vec(vec_ref, SHIFT2))
            g = jnp.concatenate([wide_of(gout_ref[f]), jnp.zeros((SPAN - TOK, D), WIDE)], 0)
            g_ref[rows, :] = narrow(g)
        mlpt_ref[...] = narrow(mm_t(perm_ref[...], mlp_ref[...]))
        acc_ref[...] = kept_ref[...] + vec(vec_ref, DOWN_B)
        dacc_ref[...] = jnp.zeros_like(dacc_ref)
        for copy in copies():
            copy.wait()

    assemble_up(place_ref, held_up_ref, up_ref, j)
    assemble_down(place_ref, held_down_ref, down_ref, j)
    mlp = mlp_ref[...]
    g = g_ref[...]
    up = up_ref[...]
    down = down_ref[...]
    hidden = mm(mlp, up) + vec_ref[pl.ds(UP_B + j, 1), :]
    sig = 1.0 / (1.0 + jnp.exp(-1.702 * hidden))
    act = narrow(hidden * sig)
    acc_ref[...] += mm(act, down)
    gact = wide_of(narrow(mm_t(g, down)))
    gh = narrow(gact * (sig + 1.702 * hidden * sig * (1.0 - sig)))
    dub_ref[0] = jnp.broadcast_to(jnp.sum(wide_of(gh), 0, keepdims=True), (8, CHUNK))
    dup = narrow(mm(mlpt_ref[...], gh))
    dup_keep_ref[...] = dup[: D // 2]
    dup_give_ref[...] = dup[D // 2 :]
    dacc_ref[...] += mm_t(gh, up)
    ddown = narrow(lax.dot_general(act, g, (((0,), (0,)), ((), ())), preferred_element_type=WIDE))
    for core in range(2):

        @pl.when(core_at == core)
        def _():
            for yl in range(2):
                for z in range(4):
                    at = (yl * 4 + z) * 2
                    down_keep_ref[yl, z, 0] = ddown[(at + core) * 48 : (at + core + 1) * 48]
                    down_give_ref[yl, z, 0] = ddown[(at + 1 - core) * 48 : (at + 2 - core) * 48]

    @pl.when(j == CHUNKS - 1)
    def _():
        for f in range(FRAMES):
            lay_ref[f] = narrow(acc_ref[f * SPAN : f * SPAN + TOK, :])
        dg = jnp.zeros((1, D), WIDE)
        dsh = jnp.zeros((1, D), WIDE)
        db = jnp.zeros((1, D), WIDE)
        for f in range(FRAMES):
            rows = pl.ds(f * SPAN, SPAN)
            normed, inverse = normed_of(kept_ref[rows, :])
            gm = dacc_ref[rows, :]
            gw = wide_of(g_ref[rows, :])
            dg += jnp.sum(gm * normed, 0, keepdims=True)
            dsh += jnp.sum(gm, 0, keepdims=True)
            db += jnp.sum(gw, 0, keepdims=True)
            gk = gw + norm_back(gm, normed, inverse, vec(vec_ref, GAIN2))
            gk_ref[rows, :] = jnp.where(valid_rows(gk.shape), gk, 0.0)
        sums_ref[...] = jnp.concatenate([dg, dsh, db, jnp.zeros((5, D), WIDE)], 0)


def once(shape):
    return pl.BlockSpec(shape, lambda *_: (0,) * len(shape), pipeline_mode=pl.Buffered(1))


def mlp(place, kept, gout, up, down, vectors, perm):
    down_spec = pl.BlockSpec((2, 4, 1, 48, D), lambda j: (j % 2, 0, j // 2, 0, 0))
    up_spec = pl.BlockSpec((D // 2, CHUNK), lambda j: (0, j))
    anywhere = pl.BlockSpec(memory_space=pl.ANY)
    return pl.pallas_call(
        mlp_kernel,
        grid=(CHUNKS,),
        in_specs=[pl.BlockSpec(memory_space=pltpu.SMEM), once((ROWS, D)), once((FRAMES, TOK, D)),
                  once((VECTOR_ROWS, D)), once((D, D))] + [anywhere] * 10,
        out_specs=[once((FRAMES, TOK, D)), once((ROWS, D)),
                   up_spec, up_spec, down_spec, down_spec,
                   once((8, D)), pl.BlockSpec((1, 8, CHUNK), lambda j: (j, 0, 0))],
        out_shape=(shaped(FRAMES, TOK, D), shaped(ROWS, D, dtype=WIDE), shaped(D // 2, FF), shaped(D // 2, FF),
                   shaped(4, 4, 2, 48, D), shaped(4, 4, 2, 48, D), shaped(8, D, dtype=WIDE),
                   shaped(CHUNKS, 8, CHUNK, dtype=WIDE)),
        scratch_shapes=[pltpu.VMEM((ROWS, D), LOW), pltpu.VMEM((D, ROWS), LOW), pltpu.VMEM((ROWS, D), LOW),
                        pltpu.VMEM((ROWS, D), WIDE), pltpu.VMEM((ROWS, D), WIDE),
                        pltpu.VMEM((4, 192, FF), LOW), pltpu.VMEM((8, 2, 96, 1536), LOW),
                        pltpu.VMEM((D, CHUNK), LOW), pltpu.VMEM((CHUNK, D), LOW), pltpu.SemaphoreType.DMA((10,))],
        compiler_params=pltpu.CompilerParams(vmem_limit_bytes=58 << 20),
        cost_estimate=cost(1),
        name="mlp_both_ways",
    )(place.reshape(1), kept, gout, vectors, perm, *up, *down)


def head_sums(go, o):
    t = wide_of(go) * wide_of(o)
    high = narrow(t)
    rest = narrow(t - wide_of(high))
    head = lax.broadcasted_iota(jnp.int32, (16, D), 0)
    lane = lax.broadcasted_iota(jnp.int32, (16, D), 1)
    pick = jnp.where((lane // HEAD_DIM) == head, 1.0, 0.0).astype(LOW)
    return mm_t(pick, high) + mm_t(pick, rest)


def out_back_kernel(gk_ref, mixed_ref, wout_ref, perm_ref, gmix_ref, dout_ref, sum_ref):
    gb = narrow(gk_ref[...])
    gmix_ref[...] = narrow(mm_t(gb, wout_ref[...]))
    turned = narrow(mm_t(perm_ref[...], mixed_ref[...]))
    dout_ref[...] = narrow(mm(turned, gb))
    sum_ref[...] = jnp.broadcast_to(jnp.sum(wide_of(gb), 0, keepdims=True), (8, D))


def out_back(gk, mixed, w_attn, perm):
    return pl.pallas_call(
        out_back_kernel,
        grid=(1,),
        in_specs=[whole(gk.shape), whole(mixed.shape), qkv_out_specs()[1], whole(perm.shape)],
        out_specs=(whole((ROWS, D)), whole((D, D)), whole((8, D))),
        out_shape=(shaped(ROWS, D), shaped(D, D), shaped(8, D, dtype=WIDE)),
        compiler_params=pltpu.CompilerParams(vmem_limit_bytes=48 << 20),
        cost_estimate=cost(1),
        name="attention_out_back",
    )(gk, mixed, w_attn, perm)


def attn_bwd_kernel(gmix_ref, mixed_ref, qkv_ref, lse_ref, msg_ref, wqkv_ref, vec_ref,
                    dqkv_ref, sums_ref, gmsg_ref,
                    kt_ref, dqt_ref, rows_ref):
    def frame(f, _):
        rows = pl.ds(pl.multiple_of(f * SPAN, SPAN), SPAN)
        kt_ref[...] = qkv_ref[rows, D : 2 * D].T
        dots = head_sums(gmix_ref[rows, :], mixed_ref[rows, :])
        for p in range(PAIRS):
            cols = lambda part: slice(part * D + p * 128, part * D + (p + 1) * 128)
            q, k, v = (qkv_ref[rows, cols(i)] for i in range(3))
            go = gmix_ref[rows, cols(0)]
            lse = [lse_ref[f, 2 * p + h : 2 * p + h + 1, :] for h in range(2)]
            dot = [dots[2 * p + h : 2 * p + h + 1, :] for h in range(2)]
            dqt, dk, dv = attend_bwd(q, k, v, kt_ref[cols(0), :], go, lse, dot, frame_mask)
            dqt_ref[cols(0), :] = dqt
            dqkv_ref[rows, cols(1)] = dk
            dqkv_ref[rows, cols(2)] = dv
        dqkv_ref[rows, :D] = dqt_ref[...].T
        return 0

    lax.fori_loop(0, FRAMES, frame, 0)
    dqb = jnp.zeros((1, D), WIDE)
    dvb = jnp.zeros((1, D), WIDE)
    for f in range(FRAMES):
        rows = pl.ds(f * SPAN, SPAN)
        dqb += jnp.sum(wide_of(dqkv_ref[rows, :D]), 0, keepdims=True)
        dvb += jnp.sum(wide_of(dqkv_ref[rows, 2 * D :]), 0, keepdims=True)
        tile = wide_of(dqkv_ref[f * SPAN + 192 : f * SPAN + 208, :])
        rows_ref[f : f + 1, :] = tile[TOK - 192 : TOK - 191, :]
    rows_ref[FRAMES:, :] = jnp.zeros((8 - FRAMES, 3 * D), WIDE)
    sums_ref[...] = jnp.concatenate([dqb, dvb, jnp.zeros((6, D), WIDE)], 0)
    back = mm_t(narrow(rows_ref[...]), wqkv_ref[...])
    normed, inverse = normed_of(msg_ref[...])
    gmsg_ref[...] = norm_back(back[:FRAMES], normed, inverse, vec(vec_ref, GAIN1))


def attn_bwd(gmix, mixed, qkv, lse, msg, w_attn, vectors):
    return pl.pallas_call(
        attn_bwd_kernel,
        grid=(1,),
        in_specs=[whole(gmix.shape), whole(mixed.shape), whole(qkv.shape), whole(lse.shape), whole(msg.shape),
                  qkv_out_specs()[0], whole(vectors.shape)],
        out_specs=(whole((ROWS, 3 * D)), whole((8, D)), whole((FRAMES, D))),
        out_shape=(shaped(ROWS, 3 * D), shaped(8, D, dtype=WIDE), shaped(FRAMES, D, dtype=WIDE)),
        scratch_shapes=[pltpu.VMEM((D, SPAN), LOW), pltpu.VMEM((D, SPAN), LOW), pltpu.VMEM((8, 3 * D), WIDE)],
        compiler_params=pltpu.CompilerParams(vmem_limit_bytes=56 << 20),
        cost_estimate=cost(1),
        name="frame_attention_back",
    )(gmix, mixed, qkv, lse, msg, w_attn, vectors)


def tokens_back_kernel(dqkv_ref, wqkv_ref, gk_ref, tok_ref, msg_ref, vec_ref, blk_ref, perm_ref, dout_ref, sums_ref,
                       out_ref, keep_ref, give_ref, joined_ref):
    turned = narrow(mm_t(perm_ref[...], blk_ref[...]))
    for n in range(3):
        cols = slice(n * D, (n + 1) * D)
        dw = narrow(mm(turned, dqkv_ref[:, cols]))
        keep_ref[:, cols] = dw[: D // 2]
        give_ref[:, cols] = dw[D // 2 :]
    keep_ref[:, 3 * D : FF] = dout_ref[: D // 2]
    give_ref[:, 3 * D : FF] = dout_ref[D // 2 :]
    fill_joined(tok_ref, msg_ref, joined_ref)
    dg = jnp.zeros((1, D), WIDE)
    dsh = jnp.zeros((1, D), WIDE)
    back_all = mm_t(dqkv_ref[...], wqkv_ref[...])
    for f in range(FRAMES):
        rows = pl.ds(f * SPAN, SPAN)
        back = back_all[f * SPAN : (f + 1) * SPAN]
        normed, inverse = normed_of(joined_ref[rows, :])
        dg += jnp.sum(back * normed, 0, keepdims=True)
        dsh += jnp.sum(back, 0, keepdims=True)
        full = gk_ref[rows, :] + norm_back(back, normed, inverse, vec(vec_ref, GAIN1))
        out_ref[f] = full[:TOK]
    sums = jnp.concatenate([dg, dsh, sums_ref[2:, :], jnp.zeros((112, D), WIDE)], 0)
    turned = narrow(mm_t(perm_ref[...], narrow(sums)))
    keep_ref[:, FF:] = turned[: D // 2]
    give_ref[:, FF:] = turned[D // 2 :]


def tokens_back(dqkv, w_attn, gk, tok, msg, vectors, blk, perm, dout, sums):
    return pl.pallas_call(
        tokens_back_kernel,
        grid=(1,),
        in_specs=[whole(dqkv.shape), qkv_out_specs()[0], whole(gk.shape), whole(tok.shape), whole(msg.shape),
                  whole(vectors.shape), whole(blk.shape), whole(perm.shape), whole(dout.shape), whole(sums.shape)],
        out_specs=(whole((FRAMES, TOK, D)), whole((D // 2, FF + 128)), whole((D // 2, FF + 128))),
        out_shape=(shaped(FRAMES, TOK, D, dtype=WIDE), shaped(D // 2, FF + 128), shaped(D // 2, FF + 128)),
        scratch_shapes=[pltpu.VMEM((ROWS, D), WIDE)],
        compiler_params=pltpu.CompilerParams(vmem_limit_bytes=56 << 20),
        cost_estimate=cost(1),
        name="tokens_back",
    )(dqkv, w_attn, gk, tok, msg, vectors, blk, perm, dout, sums)


ALL = 256


def group_mask(grow_ref, gcol_ref):
    same = gcol_ref[:, 0:1] == grow_ref[0:1, :]

    def mask(s):
        return jnp.where(same, s, -1000000000.0)

    return mask


def msg_fwd_kernel(cls_ref, w_ref, vec_ref, grow_ref, gcol_ref,
                   message_ref, token_ref, min_ref, qkv_ref, mixed_ref, lse_ref, vt_ref, ot_ref):
    message = mm(cls_ref[...], w_ref[:, :D]) + vec(vec_ref, FC_B)
    message_ref[...] = message
    normed, _ = normed_of(message)
    min_ref[...] = narrow(normed * vec(vec_ref, MSG_GAIN) + vec(vec_ref, MSG_SHIFT))
    for n in range(9):
        y = mm(min_ref[...], w_ref[:, D + n * 256 : D + (n + 1) * 256])
        if n < 3:
            y = y + vec_ref[MQ_B : MQ_B + 1, n * 256 : (n + 1) * 256]
        if n >= 6:
            y = y + vec_ref[MV_B : MV_B + 1, (n - 6) * 256 : (n - 5) * 256]
        qkv_ref[:, n * 256 : (n + 1) * 256] = narrow(y)
    vt_ref[...] = qkv_ref[:, 2 * D :].T
    mask = group_mask(grow_ref, gcol_ref)
    lse_ref[...] = jnp.zeros_like(lse_ref)
    for p in range(PAIRS):
        q = qkv_ref[:, p * 128 : (p + 1) * 128]
        k = qkv_ref[:, D + p * 128 : D + (p + 1) * 128]
        vt = vt_ref[p * 128 : (p + 1) * 128, :]
        for h, (o, l) in enumerate(attend_fwd(q, k, vt, None, mask)):
            at = p * 128 + h * HEAD_DIM
            ot_ref[at : at + HEAD_DIM, :] = narrow(o)
            lse_ref[2 * p + h : 2 * p + h + 1, :] = l
    mixed_ref[...] = ot_ref[...].T
    token_ref[...] = message + mm(mixed_ref[...], w_ref[:, 4 * D :]) + vec(vec_ref, MOUT_B)


def msg_fwd(cls, w, vectors, grow, gcol):
    return pl.pallas_call(
        msg_fwd_kernel,
        out_shape=(shaped(ALL, D, dtype=WIDE), shaped(ALL, D, dtype=WIDE), shaped(ALL, D), shaped(ALL, 3 * D),
                   shaped(ALL, D), shaped(16, ALL, dtype=WIDE)),
        scratch_shapes=[pltpu.VMEM((D, ALL), LOW), pltpu.VMEM((D, ALL), LOW)],
        compiler_params=pltpu.CompilerParams(vmem_limit_bytes=48 << 20),
        cost_estimate=cost(1),
        name="message_forward",
    )(cls, w, vectors, grow, gcol)


def msg_bwd_kernel(gm_ref, cls_ref, message_ref, min_ref, qkv_ref, mixed_ref, lse_ref, w_ref, vec_ref,
                   grow_ref, gcol_ref, pick_ref,
                   gcls_ref, dw_ref, sums_ref,
                   gmix_ref, kt_ref, dqt_ref, dqkv_ref):
    gb = gm_ref[...]
    pick = pick_ref[...]
    turned = lambda x: narrow(mm_t(pick, x))
    gmix_ref[...] = narrow(mm_t(gb, w_ref[:, 4 * D :]))
    dw_ref[:, 4 * D :] = mm(turned(mixed_ref[...]), gb)
    kt_ref[...] = qkv_ref[:, D : 2 * D].T
    mask = group_mask(grow_ref, gcol_ref)
    dots = head_sums(gmix_ref[...], mixed_ref[...])
    for p in range(PAIRS):
        cols = lambda part: slice(part * D + p * 128, part * D + (p + 1) * 128)
        q, k, v = (qkv_ref[:, cols(i)] for i in range(3))
        go = gmix_ref[:, cols(0)]
        lse = [lse_ref[2 * p + h : 2 * p + h + 1, :] for h in range(2)]
        dot = [dots[2 * p + h : 2 * p + h + 1, :] for h in range(2)]
        dqt, dk, dv = attend_bwd(q, k, v, kt_ref[cols(0), :], go, lse, dot, mask)
        dqt_ref[cols(0), :] = dqt
        dqkv_ref[:, cols(1)] = dk
        dqkv_ref[:, cols(2)] = dv
    dqkv_ref[:, :D] = dqt_ref[...].T
    dqkv = dqkv_ref[...]
    dw_ref[:, D : 4 * D] = mm(turned(min_ref[...]), dqkv)
    back = mm_t(dqkv, w_ref[:, D : 4 * D])
    normed, inverse = normed_of(message_ref[...])
    gfc = narrow(wide_of(gb) + norm_back(back, normed, inverse, vec(vec_ref, MSG_GAIN)))
    dw_ref[:, :D] = mm(turned(cls_ref[...]), gfc)
    gcls_ref[...] = mm_t(gfc, w_ref[:, :D])
    col = lambda x: jnp.sum(wide_of(x), 0, keepdims=True)
    sums_ref[...] = jnp.concatenate(
        [col(gfc), col(back * normed), col(back), col(gb), col(dqkv[:, :D]), col(dqkv[:, 2 * D :]),
         jnp.zeros((2, D), WIDE)], 0)


def msg_bwd(gm, cls, message, mins, qkv, mixed, lse, w, vectors, grow, gcol, pick):
    return pl.pallas_call(
        msg_bwd_kernel,
        out_shape=(shaped(ALL, D, dtype=WIDE), shaped(16, 5 * D, dtype=WIDE), shaped(8, D, dtype=WIDE)),
        scratch_shapes=[pltpu.VMEM((ALL, D), LOW), pltpu.VMEM((D, ALL), LOW), pltpu.VMEM((D, ALL), LOW),
                        pltpu.VMEM((ALL, 3 * D), LOW)],
        compiler_params=pltpu.CompilerParams(vmem_limit_bytes=48 << 20),
        cost_estimate=cost(1),
        name="message_back",
    )(gm, cls, message, mins, qkv, mixed, lse, w, vectors, grow, gcol, pick)


def frame_of(x_hi, y, z, core):
    return ((x_hi * 4 + y) * 4 + z) * 2 + core


PLACES = list(itertools.product(range(2), range(4), range(4), range(2), range(2)))


def moves(to):
    return [(frame_of(*p[:4]) * 2 + p[4], frame_of(*to(*p)[:4]) * 2 + to(*p)[4]) for p in PLACES]


TO_CORE = moves(lambda x, y, z, c, v: (x, y, z, 1 - c, v))
TO_VIDEO = moves(lambda x, y, z, c, v: (x, y, z, c, 1 - v))
TO_HALF = moves(lambda x, y, z, c, v: (1 - x, y, z, c, v))
TO_BOTH = moves(lambda x, y, z, c, v: (1 - x, y, z, c, 1 - v))
TO_Y = [moves(lambda x, y, z, c, v, k=k: (x, (y + k) % 4, z, c, v)) for k in range(4)]
TO_Z = [moves(lambda x, y, z, c, v, k=k: (x, y, (z + k) % 4, c, v)) for k in range(4)]
ALONG_Y = [[frame_of(x, y, z, c) for y in range(4)] for x in range(2) for z in range(4) for c in range(2)]
ALONG_Z = [[frame_of(x, y, z, c) for z in range(4)] for x in range(2) for y in range(4) for c in range(2)]
PLANE = [[frame_of(x, y, z, c) for y in range(4) for z in range(4)] for x in range(2) for c in range(2)]
def sent(x, pairs):
    return lax.ppermute(x, ("frame", "video"), pairs)


def to_everyone(x):
    return lax.all_to_all(jnp.broadcast_to(x[None], (64, *x.shape)), "frame", 0, 0, tiled=True)


def assemble_y_kernel(place_ref, *refs):
    pieces, out_ref, sems = refs[:8], refs[8], refs[9]
    x, y, _, core = place_parts(place_ref[0])
    span, half = 96, 1536
    copies = []
    for who in range(2):
        col = pl.multiple_of((core if who == 0 else 1 - core) * half, 128)
        for k in range(4):
            for h in range(2):
                row = pl.multiple_of(((x if h == 0 else 1 - x) * 4 + lax.rem(y + 4 - k, 4)) * span, span)
                copies.append(
                    pltpu.make_async_copy(
                        pieces[who * 4 + k].at[h],
                        out_ref.at[pl.ds(row, span), pl.ds(col, half)],
                        sems.at[len(copies)],
                    )
                )
                copies[-1].start()
    for done in copies:
        done.wait()


def assemble_z_kernel(place_ref, *refs):
    pieces, out_ref, held_ref, sems = refs[:-3], refs[-3], refs[-2], refs[-1]
    x, y, z, core = place_parts(place_ref[0])
    each = len(pieces) // 2
    half = pieces[0].shape[-1]
    copies = []
    for n, piece_ref in enumerate(pieces):
        col = pl.multiple_of((core if n < each else 1 - core) * half, 128)
        copies.append(pltpu.make_async_copy(piece_ref, held_ref.at[n % 4, :, pl.ds(col, half)], sems.at[n]))
        copies[-1].start()
    for done in copies:
        done.wait()
    for cols in range(0, 2 * half, D):
        for k in range(4):
            slabs = [
                wide_of(held_ref[lax.rem(z + 4 - to, 4), 48 * k : 48 * k + 48, cols : cols + D])
                for to in range(4)
            ]
            for h in range(2):
                row = pl.multiple_of(((x if h == 0 else 1 - x) * 4 + lax.rem(y + 4 - k, 4)) * 96, 96)
                out_ref[pl.ds(row, 96), cols : cols + D] = narrow(
                    jnp.concatenate([v[24 * h : 24 * h + 24] for v in slabs], 0)
                )


def assembled(kernel, place, pieces, out, scratch):
    anywhere = pl.BlockSpec(memory_space=pl.ANY)
    return pl.pallas_call(
        kernel,
        in_specs=[pl.BlockSpec(memory_space=pltpu.SMEM)] + [anywhere] * len(pieces),
        out_shape=out,
        scratch_shapes=scratch,
        compiler_params=pltpu.CompilerParams(vmem_limit_bytes=40 << 20),
        cost_estimate=cost(1),
        name="assemble_weights",
    )(place.reshape(1), *pieces)


def assemble_y(place, pieces):
    return assembled(assemble_y_kernel, place, pieces, shaped(D, FF), [pltpu.SemaphoreType.DMA((16,))])


def assemble_z(place, pieces):
    half = pieces[0].shape[-1]
    scratch = [pltpu.VMEM((4, 192, 2 * half), LOW), pltpu.SemaphoreType.DMA((len(pieces),))]
    return assembled(assemble_z_kernel, place, pieces, shaped(D, 2 * half), scratch)


def core_pair(place, shards):
    core = place % 2

    def half(which):
        cut = [lax.dynamic_slice_in_dim(w, which * (w.shape[1] // 2), w.shape[1] // 2, 1) for w in shards]
        return jnp.concatenate(cut, 1)

    mine, got = half(core), sent(half(1 - core), TO_CORE)
    return jnp.where(core == 0, jnp.concatenate([mine, got], 0), jnp.concatenate([got, mine], 0))


def both_x(pair):
    return jnp.stack([pair, sent(pair, TO_HALF)])


def ring_z(pair):
    return jnp.swapaxes(all_z(pair)[0], 0, 1).reshape(2, -1, pair.shape[2])


def ring_y(pair):
    return jnp.stack([pair, *(sent(pair, TO_Y[k]) for k in range(1, 4))]).reshape(192, -1)


def around(x, moves_by):
    return [x, *(sent(x, moves_by[k]) for k in range(1, 4))]


def all_z(x):
    copies = jnp.broadcast_to(x[None], (4, *x.shape))
    return [lax.all_to_all(copies, "frame", 0, 0, axis_index_groups=ALONG_Z, tiled=True)]


def both_cores(pieces):
    return [*pieces, *(sent(x, TO_CORE) for x in pieces)]


def after(x, *others):
    return lax.optimization_barrier((x, *others))


def row_order(place):
    row = jnp.arange(D, dtype=jnp.int32)
    r, x, z, y, c = row % 12, row // 12 % 2, row // 24 % 4, row // 96 % 4, row // 384
    natural = ((((x * 4 + y) * 4 + z) * 2) + jnp.where(c == 0, place % 2, 1 - place % 2)) * 12 + r
    return (natural[:, None] == row[None, :]).astype(LOW)


def add_pack_kernel(keep_up, got_up, keep_down, got_down, out_ref):
    up = wide_of(keep_up[...]) + wide_of(got_up[...])
    down = wide_of(keep_down[0]) + wide_of(got_down[0])
    for i in range(2):
        out_ref[i, :, :FF] = narrow(up[24 * i : 24 * i + 24])
        slab = jnp.concatenate([down[i, 0], down[i, 1]], 0)
        for q in range(4):
            both = [slab[48 * h + 12 * q : 48 * h + 12 * q + 12] for h in range(2)]
            out_ref[i, :, FF + q * D : FF + (q + 1) * D] = narrow(jnp.concatenate(both, 0))


def add_pack(keep_up, got_up, keep_down, got_down):
    down_spec = pl.BlockSpec((1, 2, 2, 48, D), lambda i: (i // 2, i % 2, 0, 0, 0))
    up_spec = pl.BlockSpec((48, FF), lambda i: (i, 0))
    return pl.pallas_call(
        add_pack_kernel,
        grid=(8,),
        in_specs=[up_spec, up_spec, down_spec, down_spec],
        out_specs=pl.BlockSpec((2, 24, 2 * FF), lambda i: (i, 0, 0)),
        out_shape=shaped(16, 24, 2 * FF),
        compiler_params=pltpu.CompilerParams(vmem_limit_bytes=32 << 20),
        cost_estimate=cost(1),
        name="add_mlp_gradients",
    )(keep_up, got_up, keep_down, got_down)


def ring_sum(parts, groups):
    return lax.psum_scatter(parts, "frame", scatter_dimension=0, axis_index_groups=groups, tiled=True)


def plane_sum(parts):
    got = lax.all_to_all(parts, "frame", 0, 0, axis_index_groups=PLANE, tiled=True)
    return narrow(jnp.sum(wide_of(got), 0))


def last_sum(rows, half):
    mine, other = (lax.dynamic_slice_in_dim(rows, which * 12, 12, 0) for which in (half, 1 - half))
    return wide_of(mine) + wide_of(sent(mine, TO_VIDEO)) + wide_of(sent(other, TO_HALF)) + wide_of(sent(other, TO_BOTH))


def shards(
    tokens_in,
    clip_ids,
    grad_out,
    msg_fc_w,
    msg_fc_b,
    msg_norm_gain,
    msg_norm_shift,
    msg_qkv_w,
    msg_qv_b,
    msg_out_w,
    msg_out_b,
    norm1_gain,
    norm1_shift,
    attn_qkv_w,
    attn_qv_b,
    attn_out_w,
    attn_out_b,
    norm2_gain,
    norm2_shift,
    mlp_in_w,
    mlp_in_b,
    mlp_out_w,
    mlp_out_b,
):
    place = lax.axis_index("frame").astype(jnp.int32)
    core, half = place % 2, place // 32
    tok = tokens_in[0]
    small = jnp.concatenate(
        [
            tok[:, 0, :].reshape(-1),
            msg_fc_b,
            msg_norm_gain,
            msg_norm_shift,
            msg_out_b,
            norm1_gain,
            norm1_shift,
            attn_out_b,
            norm2_gain,
            norm2_shift,
            mlp_out_b,
            msg_qv_b,
            attn_qv_b,
            mlp_in_b,
            clip_ids[0].astype(LOW),
        ]
    )
    small = jnp.pad(small, (0, 4096 - small.shape[0])).reshape(32, 128)
    w_cols = ((attn_qkv_w, attn_out_w), (msg_fc_w, msg_qkv_w, msg_out_w), (mlp_in_w,))
    w_pair = core_pair(place, [jnp.concatenate(w, 1) for w in w_cols])
    down_pair = core_pair(place, [mlp_out_w]).reshape(4, 24, 384).transpose(1, 0, 2).reshape(24, 1536)
    w_x = both_x(jnp.concatenate([w_pair[:, :1536], down_pair, w_pair[:, 1536:]], 1))
    by_y, by_z = ring_z(w_x[:, :, :3072]), ring_y(w_x[:, :, 3072:])
    by_y, by_z, small = after(by_y, by_z, small)
    small_all = to_everyone(small)
    msg_all, attn_all = around(by_z[:, :1920], TO_Z), around(by_y[:, :, :1536], TO_Y)
    msg_all, attn_all, small_all, late_y, late_z = after(
        msg_all, attn_all, small_all, by_y[:, :, 1536:], by_z[:, 1920:]
    )
    up_all, down_all = all_z(late_z), around(late_y, TO_Y)
    small_all = small_all.reshape(64, 4096)
    cls = small_all[:, :3072].reshape(ALL, D)
    at = 3072
    vectors = small_all[:, at : at + 120].reshape(64, 10, 12).transpose(1, 0, 2).reshape(10, D)
    biases = [small_all[:, at + 120 + a : at + 120 + b].reshape(-1, D) for a, b in ((0, 24), (24, 48), (48, 96))]
    vectors = wide_of(jnp.concatenate([vectors, *biases, jnp.zeros((VECTOR_ROWS - 18, D), LOW)], 0))
    at = at + 216
    groups = wide_of(small_all[:, at : at + 4].reshape(ALL))
    grow = jnp.broadcast_to(groups[None], (8, ALL))
    gcol = jnp.broadcast_to(groups[:, None], (ALL, 128))
    order = row_order(place)
    pick_row = jnp.arange(16, dtype=jnp.int32)[:, None]
    pick_col = jnp.arange(D, dtype=jnp.int32)[None, :]
    pick = ((pick_row < 12) & (pick_col == place * 12 + pick_row)).astype(LOW)

    msg_all, vectors, order, pick, cls, grow, gcol = after(msg_all, vectors, order, pick, cls, grow, gcol)
    w_msg = assemble_z(place, both_cores(msg_all))
    message, token, mins, mqkv, mmixed, mlse = msg_fwd(cls, w_msg, vectors, grow, gcol)
    token, attn_all = after(token, attn_all)
    w_attn = assemble_y(place, both_cores(attn_all))
    msg = lax.dynamic_slice_in_dim(token, place * FRAMES, FRAMES)
    qkv, mixed, kept, lse, blk = attn_fwd(tok, msg, w_attn, vectors)
    kept, up_all, down_all = after(kept, up_all, down_all)
    lay, gk, dup_keep, dup_give, down_keep, down_give, sums_mlp, dub = mlp(
        place, kept, grad_out[0], both_cores(up_all), both_cores(down_all), vectors, order
    )
    dup_got, down_got = sent(dup_give, TO_CORE), sent(down_give, TO_CORE)
    gmix, dout, sum_out = out_back(gk, mixed, w_attn, order)
    gmix, dup_got, down_got = after(gmix, dup_got, down_got)
    mlp_parts, gmix = after(add_pack(dup_keep, dup_got, down_keep, down_got), gmix)
    mlp_half = ring_sum(mlp_parts, ALONG_Y)
    dqkv, sums_attn, gmsg = attn_bwd(gmix, mixed, qkv, lse, msg, w_attn, vectors)
    gmsg = jnp.broadcast_to(narrow(gmsg)[None], (64, FRAMES, D))
    gmsg, dqkv = after(gmsg, dqkv)
    gmsg_all = lax.all_to_all(gmsg, "frame", 0, 0, tiled=True).reshape(ALL, D)
    by_place = lambda x, n: x.reshape(64, n, 12).transpose(1, 0, 2).reshape(n, D)
    sums = jnp.concatenate(
        [jnp.zeros((2, D), WIDE), sum_out[:1], sums_mlp[:3], by_place(sums_attn[:2], 2), by_place(dub[:, 0], 4),
         jnp.zeros((4, D), WIDE)], 0
    )
    grad_tokens, attn_keep, attn_give = tokens_back(dqkv, w_attn, gk, tok, msg, vectors, blk, order, dout, sums)
    attn_keep, attn_give, gmsg_all, mlp_half = after(attn_keep, attn_give, gmsg_all, mlp_half)
    mlp_sum = ring_sum(mlp_half, ALONG_Z).reshape(24, 2 * FF)
    attn_got = sent(attn_give, TO_CORE)
    gcls, dw_msg, sums_msg = msg_bwd(gmsg_all, cls, message, mins, mqkv, mmixed, mlse, w_msg, vectors, grow, gcol, pick)
    attn_got, gcls, dw_msg, sums_msg = after(attn_got, gcls, dw_msg, sums_msg)
    attn_part = narrow(wide_of(attn_keep) + wide_of(attn_got))
    attn_part, gcls, dw_msg, sums_msg = after(attn_part, gcls, dw_msg, sums_msg)
    attn_sum = plane_sum(attn_part.reshape(16, 24, FF + 128))
    gcls = lax.dynamic_slice_in_dim(gcls, place * FRAMES, FRAMES)
    grad_tokens = grad_tokens.at[:, 0, :].add(gcls)
    own = lax.dynamic_slice_in_dim(sums_msg[:4], place * 12, 12, 1).reshape(-1)
    own_qv = lax.dynamic_slice_in_dim(sums_msg[4:6].reshape(-1), place * 24, 24)
    own = jnp.concatenate([own, own_qv])
    own = own + sent(own, TO_VIDEO)
    fb, mg, ms, mob, mqvb = jnp.split(own, [12, 24, 36, 48])
    msg_rows = dw_msg[:12]
    msg_rows = msg_rows + wide_of(sent(narrow(msg_rows), TO_VIDEO))
    mlp_sum, msg_rows = after(mlp_sum, msg_rows)
    mlp_rows = last_sum(mlp_sum, half)
    down_rows = mlp_rows[:, FF:].reshape(12, 4, D).transpose(1, 0, 2).reshape(48, D)
    attn_sum, mlp_rows, down_rows = after(attn_sum, mlp_rows, down_rows)
    rows = last_sum(attn_sum, half)
    ends = rows[:, FF : FF + 12].T
    g1, s1, ob, g2, s2, db = (ends[k] for k in range(6))
    qvb, ub = ends[6:8].reshape(-1), ends[8:12].reshape(-1)
    return (
        lay[None],
        grad_tokens[None],
        msg_rows[:, :D],
        fb,
        mg,
        ms,
        msg_rows[:, D : 4 * D],
        mqvb,
        msg_rows[:, 4 * D :],
        mob,
        g1,
        s1,
        rows[:, : 3 * D],
        qvb,
        rows[:, 3 * D : FF],
        ob,
        g2,
        s2,
        mlp_rows[:, :FF],
        ub,
        down_rows,
        db,
    )


def solution(mesh):
    in_specs = (
        P("video", "frame", None, None),
        P("video", "frame"),
        P("video", "frame", None, None),
        P("frame", None),
        P("frame"),
        P("frame"),
        P("frame"),
        P("frame", None),
        P("frame"),
        P("frame", None),
        P("frame"),
        P("frame"),
        P("frame"),
        P("frame", None),
        P("frame"),
        P("frame", None),
        P("frame"),
        P("frame"),
        P("frame"),
        P("frame", None),
        P("frame"),
        P("frame", None),
        P("frame"),
    )
    out_specs = (
        P("video", "frame", None, None),
        P("video", "frame", None, None),
        P("frame", None),
        P("frame"),
        P("frame"),
        P("frame"),
        P("frame", None),
        P("frame"),
        P("frame", None),
        P("frame"),
        P("frame"),
        P("frame"),
        P("frame", None),
        P("frame"),
        P("frame", None),
        P("frame"),
        P("frame"),
        P("frame"),
        P("frame", None),
        P("frame"),
        P("frame", None),
        P("frame"),
    )
    return jax.shard_map(shards, mesh=mesh, in_specs=in_specs, out_specs=out_specs, check_vma=False)
```

```python
import functools
import itertools
import jax
import jax.numpy as jnp
from jax import lax
from jax.experimental import pallas as pl
from jax.experimental.pallas import tpu as pltpu
from jax.sharding import PartitionSpec as P

HEAD_DIM = 64
FRAMES = 4
TOK = 197
SPAN = 208
ROWS = FRAMES * SPAN
D = 768
FF = 3072
HEADS = 12
PAIRS = 6
WIDE = jnp.float32
LOW = jnp.bfloat16
SCALE = HEAD_DIM ** (-0.5)
FC_B, MSG_GAIN, MSG_SHIFT, MOUT_B, GAIN1, SHIFT1, OUT_B, GAIN2, SHIFT2, DOWN_B, MQ_B, MV_B, Q_B, V_B, UP_B = range(15)
VECTOR_ROWS = 24


def narrow(x):
    return x.astype(LOW)


def wide_of(x):
    return x.astype(WIDE)


def mm(a, b):
    return lax.dot_general(a, b, (((1,), (0,)), ((), ())), preferred_element_type=WIDE)


def mm_t(a, b):
    return lax.dot_general(a, b, (((1,), (1,)), ((), ())), preferred_element_type=WIDE)


def normed_of(x):
    center = x - jnp.mean(x, -1, keepdims=True)
    inverse = lax.rsqrt(jnp.mean(center * center, -1, keepdims=True) + 1e-05)
    return center * inverse, inverse


def norm_back(grad, normed, inverse, gain):
    scaled = grad * gain
    return inverse * (
        scaled
        - jnp.mean(scaled, -1, keepdims=True)
        - normed * jnp.mean(scaled * normed, -1, keepdims=True)
    )


def own_lanes(x, which):
    lane = lax.broadcasted_iota(jnp.int32, x.shape, 1)
    return jnp.where((lane < HEAD_DIM) == (which == 0), x, jnp.zeros_like(x))


def either(a, b):
    lane = lax.broadcasted_iota(jnp.int32, a.shape, 1)
    return jnp.where(lane < HEAD_DIM, a, b)


def vec(vec_ref, row):
    return vec_ref[row : row + 1, :]


def fill_joined(tok_ref, msg_ref, joined_ref):
    for f in range(FRAMES):
        joined_ref[f * SPAN : f * SPAN + TOK, :] = wide_of(tok_ref[f])
        joined_ref[f * SPAN + TOK : f * SPAN + TOK + 1, :] = msg_ref[f : f + 1, :]
        joined_ref[f * SPAN + TOK + 1 : (f + 1) * SPAN, :] = jnp.zeros((SPAN - TOK - 1, D), WIDE)


def attend_fwd(q, k, vt, valid, mask):
    out = []
    for h in range(2):
        s = mm_t(own_lanes(k, h), q) * SCALE
        s = mask(s)
        peak = jnp.max(s, 0, keepdims=True)
        e = jnp.exp(s - peak)
        total = jnp.sum(e, 0, keepdims=True)
        o = mm(vt[h * HEAD_DIM : (h + 1) * HEAD_DIM], narrow(e)) / total
        out.append((o, peak + jnp.log(total)))
    return out


def attend_bwd(q, k, v, kt, go, lse, dot, mask):
    dqt, dk, dv = [], [], []
    for h in range(2):
        s = mask(mm_t(own_lanes(k, h), q) * SCALE)
        p = jnp.exp(s - lse[h])
        dp = mm_t(own_lanes(v, h), go)
        ds = narrow(p * (dp - dot[h]))
        dv.append(mm(narrow(p), go))
        dk.append(mm(ds, q))
        dqt.append(mm(kt[h * HEAD_DIM : (h + 1) * HEAD_DIM], ds))
    return (
        narrow(jnp.concatenate(dqt, 0) * SCALE),
        narrow(either(*dk) * SCALE),
        narrow(either(*dv)),
    )


def frame_mask(s):
    key = lax.broadcasted_iota(jnp.int32, s.shape, 0)
    return jnp.where(key <= TOK, s, -1e30)


def attn_fwd_kernel(tok_ref, msg_ref, wqkv_ref, wout_ref, vec_ref,
                    qkv_ref, mixed_ref, kept_ref, lse_ref, blk_ref, vt_ref, ot_ref):
    fill_joined(tok_ref, msg_ref, kept_ref)
    for f in range(FRAMES):
        rows = pl.ds(f * SPAN, SPAN)
        normed, _ = normed_of(kept_ref[rows, :])
        blk_ref[rows, :] = narrow(normed * vec(vec_ref, GAIN1) + vec(vec_ref, SHIFT1))
    for n in range(9):
        cols = pl.ds(n * 256, 256)
        y = mm(blk_ref[...], wqkv_ref[:, cols])
        if n < 3:
            y = y + vec_ref[Q_B : Q_B + 1, n * 256 : (n + 1) * 256]
        if n >= 6:
            y = y + vec_ref[V_B : V_B + 1, (n - 6) * 256 : (n - 5) * 256]
        qkv_ref[:, cols] = narrow(y)
    lse_ref[...] = jnp.zeros_like(lse_ref)

    def frame(f, _):
        rows = pl.ds(pl.multiple_of(f * SPAN, SPAN), SPAN)
        vt_ref[...] = qkv_ref[rows, 2 * D :].T
        for p in range(PAIRS):
            q = qkv_ref[rows, p * 128 : (p + 1) * 128]
            k = qkv_ref[rows, D + p * 128 : D + (p + 1) * 128]
            vt = vt_ref[p * 128 : (p + 1) * 128, :]
            for h, (o, l) in enumerate(attend_fwd(q, k, vt, None, frame_mask)):
                at = p * 128 + h * HEAD_DIM
                ot_ref[at : at + HEAD_DIM, :] = narrow(o)
                lse_ref[f, 2 * p + h : 2 * p + h + 1, :] = l
        mixed_ref[rows, :] = ot_ref[...].T
        return 0

    lax.fori_loop(0, FRAMES, frame, 0)
    kept_ref[...] = kept_ref[...] + mm(mixed_ref[...], wout_ref[...]) + vec(vec_ref, OUT_B)


def cost(us):
    return pl.CostEstimate(flops=int(us * 1e6), bytes_accessed=int(us * 1e3), transcendentals=0)


def qkv_out_specs():
    return [pl.BlockSpec((D, 3 * D), lambda *_: (0, 0)), pl.BlockSpec((D, D), lambda *_: (0, 3))]


def whole(shape):
    return pl.BlockSpec(shape, lambda *_: (0,) * len(shape))


def shaped(*shape, dtype=LOW):
    return jax.ShapeDtypeStruct(shape, dtype)


def attn_fwd(tok, msg, w_attn, vectors):
    return pl.pallas_call(
        attn_fwd_kernel,
        grid=(1,),
        in_specs=[whole(tok.shape), whole(msg.shape), *qkv_out_specs(), whole(vectors.shape)],
        out_specs=(whole((ROWS, 3 * D)), whole((ROWS, D)), whole((ROWS, D)), whole((FRAMES, 16, SPAN)), whole((ROWS, D))),
        out_shape=(shaped(ROWS, 3 * D), shaped(ROWS, D), shaped(ROWS, D, dtype=WIDE),
                   shaped(FRAMES, 16, SPAN, dtype=WIDE), shaped(ROWS, D)),
        scratch_shapes=[pltpu.VMEM((D, SPAN), LOW), pltpu.VMEM((D, SPAN), LOW)],
        compiler_params=pltpu.CompilerParams(vmem_limit_bytes=30 << 20),
        cost_estimate=cost(1),
        name="frame_attention",
    )(tok, msg, w_attn, w_attn, vectors)


def framed_kernel(x_ref, out_ref):
    for f in range(FRAMES):
        rows = jnp.concatenate([wide_of(x_ref[f]), jnp.zeros((SPAN - TOK, D), WIDE)], 0)
        out_ref[f * SPAN : (f + 1) * SPAN, :] = narrow(rows)


def framed(x):
    return pl.pallas_call(
        framed_kernel,
        out_shape=shaped(ROWS, D),
        compiler_params=pltpu.CompilerParams(vmem_limit_bytes=10 << 20),
        cost_estimate=cost(1),
        name="framed",
    )(x)


def valid_rows(shape, first=0):
    row = lax.broadcasted_iota(jnp.int32, shape, 0) + first
    return row % SPAN < TOK


def place_parts(place):
    return lax.div(place, 32), lax.rem(lax.div(place, 8), 4), lax.rem(lax.div(place, 2), 4), lax.rem(place, 2)


CHUNK = 768
CHUNKS = FF // CHUNK


def assemble_up(place_ref, held_ref, out_ref, j):
    x, y, _, _ = place_parts(place_ref[0])
    cols = pl.ds(pl.multiple_of(j * CHUNK, CHUNK), CHUNK)
    for k in range(4):
        slabs = [wide_of(held_ref[z, 48 * k : 48 * k + 48, cols]) for z in range(4)]
        for h in range(2):
            row = pl.multiple_of(((x if h == 0 else 1 - x) * 4 + lax.rem(y + 4 - k, 4)) * 96, 96)
            out_ref[pl.ds(row, 96), :] = narrow(jnp.concatenate([v[24 * h : 24 * h + 24] for v in slabs], 0))


def assemble_down(place_ref, held_ref, out_ref, j):
    x, y, _, core = place_parts(place_ref[0])
    side = lax.rem(lax.div(j, 2) + x, 2)
    for who in range(2):
        col = pl.multiple_of((core if who == 0 else 1 - core) * (D // 2), 128)
        for yl in range(2):
            piece = who * 4 + lax.rem(y + 4 - (lax.rem(j, 2) * 2 + yl), 4)
            for pair in range(2):
                slab = wide_of(held_ref[piece, side, 48 * pair : 48 * pair + 48, :])
                parts = [slab[24 * z : 24 * z + 24, q * (D // 2) : (q + 1) * (D // 2)] for z in range(2) for q in range(4)]
                at = yl * 384 + pair * 192
                out_ref[at : at + 192, pl.ds(col, D // 2)] = narrow(jnp.concatenate(parts, 0))


def mlp_kernel(place_ref, kept_ref, g_ref, vec_ref, perm_ref, *refs):
    up_pieces, down_pieces = refs[:2], refs[2:10]
    lay_ref, gk_ref, dup_keep_ref, dup_give_ref, down_keep_ref, down_give_ref, sums_ref, dub_ref = refs[10:18]
    mlp_ref, mlpt_ref, gt_ref, acc_ref, dacc_ref, held_up_ref, held_down_ref, up_ref, down_ref, sems = refs[18:]
    j = pl.program_id(0)
    core_at = lax.rem(place_ref[0], 2)

    def copies():
        for who in range(2):
            col = pl.multiple_of((core_at if who == 0 else 1 - core_at) * (FF // 2), 128)
            yield pltpu.make_async_copy(up_pieces[who], held_up_ref.at[:, :, pl.ds(col, FF // 2)], sems.at[who])
        for n in range(8):
            yield pltpu.make_async_copy(down_pieces[n], held_down_ref.at[n], sems.at[2 + n])

    @pl.when(j == 0)
    def _():
        for copy in copies():
            copy.start()

    @pl.when(j == 0)
    def _():
        for f in range(FRAMES):
            rows = pl.ds(f * SPAN, SPAN)
            normed, _ = normed_of(kept_ref[rows, :])
            mlp_ref[rows, :] = narrow(normed * vec(vec_ref, GAIN2) + vec(vec_ref, SHIFT2))
        mlpt_ref[...] = narrow(mm_t(perm_ref[...], mlp_ref[...]))
        gt_ref[...] = g_ref[...].T
        acc_ref[...] = kept_ref[...] + vec(vec_ref, DOWN_B)
        dacc_ref[...] = jnp.zeros_like(dacc_ref)
        for copy in copies():
            copy.wait()

    assemble_up(place_ref, held_up_ref, up_ref, j)
    assemble_down(place_ref, held_down_ref, down_ref, j)
    mlp = mlp_ref[...]
    g = g_ref[...]
    up = up_ref[...]
    down = down_ref[...]
    hidden = mm(mlp, up) + vec_ref[pl.ds(UP_B + j, 1), :]
    sig = 0.5 * jnp.tanh(0.851 * hidden) + 0.5
    gated = hidden * sig
    act = narrow(gated)
    acc_ref[...] += mm(act, down)
    gact = wide_of(narrow(mm_t(g, down)))
    gh = narrow(gact * (sig + 1.702 * gated * (1.0 - sig)))
    dub_ref[0] = jnp.broadcast_to(jnp.sum(wide_of(gh), 0, keepdims=True), (8, CHUNK))
    dup = narrow(mm(mlpt_ref[...], gh))
    dup_keep_ref[...] = dup[: D // 2]
    dup_give_ref[...] = dup[D // 2 :]
    dacc_ref[...] += mm_t(gh, up)
    ddown = narrow(mm(gt_ref[...], act).T)
    for core in range(2):

        @pl.when(core_at == core)
        def _():
            for yl in range(2):
                for z in range(4):
                    at = (yl * 4 + z) * 2
                    down_keep_ref[yl, z, 0] = ddown[(at + core) * 48 : (at + core + 1) * 48]
                    down_give_ref[yl, z, 0] = ddown[(at + 1 - core) * 48 : (at + 2 - core) * 48]

    @pl.when(j == CHUNKS - 1)
    def _():
        for f in range(FRAMES):
            lay_ref[f] = narrow(acc_ref[f * SPAN : f * SPAN + TOK, :])
        dg = jnp.zeros((1, D), WIDE)
        dsh = jnp.zeros((1, D), WIDE)
        db = jnp.zeros((1, D), WIDE)
        for f in range(FRAMES):
            rows = pl.ds(f * SPAN, SPAN)
            normed, inverse = normed_of(kept_ref[rows, :])
            gm = dacc_ref[rows, :]
            gw = wide_of(g_ref[rows, :])
            dg += jnp.sum(gm * normed, 0, keepdims=True)
            dsh += jnp.sum(gm, 0, keepdims=True)
            db += jnp.sum(gw, 0, keepdims=True)
            gk = gw + norm_back(gm, normed, inverse, vec(vec_ref, GAIN2))
            gk_ref[rows, :] = jnp.where(valid_rows(gk.shape), gk, 0.0)
        sums_ref[...] = jnp.concatenate([dg, dsh, db, jnp.zeros((5, D), WIDE)], 0)


def once(shape):
    return pl.BlockSpec(shape, lambda *_: (0,) * len(shape), pipeline_mode=pl.Buffered(1))


def mlp(place, kept, grads, up, down, vectors, perm):
    down_spec = pl.BlockSpec((2, 4, 1, 48, D), lambda j: (j % 2, 0, j // 2, 0, 0))
    up_spec = pl.BlockSpec((D // 2, CHUNK), lambda j: (0, j))
    anywhere = pl.BlockSpec(memory_space=pltpu.HBM)
    return pl.pallas_call(
        mlp_kernel,
        grid=(CHUNKS,),
        in_specs=[pl.BlockSpec(memory_space=pltpu.SMEM), once((ROWS, D)), once((ROWS, D)),
                  once((VECTOR_ROWS, D)), once((D, D))] + [anywhere] * 10,
        out_specs=[once((FRAMES, TOK, D)), once((ROWS, D)),
                   up_spec, up_spec, down_spec, down_spec,
                   once((8, D)), pl.BlockSpec((1, 8, CHUNK), lambda j: (j, 0, 0))],
        out_shape=(shaped(FRAMES, TOK, D), shaped(ROWS, D, dtype=WIDE), shaped(D // 2, FF), shaped(D // 2, FF),
                   shaped(4, 4, 2, 48, D), shaped(4, 4, 2, 48, D), shaped(8, D, dtype=WIDE),
                   shaped(CHUNKS, 8, CHUNK, dtype=WIDE)),
        scratch_shapes=[pltpu.VMEM((ROWS, D), LOW), pltpu.VMEM((D, ROWS), LOW), pltpu.VMEM((D, ROWS), LOW),
                        pltpu.VMEM((ROWS, D), WIDE), pltpu.VMEM((ROWS, D), WIDE),
                        pltpu.VMEM((4, 192, FF), LOW), pltpu.VMEM((8, 2, 96, 1536), LOW),
                        pltpu.VMEM((D, CHUNK), LOW), pltpu.VMEM((CHUNK, D), LOW), pltpu.SemaphoreType.DMA((10,))],
        compiler_params=pltpu.CompilerParams(vmem_limit_bytes=52 << 20),
        cost_estimate=cost(1),
        name="mlp_both_ways",
    )(place.reshape(1), kept, grads, vectors, perm, *up, *down)


def head_sums(go, o):
    t = wide_of(go) * wide_of(o)
    high = narrow(t)
    rest = narrow(t - wide_of(high))
    head = lax.broadcasted_iota(jnp.int32, (16, D), 0)
    lane = lax.broadcasted_iota(jnp.int32, (16, D), 1)
    pick = jnp.where((lane // HEAD_DIM) == head, 1.0, 0.0).astype(LOW)
    return mm_t(pick, high) + mm_t(pick, rest)


def out_back_kernel(gk_ref, mixed_ref, wout_ref, perm_ref, gmix_ref, dout_ref, sum_ref):
    gb = narrow(gk_ref[...])
    gmix_ref[...] = narrow(mm_t(gb, wout_ref[...]))
    turned = narrow(mm_t(perm_ref[...], mixed_ref[...]))
    dout_ref[...] = narrow(mm(turned, gb))
    sum_ref[...] = jnp.broadcast_to(jnp.sum(wide_of(gb), 0, keepdims=True), (8, D))


def out_back(gk, mixed, w_attn, perm):
    return pl.pallas_call(
        out_back_kernel,
        grid=(1,),
        in_specs=[whole(gk.shape), whole(mixed.shape), qkv_out_specs()[1], whole(perm.shape)],
        out_specs=(whole((ROWS, D)), whole((D, D)), whole((8, D))),
        out_shape=(shaped(ROWS, D), shaped(D, D), shaped(8, D, dtype=WIDE)),
        compiler_params=pltpu.CompilerParams(vmem_limit_bytes=20 << 20),
        cost_estimate=cost(1),
        name="attention_out_back",
    )(gk, mixed, w_attn, perm)


def attn_bwd_kernel(gmix_ref, mixed_ref, qkv_ref, lse_ref, msg_ref, wqkv_ref, vec_ref,
                    dqkv_ref, sums_ref, gmsg_ref,
                    kt_ref, dqt_ref, rows_ref):
    def frame(f, _):
        rows = pl.ds(pl.multiple_of(f * SPAN, SPAN), SPAN)
        kt_ref[...] = qkv_ref[rows, D : 2 * D].T
        dots = head_sums(gmix_ref[rows, :], mixed_ref[rows, :])
        for p in range(PAIRS):
            cols = lambda part: slice(part * D + p * 128, part * D + (p + 1) * 128)
            q, k, v = (qkv_ref[rows, cols(i)] for i in range(3))
            go = gmix_ref[rows, cols(0)]
            lse = [lse_ref[f, 2 * p + h : 2 * p + h + 1, :] for h in range(2)]
            dot = [dots[2 * p + h : 2 * p + h + 1, :] for h in range(2)]
            dqt, dk, dv = attend_bwd(q, k, v, kt_ref[cols(0), :], go, lse, dot, frame_mask)
            dqt_ref[cols(0), :] = dqt
            dqkv_ref[rows, cols(1)] = dk
            dqkv_ref[rows, cols(2)] = dv
        dqkv_ref[rows, :D] = dqt_ref[...].T
        return 0

    lax.fori_loop(0, FRAMES, frame, 0)
    dqb = jnp.zeros((1, D), WIDE)
    dvb = jnp.zeros((1, D), WIDE)
    for f in range(FRAMES):
        rows = pl.ds(f * SPAN, SPAN)
        dqb += jnp.sum(wide_of(dqkv_ref[rows, :D]), 0, keepdims=True)
        dvb += jnp.sum(wide_of(dqkv_ref[rows, 2 * D :]), 0, keepdims=True)
        tile = wide_of(dqkv_ref[f * SPAN + 192 : f * SPAN + 208, :])
        rows_ref[f : f + 1, :] = tile[TOK - 192 : TOK - 191, :]
    rows_ref[FRAMES:, :] = jnp.zeros((8 - FRAMES, 3 * D), WIDE)
    sums_ref[...] = jnp.concatenate([dqb, dvb, jnp.zeros((6, D), WIDE)], 0)
    back = mm_t(narrow(rows_ref[...]), wqkv_ref[...])
    normed, inverse = normed_of(msg_ref[...])
    gmsg_ref[...] = norm_back(back[:FRAMES], normed, inverse, vec(vec_ref, GAIN1))


def attn_bwd(gmix, mixed, qkv, lse, msg, w_attn, vectors):
    return pl.pallas_call(
        attn_bwd_kernel,
        grid=(1,),
        in_specs=[whole(gmix.shape), whole(mixed.shape), whole(qkv.shape), whole(lse.shape), whole(msg.shape),
                  qkv_out_specs()[0], whole(vectors.shape)],
        out_specs=(whole((ROWS, 3 * D)), whole((8, D)), whole((FRAMES, D))),
        out_shape=(shaped(ROWS, 3 * D), shaped(8, D, dtype=WIDE), shaped(FRAMES, D, dtype=WIDE)),
        scratch_shapes=[pltpu.VMEM((D, SPAN), LOW), pltpu.VMEM((D, SPAN), LOW), pltpu.VMEM((8, 3 * D), WIDE)],
        compiler_params=pltpu.CompilerParams(vmem_limit_bytes=56 << 20),
        cost_estimate=cost(1),
        name="frame_attention_back",
    )(gmix, mixed, qkv, lse, msg, w_attn, vectors)


def tokens_back_kernel(dqkv_ref, wqkv_ref, gk_ref, tok_ref, msg_ref, vec_ref, blk_ref, perm_ref, dout_ref,
                       sum_out_ref, sums_mlp_ref, placed_ref, out_ref, keep_ref, give_ref, joined_ref):
    turned = narrow(mm_t(perm_ref[...], blk_ref[...]))
    for n in range(3):
        cols = slice(n * D, (n + 1) * D)
        dw = narrow(mm(turned, dqkv_ref[:, cols]))
        keep_ref[:, cols] = dw[: D // 2]
        give_ref[:, cols] = dw[D // 2 :]
    keep_ref[:, 3 * D : FF] = dout_ref[: D // 2]
    give_ref[:, 3 * D : FF] = dout_ref[D // 2 :]
    fill_joined(tok_ref, msg_ref, joined_ref)
    dg = jnp.zeros((1, D), WIDE)
    dsh = jnp.zeros((1, D), WIDE)
    back_all = mm_t(dqkv_ref[...], wqkv_ref[...])
    for f in range(FRAMES):
        rows = pl.ds(f * SPAN, SPAN)
        back = back_all[f * SPAN : (f + 1) * SPAN]
        normed, inverse = normed_of(joined_ref[rows, :])
        dg += jnp.sum(back * normed, 0, keepdims=True)
        dsh += jnp.sum(back, 0, keepdims=True)
        full = gk_ref[rows, :] + norm_back(back, normed, inverse, vec(vec_ref, GAIN1))
        out_ref[f] = full[:TOK]
    sums = jnp.concatenate(
        [dg, dsh, sum_out_ref[:1, :], sums_mlp_ref[:3, :], placed_ref[...], jnp.zeros((116, D), WIDE)], 0
    )
    turned = narrow(mm_t(perm_ref[...], narrow(sums)))
    keep_ref[:, FF:] = turned[: D // 2]
    give_ref[:, FF:] = turned[D // 2 :]


def tokens_back(dqkv, w_attn, gk, tok, msg, vectors, blk, perm, dout, sum_out, sums_mlp, placed):
    return pl.pallas_call(
        tokens_back_kernel,
        grid=(1,),
        in_specs=[whole(dqkv.shape), qkv_out_specs()[0], whole(gk.shape), whole(tok.shape), whole(msg.shape),
                  whole(vectors.shape), whole(blk.shape), whole(perm.shape), whole(dout.shape),
                  whole(sum_out.shape), whole(sums_mlp.shape), whole(placed.shape)],
        out_specs=(whole((FRAMES, TOK, D)), whole((D // 2, FF + 128)), whole((D // 2, FF + 128))),
        out_shape=(shaped(FRAMES, TOK, D, dtype=WIDE), shaped(D // 2, FF + 128), shaped(D // 2, FF + 128)),
        scratch_shapes=[pltpu.VMEM((ROWS, D), WIDE)],
        compiler_params=pltpu.CompilerParams(vmem_limit_bytes=42 << 20),
        cost_estimate=cost(1),
        name="tokens_back",
    )(dqkv, w_attn, gk, tok, msg, vectors, blk, perm, dout, sum_out, sums_mlp, placed)


ALL = 256


def group_mask(grow_ref, gcol_ref):
    same = gcol_ref[:, 0:1] == grow_ref[0:1, :]

    def mask(s):
        return jnp.where(same, s, -1000000000.0)

    return mask


def msg_fwd_kernel(cls_ref, w_ref, vec_ref, grow_ref, gcol_ref,
                   message_ref, token_ref, min_ref, qkv_ref, mixed_ref, lse_ref, vt_ref, ot_ref):
    message = mm(cls_ref[...], w_ref[:, :D]) + vec(vec_ref, FC_B)
    message_ref[...] = message
    normed, _ = normed_of(message)
    min_ref[...] = narrow(normed * vec(vec_ref, MSG_GAIN) + vec(vec_ref, MSG_SHIFT))
    for n in range(9):
        y = mm(min_ref[...], w_ref[:, D + n * 256 : D + (n + 1) * 256])
        if n < 3:
            y = y + vec_ref[MQ_B : MQ_B + 1, n * 256 : (n + 1) * 256]
        if n >= 6:
            y = y + vec_ref[MV_B : MV_B + 1, (n - 6) * 256 : (n - 5) * 256]
        qkv_ref[:, n * 256 : (n + 1) * 256] = narrow(y)
    vt_ref[...] = qkv_ref[:, 2 * D :].T
    mask = group_mask(grow_ref, gcol_ref)
    lse_ref[...] = jnp.zeros_like(lse_ref)
    for p in range(PAIRS):
        q = qkv_ref[:, p * 128 : (p + 1) * 128]
        k = qkv_ref[:, D + p * 128 : D + (p + 1) * 128]
        vt = vt_ref[p * 128 : (p + 1) * 128, :]
        for h, (o, l) in enumerate(attend_fwd(q, k, vt, None, mask)):
            at = p * 128 + h * HEAD_DIM
            ot_ref[at : at + HEAD_DIM, :] = narrow(o)
            lse_ref[2 * p + h : 2 * p + h + 1, :] = l
    mixed_ref[...] = ot_ref[...].T
    token_ref[...] = message + mm(mixed_ref[...], w_ref[:, 4 * D :]) + vec(vec_ref, MOUT_B)


def msg_fwd(cls, w, vectors, grow, gcol):
    return pl.pallas_call(
        msg_fwd_kernel,
        out_shape=(shaped(ALL, D, dtype=WIDE), shaped(ALL, D, dtype=WIDE), shaped(ALL, D), shaped(ALL, 3 * D),
                   shaped(ALL, D), shaped(16, ALL, dtype=WIDE)),
        scratch_shapes=[pltpu.VMEM((D, ALL), LOW), pltpu.VMEM((D, ALL), LOW)],
        compiler_params=pltpu.CompilerParams(vmem_limit_bytes=20 << 20),
        cost_estimate=cost(1),
        name="message_forward",
    )(cls, w, vectors, grow, gcol)


def msg_bwd_kernel(gm_ref, cls_ref, message_ref, min_ref, qkv_ref, mixed_ref, lse_ref, w_ref, vec_ref,
                   grow_ref, gcol_ref, pick_ref,
                   gcls_ref, dw_ref, sums_ref,
                   gmix_ref, kt_ref, dqt_ref, dqkv_ref):
    gb = gm_ref[...]
    pick = pick_ref[...]
    turned = lambda x: narrow(mm_t(pick, x))
    gmix_ref[...] = narrow(mm_t(gb, w_ref[:, 4 * D :]))
    dw_ref[:, 4 * D :] = mm(turned(mixed_ref[...]), gb)
    kt_ref[...] = qkv_ref[:, D : 2 * D].T
    mask = group_mask(grow_ref, gcol_ref)
    dots = head_sums(gmix_ref[...], mixed_ref[...])
    for p in range(PAIRS):
        cols = lambda part: slice(part * D + p * 128, part * D + (p + 1) * 128)
        q, k, v = (qkv_ref[:, cols(i)] for i in range(3))
        go = gmix_ref[:, cols(0)]
        lse = [lse_ref[2 * p + h : 2 * p + h + 1, :] for h in range(2)]
        dot = [dots[2 * p + h : 2 * p + h + 1, :] for h in range(2)]
        dqt, dk, dv = attend_bwd(q, k, v, kt_ref[cols(0), :], go, lse, dot, mask)
        dqt_ref[cols(0), :] = dqt
        dqkv_ref[:, cols(1)] = dk
        dqkv_ref[:, cols(2)] = dv
    dqkv_ref[:, :D] = dqt_ref[...].T
    dqkv = dqkv_ref[...]
    dw_ref[:, D : 4 * D] = mm(turned(min_ref[...]), dqkv)
    back = mm_t(dqkv, w_ref[:, D : 4 * D])
    normed, inverse = normed_of(message_ref[...])
    gfc = narrow(wide_of(gb) + norm_back(back, normed, inverse, vec(vec_ref, MSG_GAIN)))
    dw_ref[:, :D] = mm(turned(cls_ref[...]), gfc)
    gcls_ref[...] = mm_t(gfc, w_ref[:, :D])
    col = lambda x: jnp.sum(wide_of(x), 0, keepdims=True)
    sums_ref[...] = jnp.concatenate(
        [col(gfc), col(back * normed), col(back), col(gb), col(dqkv[:, :D]), col(dqkv[:, 2 * D :]),
         jnp.zeros((2, D), WIDE)], 0)


def msg_bwd(gm, cls, message, mins, qkv, mixed, lse, w, vectors, grow, gcol, pick):
    return pl.pallas_call(
        msg_bwd_kernel,
        out_shape=(shaped(ALL, D, dtype=WIDE), shaped(16, 5 * D, dtype=WIDE), shaped(8, D, dtype=WIDE)),
        scratch_shapes=[pltpu.VMEM((ALL, D), LOW), pltpu.VMEM((D, ALL), LOW), pltpu.VMEM((D, ALL), LOW),
                        pltpu.VMEM((ALL, 3 * D), LOW)],
        compiler_params=pltpu.CompilerParams(vmem_limit_bytes=48 << 20),
        cost_estimate=cost(1),
        name="message_back",
    )(gm, cls, message, mins, qkv, mixed, lse, w, vectors, grow, gcol, pick)


def frame_of(x_hi, y, z, core):
    return ((x_hi * 4 + y) * 4 + z) * 2 + core


PLACES = list(itertools.product(range(2), range(4), range(4), range(2), range(2)))


def moves(to):
    return [(frame_of(*p[:4]) * 2 + p[4], frame_of(*to(*p)[:4]) * 2 + to(*p)[4]) for p in PLACES]


TO_CORE = moves(lambda x, y, z, c, v: (x, y, z, 1 - c, v))
TO_VIDEO = moves(lambda x, y, z, c, v: (x, y, z, c, 1 - v))
TO_HALF = moves(lambda x, y, z, c, v: (1 - x, y, z, c, v))
TO_BOTH = moves(lambda x, y, z, c, v: (1 - x, y, z, c, 1 - v))
TO_Y = [moves(lambda x, y, z, c, v, k=k: (x, (y + k) % 4, z, c, v)) for k in range(4)]
TO_Z = [moves(lambda x, y, z, c, v, k=k: (x, y, (z + k) % 4, c, v)) for k in range(4)]
ALONG_Y = [[frame_of(x, y, z, c) for y in range(4)] for x in range(2) for z in range(4) for c in range(2)]
ALONG_Z = [[frame_of(x, y, z, c) for z in range(4)] for x in range(2) for y in range(4) for c in range(2)]
PLANE = [[frame_of(x, y, z, c) for y in range(4) for z in range(4)] for x in range(2) for c in range(2)]
def sent(x, pairs):
    return lax.ppermute(x, ("frame", "video"), pairs)


def to_everyone(x):
    return lax.all_to_all(jnp.broadcast_to(x[None], (64, *x.shape)), "frame", 0, 0, tiled=True)


def assemble_y_kernel(place_ref, *refs):
    pieces, out_ref, sems = refs[:8], refs[8], refs[9]
    x, y, _, core = place_parts(place_ref[0])
    span, half = 96, 1536
    copies = []
    for who in range(2):
        col = pl.multiple_of((core if who == 0 else 1 - core) * half, 128)
        for k in range(4):
            for h in range(2):
                row = pl.multiple_of(((x if h == 0 else 1 - x) * 4 + lax.rem(y + 4 - k, 4)) * span, span)
                copies.append(
                    pltpu.make_async_copy(
                        pieces[who * 4 + k].at[h],
                        out_ref.at[pl.ds(row, span), pl.ds(col, half)],
                        sems.at[len(copies)],
                    )
                )
                copies[-1].start()
    for done in copies:
        done.wait()


def assemble_z_kernel(place_ref, *refs):
    pieces, out_ref, held_ref, sems = refs[:-3], refs[-3], refs[-2], refs[-1]
    x, y, z, core = place_parts(place_ref[0])
    each = len(pieces) // 2
    half = pieces[0].shape[-1]
    copies = []
    for n, piece_ref in enumerate(pieces):
        col = pl.multiple_of((core if n < each else 1 - core) * half, 128)
        copies.append(pltpu.make_async_copy(piece_ref, held_ref.at[n % 4, :, pl.ds(col, half)], sems.at[n]))
        copies[-1].start()
    for done in copies:
        done.wait()
    for cols in range(0, 2 * half, D):
        for k in range(4):
            slabs = [
                wide_of(held_ref[lax.rem(z + 4 - to, 4), 48 * k : 48 * k + 48, cols : cols + D])
                for to in range(4)
            ]
            for h in range(2):
                row = pl.multiple_of(((x if h == 0 else 1 - x) * 4 + lax.rem(y + 4 - k, 4)) * 96, 96)
                out_ref[pl.ds(row, 96), cols : cols + D] = narrow(
                    jnp.concatenate([v[24 * h : 24 * h + 24] for v in slabs], 0)
                )


def assembled(kernel, place, pieces, out, scratch):
    anywhere = pl.BlockSpec(memory_space=pltpu.HBM)
    return pl.pallas_call(
        kernel,
        in_specs=[pl.BlockSpec(memory_space=pltpu.SMEM)] + [anywhere] * len(pieces),
        out_shape=out,
        scratch_shapes=scratch,
        compiler_params=pltpu.CompilerParams(vmem_limit_bytes=24 << 20),
        cost_estimate=cost(1),
        name="assemble_weights",
    )(place.reshape(1), *pieces)


def assemble_y(place, pieces):
    return assembled(assemble_y_kernel, place, pieces, shaped(D, FF), [pltpu.SemaphoreType.DMA((16,))])


def assemble_z(place, pieces):
    half = pieces[0].shape[-1]
    scratch = [pltpu.VMEM((4, 192, 2 * half), LOW), pltpu.SemaphoreType.DMA((len(pieces),))]
    return assembled(assemble_z_kernel, place, pieces, shaped(D, 2 * half), scratch)


def pack_kernel(place_ref, qkv_ref, out_ref, fc_ref, mqkv_ref, mout_ref, up_ref, down_ref, mine_ref, give_ref,
                down_mine_ref, down_give_ref):
    def put(which, to_ref, down_to_ref):
        parts = (
            (qkv_ref[:, :1536], fc_ref[...], mqkv_ref[:, :1152], up_ref[:, :1536]),
            (qkv_ref[:, 1536:], out_ref[...], mqkv_ref[:, 1152:], mout_ref[...], up_ref[:, 1536:]),
        )[which]
        to_ref[...] = jnp.concatenate(parts, 1)
        down_to_ref[...] = down_ref[:, which * 384 : which * 384 + 384]

    for core in range(2):

        @pl.when(lax.rem(place_ref[0], 2) == core)
        def _():
            put(core, mine_ref, down_mine_ref)
            put(1 - core, give_ref, down_give_ref)


def packed(place, *shards):
    mine, give, down_mine, down_give = pl.pallas_call(
        pack_kernel,
        in_specs=[pl.BlockSpec(memory_space=pltpu.SMEM)] + [pl.BlockSpec(memory_space=pltpu.VMEM)] * 7,
        out_shape=(shaped(12, 4992), shaped(12, 4992), shaped(48, 384), shaped(48, 384)),
        cost_estimate=cost(1),
        name="pack_weights",
    )(place.reshape(1), *shards)
    return (mine, give), (down_mine, down_give)


def core_pair(place, halves):
    mine, got = halves[0], sent(halves[1], TO_CORE)
    return jnp.where(place % 2 == 0, jnp.concatenate([mine, got], 0), jnp.concatenate([got, mine], 0))


def both_x(pair):
    return jnp.stack([pair, sent(pair, TO_HALF)])


def ring_z(pair):
    return jnp.swapaxes(from_z(jnp.broadcast_to(pair[None], (4, *pair.shape))), 0, 1).reshape(2, -1, pair.shape[2])


def ring_y(pair):
    return jnp.stack([pair, *(sent(pair, TO_Y[k]) for k in range(1, 4))]).reshape(192, -1)


def around(x, moves_by):
    return [x, *(sent(x, moves_by[k]) for k in range(1, 4))]


def from_z(copies):
    return lax.all_to_all(copies, "frame", 0, 0, axis_index_groups=ALONG_Z, tiled=True)


def both_cores(pieces):
    return [*pieces, *(sent(x, TO_CORE) for x in pieces)]


def after(x, *others):
    return lax.optimization_barrier((x, *others))


def row_order(place):
    row = jnp.arange(D, dtype=jnp.int32)
    r, x, z, y, c = row % 12, row // 12 % 2, row // 24 % 4, row // 96 % 4, row // 384
    natural = ((((x * 4 + y) * 4 + z) * 2) + jnp.where(c == 0, place % 2, 1 - place % 2)) * 12 + r
    return (natural[:, None] == row[None, :]).astype(LOW)


def add_pack_kernel(keep_up, got_up, keep_down, got_down, out_ref):
    up = wide_of(keep_up[...]) + wide_of(got_up[...])
    down = wide_of(keep_down[0]) + wide_of(got_down[0])
    for i in range(2):
        out_ref[i, :, :FF] = narrow(up[24 * i : 24 * i + 24])
        slab = jnp.concatenate([down[i, 0], down[i, 1]], 0)
        for q in range(4):
            both = [slab[48 * h + 12 * q : 48 * h + 12 * q + 12] for h in range(2)]
            out_ref[i, :, FF + q * D : FF + (q + 1) * D] = narrow(jnp.concatenate(both, 0))


def add_pack(keep_up, got_up, keep_down, got_down):
    down_spec = pl.BlockSpec((1, 2, 2, 48, D), lambda i: (i // 2, i % 2, 0, 0, 0))
    up_spec = pl.BlockSpec((48, FF), lambda i: (i, 0))
    return pl.pallas_call(
        add_pack_kernel,
        grid=(8,),
        in_specs=[up_spec, up_spec, down_spec, down_spec],
        out_specs=pl.BlockSpec((2, 24, 2 * FF), lambda i: (i, 0, 0)),
        out_shape=shaped(16, 24, 2 * FF),
        compiler_params=pltpu.CompilerParams(vmem_limit_bytes=14 << 20),
        cost_estimate=cost(1),
        name="add_mlp_gradients",
    )(keep_up, got_up, keep_down, got_down)


def ring_sum(parts, groups):
    return lax.psum_scatter(parts, "frame", scatter_dimension=0, axis_index_groups=groups, tiled=True)


def plane_sum(parts):
    got = lax.all_to_all(parts, "frame", 0, 0, axis_index_groups=PLANE, tiled=True)
    return narrow(jnp.sum(wide_of(got), 0))


def last_kernel(mine_ref, video_ref, half_ref, both_ref, *out_refs):
    total = wide_of(mine_ref[...]) + wide_of(video_ref[...]) + wide_of(half_ref[...]) + wide_of(both_ref[...])
    at = 0
    for out_ref in out_refs:
        out_ref[...] = total[:, at : at + out_ref.shape[1]]
        at += out_ref.shape[1]


def last_sums(rows, half, widths):
    mine, other = (lax.dynamic_slice_in_dim(rows, which * 12, 12, 0) for which in (half, 1 - half))
    return pl.pallas_call(
        last_kernel,
        out_shape=tuple(shaped(12, w, dtype=WIDE) for w in widths),
        cost_estimate=cost(1),
        name="last_sums",
    )(mine, sent(mine, TO_VIDEO), sent(other, TO_HALF), sent(other, TO_BOTH))


def shards(
    tokens_in,
    clip_ids,
    grad_out,
    msg_fc_w,
    msg_fc_b,
    msg_norm_gain,
    msg_norm_shift,
    msg_qkv_w,
    msg_qv_b,
    msg_out_w,
    msg_out_b,
    norm1_gain,
    norm1_shift,
    attn_qkv_w,
    attn_qv_b,
    attn_out_w,
    attn_out_b,
    norm2_gain,
    norm2_shift,
    mlp_in_w,
    mlp_in_b,
    mlp_out_w,
    mlp_out_b,
):
    place = lax.axis_index("frame").astype(jnp.int32)
    core, half = place % 2, place // 32
    tok = tokens_in[0]
    small = jnp.concatenate(
        [
            tok[:, 0, :].reshape(-1),
            msg_fc_b,
            msg_norm_gain,
            msg_norm_shift,
            msg_out_b,
            norm1_gain,
            norm1_shift,
            attn_out_b,
            norm2_gain,
            norm2_shift,
            mlp_out_b,
            msg_qv_b,
            attn_qv_b,
            mlp_in_b,
            clip_ids[0].astype(LOW),
        ]
    )
    small = jnp.pad(small, (0, 4096 - small.shape[0])).reshape(32, 128)
    w_halves, down_halves = packed(
        place, attn_qkv_w, attn_out_w, msg_fc_w, msg_qkv_w, msg_out_w, mlp_in_w, mlp_out_w
    )
    w_pair = core_pair(place, w_halves)
    down_pair = core_pair(place, down_halves).reshape(4, 24, 384).transpose(1, 0, 2).reshape(24, 1536)
    w_x = both_x(jnp.concatenate([w_pair[:, :1536], down_pair, w_pair[:, 1536:]], 1))
    by_y, by_z = ring_z(w_x[:, :, :3072]), ring_y(w_x[:, :, 3072:])
    by_y, by_z, small = after(by_y, by_z, small)
    small_all = to_everyone(small)
    attn = by_y[:, :, :1536]
    attn_last, late_z = after(attn, jnp.broadcast_to(by_z[None, :, 1920:], (4, 192, 1536)))
    msg_all = around(by_z[:, :1920], TO_Z)
    attn_all = [attn, sent(attn_last, TO_Y[1]), sent(attn, TO_Y[2]), sent(attn, TO_Y[3])]
    msg_all, attn_all, small_all, late_y, late_z, grads = after(
        msg_all, attn_all, small_all, by_y[:, :, 1536:], late_z, framed(grad_out[0])
    )
    up_all, down_all = [from_z(late_z)], around(late_y, TO_Y)
    small_all = small_all.reshape(64, 4096)
    cls = small_all[:, :3072].reshape(ALL, D)
    at = 3072
    vectors = small_all[:, at : at + 120].reshape(64, 10, 12).transpose(1, 0, 2).reshape(10, D)
    biases = [small_all[:, at + 120 + a : at + 120 + b].reshape(-1, D) for a, b in ((0, 24), (24, 48), (48, 96))]
    vectors = wide_of(jnp.concatenate([vectors, *biases, jnp.zeros((VECTOR_ROWS - 18, D), LOW)], 0))
    at = at + 216
    groups = wide_of(small_all[:, at : at + 4].reshape(ALL))
    grow = jnp.broadcast_to(groups[None], (8, ALL))
    gcol = jnp.broadcast_to(groups[:, None], (ALL, 128))
    order = row_order(place)
    pick_row = jnp.arange(16, dtype=jnp.int32)[:, None]
    pick_col = jnp.arange(D, dtype=jnp.int32)[None, :]
    pick = ((pick_row < 12) & (pick_col == place * 12 + pick_row)).astype(LOW)

    msg_all, vectors, order, pick, cls, grow, gcol = after(msg_all, vectors, order, pick, cls, grow, gcol)
    w_msg = assemble_z(place, both_cores(msg_all))
    message, token, mins, mqkv, mmixed, mlse = msg_fwd(cls, w_msg, vectors, grow, gcol)
    token, attn_all = after(token, attn_all)
    w_attn = assemble_y(place, both_cores(attn_all))
    msg = lax.dynamic_slice_in_dim(token, place * FRAMES, FRAMES)
    qkv, mixed, kept, lse, blk = attn_fwd(tok, msg, w_attn, vectors)
    kept, up_all, down_all = after(kept, up_all, down_all)
    lay, gk, dup_keep, dup_give, down_keep, down_give, sums_mlp, dub = mlp(
        place, kept, grads, both_cores(up_all), both_cores(down_all), vectors, order
    )
    dup_got, down_got = sent(dup_give, TO_CORE), sent(down_give, TO_CORE)
    gmix, dout, sum_out = out_back(gk, mixed, w_attn, order)
    gmix, dup_got, down_got = after(gmix, dup_got, down_got)
    mlp_parts, gmix = after(add_pack(dup_keep, dup_got, down_keep, down_got), gmix)
    mlp_half = ring_sum(mlp_parts, ALONG_Y)
    dqkv, sums_attn, gmsg = attn_bwd(gmix, mixed, qkv, lse, msg, w_attn, vectors)
    gmsg = jnp.broadcast_to(narrow(gmsg)[None], (64, FRAMES, D))
    gmsg, dqkv = after(gmsg, dqkv)
    gmsg_all = lax.all_to_all(gmsg, "frame", 0, 0, tiled=True).reshape(ALL, D)
    by_place = lambda x, n: x.reshape(64, n, 12).transpose(1, 0, 2).reshape(n, D)
    placed = jnp.concatenate([by_place(sums_attn[:2], 2), by_place(dub[:, 0], 4)], 0)
    grad_tokens, attn_keep, attn_give = tokens_back(dqkv, w_attn, gk, tok, msg, vectors, blk, order, dout, sum_out, sums_mlp, placed)
    attn_keep, attn_give, gmsg_all, mlp_half = after(attn_keep, attn_give, gmsg_all, mlp_half)
    mlp_sum = ring_sum(mlp_half, ALONG_Z).reshape(24, 2 * FF)
    attn_got = sent(attn_give, TO_CORE)
    gcls, dw_msg, sums_msg = msg_bwd(gmsg_all, cls, message, mins, mqkv, mmixed, mlse, w_msg, vectors, grow, gcol, pick)
    attn_got, gcls, dw_msg, sums_msg = after(attn_got, gcls, dw_msg, sums_msg)
    attn_part = narrow(wide_of(attn_keep) + wide_of(attn_got))
    attn_part, lay = after(attn_part, lay)
    attn_part, gcls, dw_msg, sums_msg = after(attn_part, gcls, dw_msg, sums_msg)
    attn_sum = plane_sum(attn_part.reshape(16, 24, FF + 128))
    gcls = lax.dynamic_slice_in_dim(gcls, place * FRAMES, FRAMES)
    grad_tokens = grad_tokens.at[:, 0, :].add(gcls)
    own = lax.dynamic_slice_in_dim(sums_msg[:4], place * 12, 12, 1).reshape(-1)
    own_qv = lax.dynamic_slice_in_dim(sums_msg[4:6].reshape(-1), place * 24, 24)
    own = jnp.concatenate([own, own_qv])
    own = own + sent(own, TO_VIDEO)
    fb, mg, ms, mob, mqvb = jnp.split(own, [12, 24, 36, 48])
    msg_rows = dw_msg[:12]
    msg_rows = msg_rows + wide_of(sent(narrow(msg_rows), TO_VIDEO))
    mlp_sum, msg_rows = after(mlp_sum, msg_rows)
    mlp_rows, *down_rows = last_sums(mlp_sum, half, (FF, D, D, D, D))
    down_rows = jnp.concatenate(down_rows, 0)
    attn_sum, mlp_rows, down_rows = after(attn_sum, mlp_rows, down_rows)
    qkv_rows, out_rows, ends = last_sums(attn_sum, half, (3 * D, D, 128))
    ends = ends[:, :12].T
    g1, s1, ob, g2, s2, db = (ends[k] for k in range(6))
    qvb, ub = ends[6:8].reshape(-1), ends[8:12].reshape(-1)
    return (
        lay[None],
        grad_tokens[None],
        msg_rows[:, :D],
        fb,
        mg,
        ms,
        msg_rows[:, D : 4 * D],
        mqvb,
        msg_rows[:, 4 * D :],
        mob,
        g1,
        s1,
        qkv_rows,
        qvb,
        out_rows,
        ob,
        g2,
        s2,
        mlp_rows,
        ub,
        down_rows,
        db,
    )


def solution(mesh):
    in_specs = (
        P("video", "frame", None, None),
        P("video", "frame"),
        P("video", "frame", None, None),
        P("frame", None),
        P("frame"),
        P("frame"),
        P("frame"),
        P("frame", None),
        P("frame"),
        P("frame", None),
        P("frame"),
        P("frame"),
        P("frame"),
        P("frame", None),
        P("frame"),
        P("frame", None),
        P("frame"),
        P("frame"),
        P("frame"),
        P("frame", None),
        P("frame"),
        P("frame", None),
        P("frame"),
    )
    out_specs = (
        P("video", "frame", None, None),
        P("video", "frame", None, None),
        P("frame", None),
        P("frame"),
        P("frame"),
        P("frame"),
        P("frame", None),
        P("frame"),
        P("frame", None),
        P("frame"),
        P("frame"),
        P("frame"),
        P("frame", None),
        P("frame"),
        P("frame", None),
        P("frame"),
        P("frame"),
        P("frame"),
        P("frame", None),
        P("frame"),
        P("frame", None),
        P("frame"),
    )
    return jax.shard_map(shards, mesh=mesh, in_specs=in_specs, out_specs=out_specs, check_vma=False)
```

```python
import functools
import itertools
import jax
import jax.numpy as jnp
from jax import lax
from jax.experimental import pallas as pl
from jax.experimental.pallas import tpu as pltpu
from jax.sharding import PartitionSpec as P

HEAD_DIM = 64
FRAMES = 4
TOK = 197
SPAN = 208
ROWS = FRAMES * SPAN
D = 768
FF = 3072
HEADS = 12
PAIRS = 6
WIDE = jnp.float32
LOW = jnp.bfloat16
SCALE = HEAD_DIM ** (-0.5)
FC_B, MSG_GAIN, MSG_SHIFT, MOUT_B, GAIN1, SHIFT1, OUT_B, GAIN2, SHIFT2, DOWN_B, MQ_B, MV_B, Q_B, V_B, UP_B = range(15)
VECTOR_ROWS = 24


def narrow(x):
    return x.astype(LOW)


def wide_of(x):
    return x.astype(WIDE)


def mm(a, b):
    return lax.dot_general(a, b, (((1,), (0,)), ((), ())), preferred_element_type=WIDE)


def mm_t(a, b):
    return lax.dot_general(a, b, (((1,), (1,)), ((), ())), preferred_element_type=WIDE)


def normed_of(x):
    center = x - jnp.mean(x, -1, keepdims=True)
    inverse = lax.rsqrt(jnp.mean(center * center, -1, keepdims=True) + 1e-05)
    return center * inverse, inverse


def norm_back(grad, normed, inverse, gain):
    scaled = grad * gain
    return inverse * (
        scaled
        - jnp.mean(scaled, -1, keepdims=True)
        - normed * jnp.mean(scaled * normed, -1, keepdims=True)
    )


def own_lanes(x, which):
    lane = lax.broadcasted_iota(jnp.int32, x.shape, 1)
    return jnp.where((lane < HEAD_DIM) == (which == 0), x, jnp.zeros_like(x))


def either(a, b):
    lane = lax.broadcasted_iota(jnp.int32, a.shape, 1)
    return jnp.where(lane < HEAD_DIM, a, b)


def vec(vec_ref, row):
    return vec_ref[row : row + 1, :]


def fill_joined(tok_ref, msg_ref, joined_ref):
    for f in range(FRAMES):
        joined_ref[f * SPAN : f * SPAN + TOK, :] = wide_of(tok_ref[f])
        joined_ref[f * SPAN + TOK : f * SPAN + TOK + 1, :] = msg_ref[f : f + 1, :]
        joined_ref[f * SPAN + TOK + 1 : (f + 1) * SPAN, :] = jnp.zeros((SPAN - TOK - 1, D), WIDE)


def attend_fwd(q, k, vt, valid, mask):
    out = []
    for h in range(2):
        s = mm_t(own_lanes(k, h), q) * SCALE
        s = mask(s)
        peak = jnp.max(s, 0, keepdims=True)
        e = jnp.exp(s - peak)
        total = jnp.sum(e, 0, keepdims=True)
        o = mm(vt[h * HEAD_DIM : (h + 1) * HEAD_DIM], narrow(e)) / total
        out.append((o, peak + jnp.log(total)))
    return out


def attend_bwd(q, k, v, kt, go, lse, dot, mask):
    dqt, dk, dv = [], [], []
    for h in range(2):
        s = mask(mm_t(own_lanes(k, h), q) * SCALE)
        p = jnp.exp(s - lse[h])
        dp = mm_t(own_lanes(v, h), go)
        ds = narrow(p * (dp - dot[h]))
        dv.append(mm(narrow(p), go))
        dk.append(mm(ds, q))
        dqt.append(mm(kt[h * HEAD_DIM : (h + 1) * HEAD_DIM], ds))
    return (
        narrow(jnp.concatenate(dqt, 0) * SCALE),
        narrow(either(*dk) * SCALE),
        narrow(either(*dv)),
    )


def frame_mask(s):
    key = lax.broadcasted_iota(jnp.int32, s.shape, 0)
    return jnp.where(key <= TOK, s, -1e30)


def attn_fwd_kernel(tok_ref, msg_ref, wqkv_ref, wout_ref, vec_ref,
                    qkv_ref, mixed_ref, kept_ref, lse_ref, blk_ref, vt_ref, ot_ref):
    fill_joined(tok_ref, msg_ref, kept_ref)
    for f in range(FRAMES):
        rows = pl.ds(f * SPAN, SPAN)
        normed, _ = normed_of(kept_ref[rows, :])
        blk_ref[rows, :] = narrow(normed * vec(vec_ref, GAIN1) + vec(vec_ref, SHIFT1))
    for n in range(9):
        cols = pl.ds(n * 256, 256)
        y = mm(blk_ref[...], wqkv_ref[:, cols])
        if n < 3:
            y = y + vec_ref[Q_B : Q_B + 1, n * 256 : (n + 1) * 256]
        if n >= 6:
            y = y + vec_ref[V_B : V_B + 1, (n - 6) * 256 : (n - 5) * 256]
        qkv_ref[:, cols] = narrow(y)
    lse_ref[...] = jnp.zeros_like(lse_ref)

    def frame(f, _):
        rows = pl.ds(pl.multiple_of(f * SPAN, SPAN), SPAN)
        vt_ref[...] = qkv_ref[rows, 2 * D :].T
        for p in range(PAIRS):
            q = qkv_ref[rows, p * 128 : (p + 1) * 128]
            k = qkv_ref[rows, D + p * 128 : D + (p + 1) * 128]
            vt = vt_ref[p * 128 : (p + 1) * 128, :]
            for h, (o, l) in enumerate(attend_fwd(q, k, vt, None, frame_mask)):
                at = p * 128 + h * HEAD_DIM
                ot_ref[at : at + HEAD_DIM, :] = narrow(o)
                lse_ref[f, 2 * p + h : 2 * p + h + 1, :] = l
        mixed_ref[rows, :] = ot_ref[...].T
        return 0

    lax.fori_loop(0, FRAMES, frame, 0)
    kept_ref[...] = kept_ref[...] + mm(mixed_ref[...], wout_ref[...]) + vec(vec_ref, OUT_B)


def cost(us):
    return pl.CostEstimate(flops=int(us * 1e6), bytes_accessed=int(us * 1e3), transcendentals=0)


def qkv_out_specs():
    return [pl.BlockSpec((D, 3 * D), lambda *_: (0, 0)), pl.BlockSpec((D, D), lambda *_: (0, 3))]


def whole(shape):
    return pl.BlockSpec(shape, lambda *_: (0,) * len(shape))


def shaped(*shape, dtype=LOW):
    return jax.ShapeDtypeStruct(shape, dtype)


def attn_fwd(tok, msg, w_attn, vectors):
    return pl.pallas_call(
        attn_fwd_kernel,
        grid=(1,),
        in_specs=[whole(tok.shape), whole(msg.shape), *qkv_out_specs(), whole(vectors.shape)],
        out_specs=(whole((ROWS, 3 * D)), whole((ROWS, D)), whole((ROWS, D)), whole((FRAMES, 16, SPAN)), whole((ROWS, D))),
        out_shape=(shaped(ROWS, 3 * D), shaped(ROWS, D), shaped(ROWS, D, dtype=WIDE),
                   shaped(FRAMES, 16, SPAN, dtype=WIDE), shaped(ROWS, D)),
        scratch_shapes=[pltpu.VMEM((D, SPAN), LOW), pltpu.VMEM((D, SPAN), LOW)],
        compiler_params=pltpu.CompilerParams(vmem_limit_bytes=30 << 20),
        cost_estimate=cost(1),
        name="frame_attention",
    )(tok, msg, w_attn, w_attn, vectors)


def framed_kernel(x_ref, out_ref):
    for f in range(FRAMES):
        rows = jnp.concatenate([wide_of(x_ref[f]), jnp.zeros((SPAN - TOK, D), WIDE)], 0)
        out_ref[f * SPAN : (f + 1) * SPAN, :] = narrow(rows)


def framed(x):
    return pl.pallas_call(
        framed_kernel,
        out_shape=shaped(ROWS, D),
        compiler_params=pltpu.CompilerParams(vmem_limit_bytes=10 << 20),
        cost_estimate=cost(1),
        name="framed",
    )(x)


def valid_rows(shape, first=0):
    row = lax.broadcasted_iota(jnp.int32, shape, 0) + first
    return row % SPAN < TOK


def place_parts(place):
    return lax.div(place, 32), lax.rem(lax.div(place, 8), 4), lax.rem(lax.div(place, 2), 4), lax.rem(place, 2)


CHUNK = 768
CHUNKS = FF // CHUNK


def assemble_up(place_ref, held_ref, out_ref, j):
    x, y, _, _ = place_parts(place_ref[0])
    cols = pl.ds(pl.multiple_of(j * CHUNK, CHUNK), CHUNK)
    for k in range(4):
        slabs = [wide_of(held_ref[z, 48 * k : 48 * k + 48, cols]) for z in range(4)]
        for h in range(2):
            row = pl.multiple_of(((x if h == 0 else 1 - x) * 4 + lax.rem(y + 4 - k, 4)) * 96, 96)
            out_ref[pl.ds(row, 96), :] = narrow(jnp.concatenate([v[24 * h : 24 * h + 24] for v in slabs], 0))


def assemble_down(place_ref, held_ref, out_ref, j):
    x, y, _, core = place_parts(place_ref[0])
    side = lax.rem(lax.div(j, 2) + x, 2)
    for who in range(2):
        col = pl.multiple_of((core if who == 0 else 1 - core) * (D // 2), 128)
        for yl in range(2):
            piece = who * 4 + lax.rem(y + 4 - (lax.rem(j, 2) * 2 + yl), 4)
            for pair in range(2):
                slab = wide_of(held_ref[piece, side, 48 * pair : 48 * pair + 48, :])
                parts = [slab[24 * z : 24 * z + 24, q * (D // 2) : (q + 1) * (D // 2)] for z in range(2) for q in range(4)]
                at = yl * 384 + pair * 192
                out_ref[at : at + 192, pl.ds(col, D // 2)] = narrow(jnp.concatenate(parts, 0))


def mlp_kernel(place_ref, kept_ref, g_ref, vec_ref, perm_ref, *refs):
    up_pieces, down_pieces = refs[:2], refs[2:10]
    lay_ref, gk_ref, dup_keep_ref, dup_give_ref, down_keep_ref, down_give_ref, sums_ref, dub_ref = refs[10:18]
    mlp_ref, mlpt_ref, gt_ref, acc_ref, dacc_ref, held_up_ref, held_down_ref, up_ref, down_ref, sems = refs[18:]
    j = pl.program_id(0)
    core_at = lax.rem(place_ref[0], 2)

    def copies():
        for who in range(2):
            col = pl.multiple_of((core_at if who == 0 else 1 - core_at) * (FF // 2), 128)
            yield pltpu.make_async_copy(up_pieces[who], held_up_ref.at[:, :, pl.ds(col, FF // 2)], sems.at[who])
        for n in range(8):
            yield pltpu.make_async_copy(down_pieces[n], held_down_ref.at[n], sems.at[2 + n])

    @pl.when(j == 0)
    def _():
        for copy in copies():
            copy.start()

    @pl.when(j == 0)
    def _():
        for f in range(FRAMES):
            rows = pl.ds(f * SPAN, SPAN)
            normed, _ = normed_of(kept_ref[rows, :])
            mlp_ref[rows, :] = narrow(normed * vec(vec_ref, GAIN2) + vec(vec_ref, SHIFT2))
        mlpt_ref[...] = narrow(mm_t(perm_ref[...], mlp_ref[...]))
        gt_ref[...] = g_ref[...].T
        acc_ref[...] = kept_ref[...] + vec(vec_ref, DOWN_B)
        dacc_ref[...] = jnp.zeros_like(dacc_ref)
        for copy in copies():
            copy.wait()

    assemble_up(place_ref, held_up_ref, up_ref, j)
    assemble_down(place_ref, held_down_ref, down_ref, j)
    mlp = mlp_ref[...]
    g = g_ref[...]
    up = up_ref[...]
    down = down_ref[...]
    hidden = mm(mlp, up) + vec_ref[pl.ds(UP_B + j, 1), :]
    sig = 0.5 * jnp.tanh(0.851 * hidden) + 0.5
    gated = hidden * sig
    act = narrow(gated)
    acc_ref[...] += mm(act, down)
    gact = wide_of(narrow(mm_t(g, down)))
    gh = narrow(gact * (sig + 1.702 * gated * (1.0 - sig)))
    dub_ref[0] = jnp.broadcast_to(jnp.sum(wide_of(gh), 0, keepdims=True), (8, CHUNK))
    dup = narrow(mm(mlpt_ref[...], gh))
    dup_keep_ref[...] = dup[: D // 2]
    dup_give_ref[...] = dup[D // 2 :]
    dacc_ref[...] += mm_t(gh, up)
    ddown = narrow(mm(gt_ref[...], act).T)
    for core in range(2):

        @pl.when(core_at == core)
        def _():
            for yl in range(2):
                for z in range(4):
                    at = (yl * 4 + z) * 2
                    down_keep_ref[yl, z, 0] = ddown[(at + core) * 48 : (at + core + 1) * 48]
                    down_give_ref[yl, z, 0] = ddown[(at + 1 - core) * 48 : (at + 2 - core) * 48]

    @pl.when(j == CHUNKS - 1)
    def _():
        for f in range(FRAMES):
            lay_ref[f] = narrow(acc_ref[f * SPAN : f * SPAN + TOK, :])
        dg = jnp.zeros((1, D), WIDE)
        dsh = jnp.zeros((1, D), WIDE)
        db = jnp.zeros((1, D), WIDE)
        for f in range(FRAMES):
            rows = pl.ds(f * SPAN, SPAN)
            normed, inverse = normed_of(kept_ref[rows, :])
            gm = dacc_ref[rows, :]
            gw = wide_of(g_ref[rows, :])
            dg += jnp.sum(gm * normed, 0, keepdims=True)
            dsh += jnp.sum(gm, 0, keepdims=True)
            db += jnp.sum(gw, 0, keepdims=True)
            gk = gw + norm_back(gm, normed, inverse, vec(vec_ref, GAIN2))
            gk_ref[rows, :] = jnp.where(valid_rows(gk.shape), gk, 0.0)
        sums_ref[...] = jnp.concatenate([dg, dsh, db, jnp.zeros((5, D), WIDE)], 0)


def once(shape):
    return pl.BlockSpec(shape, lambda *_: (0,) * len(shape), pipeline_mode=pl.Buffered(1))


def mlp(place, kept, grads, up, down, vectors, perm):
    down_spec = pl.BlockSpec((2, 4, 1, 48, D), lambda j: (j % 2, 0, j // 2, 0, 0))
    up_spec = pl.BlockSpec((D // 2, CHUNK), lambda j: (0, j))
    anywhere = pl.BlockSpec(memory_space=pltpu.HBM)
    return pl.pallas_call(
        mlp_kernel,
        grid=(CHUNKS,),
        in_specs=[pl.BlockSpec(memory_space=pltpu.SMEM), once((ROWS, D)), once((ROWS, D)),
                  once((VECTOR_ROWS, D)), once((D, D))] + [anywhere] * 10,
        out_specs=[once((FRAMES, TOK, D)), once((ROWS, D)),
                   up_spec, up_spec, down_spec, down_spec,
                   once((8, D)), pl.BlockSpec((1, 8, CHUNK), lambda j: (j, 0, 0))],
        out_shape=(shaped(FRAMES, TOK, D), shaped(ROWS, D, dtype=WIDE), shaped(D // 2, FF), shaped(D // 2, FF),
                   shaped(4, 4, 2, 48, D), shaped(4, 4, 2, 48, D), shaped(8, D, dtype=WIDE),
                   shaped(CHUNKS, 8, CHUNK, dtype=WIDE)),
        scratch_shapes=[pltpu.VMEM((ROWS, D), LOW), pltpu.VMEM((D, ROWS), LOW), pltpu.VMEM((D, ROWS), LOW),
                        pltpu.VMEM((ROWS, D), WIDE), pltpu.VMEM((ROWS, D), WIDE),
                        pltpu.VMEM((4, 192, FF), LOW), pltpu.VMEM((8, 2, 96, 1536), LOW),
                        pltpu.VMEM((D, CHUNK), LOW), pltpu.VMEM((CHUNK, D), LOW), pltpu.SemaphoreType.DMA((10,))],
        compiler_params=pltpu.CompilerParams(vmem_limit_bytes=52 << 20),
        cost_estimate=cost(1),
        name="mlp_both_ways",
    )(place.reshape(1), kept, grads, vectors, perm, *up, *down)


def head_sums(go, o):
    t = wide_of(go) * wide_of(o)
    high = narrow(t)
    rest = narrow(t - wide_of(high))
    head = lax.broadcasted_iota(jnp.int32, (16, D), 0)
    lane = lax.broadcasted_iota(jnp.int32, (16, D), 1)
    pick = jnp.where((lane // HEAD_DIM) == head, 1.0, 0.0).astype(LOW)
    return mm_t(pick, high) + mm_t(pick, rest)


def out_back_kernel(gk_ref, mixed_ref, wout_ref, perm_ref, gmix_ref, dout_ref, sum_ref):
    gb = narrow(gk_ref[...])
    gmix_ref[...] = narrow(mm_t(gb, wout_ref[...]))
    turned = narrow(mm_t(perm_ref[...], mixed_ref[...]))
    dout_ref[...] = narrow(mm(turned, gb))
    sum_ref[...] = jnp.broadcast_to(jnp.sum(wide_of(gb), 0, keepdims=True), (8, D))


def out_back(gk, mixed, w_attn, perm):
    return pl.pallas_call(
        out_back_kernel,
        grid=(1,),
        in_specs=[whole(gk.shape), whole(mixed.shape), qkv_out_specs()[1], whole(perm.shape)],
        out_specs=(whole((ROWS, D)), whole((D, D)), whole((8, D))),
        out_shape=(shaped(ROWS, D), shaped(D, D), shaped(8, D, dtype=WIDE)),
        compiler_params=pltpu.CompilerParams(vmem_limit_bytes=20 << 20),
        cost_estimate=cost(1),
        name="attention_out_back",
    )(gk, mixed, w_attn, perm)


def attn_bwd_kernel(gmix_ref, mixed_ref, qkv_ref, lse_ref, msg_ref, wqkv_ref, vec_ref,
                    dqkv_ref, sums_ref, gmsg_ref,
                    kt_ref, dqt_ref, rows_ref):
    def frame(f, _):
        rows = pl.ds(pl.multiple_of(f * SPAN, SPAN), SPAN)
        kt_ref[...] = qkv_ref[rows, D : 2 * D].T
        dots = head_sums(gmix_ref[rows, :], mixed_ref[rows, :])
        for p in range(PAIRS):
            cols = lambda part: slice(part * D + p * 128, part * D + (p + 1) * 128)
            q, k, v = (qkv_ref[rows, cols(i)] for i in range(3))
            go = gmix_ref[rows, cols(0)]
            lse = [lse_ref[f, 2 * p + h : 2 * p + h + 1, :] for h in range(2)]
            dot = [dots[2 * p + h : 2 * p + h + 1, :] for h in range(2)]
            dqt, dk, dv = attend_bwd(q, k, v, kt_ref[cols(0), :], go, lse, dot, frame_mask)
            dqt_ref[cols(0), :] = dqt
            dqkv_ref[rows, cols(1)] = dk
            dqkv_ref[rows, cols(2)] = dv
        dqkv_ref[rows, :D] = dqt_ref[...].T
        return 0

    lax.fori_loop(0, FRAMES, frame, 0)
    dqb = jnp.zeros((1, D), WIDE)
    dvb = jnp.zeros((1, D), WIDE)
    for f in range(FRAMES):
        rows = pl.ds(f * SPAN, SPAN)
        dqb += jnp.sum(wide_of(dqkv_ref[rows, :D]), 0, keepdims=True)
        dvb += jnp.sum(wide_of(dqkv_ref[rows, 2 * D :]), 0, keepdims=True)
        tile = wide_of(dqkv_ref[f * SPAN + 192 : f * SPAN + 208, :])
        rows_ref[f : f + 1, :] = tile[TOK - 192 : TOK - 191, :]
    rows_ref[FRAMES:, :] = jnp.zeros((8 - FRAMES, 3 * D), WIDE)
    sums_ref[...] = jnp.concatenate([dqb, dvb, jnp.zeros((6, D), WIDE)], 0)
    back = mm_t(narrow(rows_ref[...]), wqkv_ref[...])
    normed, inverse = normed_of(msg_ref[...])
    gmsg_ref[...] = norm_back(back[:FRAMES], normed, inverse, vec(vec_ref, GAIN1))


def attn_bwd(gmix, mixed, qkv, lse, msg, w_attn, vectors):
    return pl.pallas_call(
        attn_bwd_kernel,
        grid=(1,),
        in_specs=[whole(gmix.shape), whole(mixed.shape), whole(qkv.shape), whole(lse.shape), whole(msg.shape),
                  qkv_out_specs()[0], whole(vectors.shape)],
        out_specs=(whole((ROWS, 3 * D)), whole((8, D)), whole((FRAMES, D))),
        out_shape=(shaped(ROWS, 3 * D), shaped(8, D, dtype=WIDE), shaped(FRAMES, D, dtype=WIDE)),
        scratch_shapes=[pltpu.VMEM((D, SPAN), LOW), pltpu.VMEM((D, SPAN), LOW), pltpu.VMEM((8, 3 * D), WIDE)],
        compiler_params=pltpu.CompilerParams(vmem_limit_bytes=56 << 20),
        cost_estimate=cost(1),
        name="frame_attention_back",
    )(gmix, mixed, qkv, lse, msg, w_attn, vectors)


def tokens_back_kernel(dqkv_ref, wqkv_ref, gk_ref, tok_ref, msg_ref, vec_ref, blk_ref, perm_ref, dout_ref,
                       sum_out_ref, sums_mlp_ref, placed_ref, out_ref, keep_ref, give_ref, joined_ref):
    turned = narrow(mm_t(perm_ref[...], blk_ref[...]))
    for n in range(3):
        cols = slice(n * D, (n + 1) * D)
        dw = narrow(mm(turned, dqkv_ref[:, cols]))
        keep_ref[:, cols] = dw[: D // 2]
        give_ref[:, cols] = dw[D // 2 :]
    keep_ref[:, 3 * D : FF] = dout_ref[: D // 2]
    give_ref[:, 3 * D : FF] = dout_ref[D // 2 :]
    fill_joined(tok_ref, msg_ref, joined_ref)
    dg = jnp.zeros((1, D), WIDE)
    dsh = jnp.zeros((1, D), WIDE)
    back_all = mm_t(dqkv_ref[...], wqkv_ref[...])
    for f in range(FRAMES):
        rows = pl.ds(f * SPAN, SPAN)
        back = back_all[f * SPAN : (f + 1) * SPAN]
        normed, inverse = normed_of(joined_ref[rows, :])
        dg += jnp.sum(back * normed, 0, keepdims=True)
        dsh += jnp.sum(back, 0, keepdims=True)
        full = gk_ref[rows, :] + norm_back(back, normed, inverse, vec(vec_ref, GAIN1))
        out_ref[f] = full[:TOK]
    sums = jnp.concatenate(
        [dg, dsh, sum_out_ref[:1, :], sums_mlp_ref[:3, :], placed_ref[...], jnp.zeros((116, D), WIDE)], 0
    )
    turned = narrow(mm_t(perm_ref[...], narrow(sums)))
    keep_ref[:, FF:] = turned[: D // 2]
    give_ref[:, FF:] = turned[D // 2 :]


def tokens_back(dqkv, w_attn, gk, tok, msg, vectors, blk, perm, dout, sum_out, sums_mlp, placed):
    return pl.pallas_call(
        tokens_back_kernel,
        grid=(1,),
        in_specs=[whole(dqkv.shape), qkv_out_specs()[0], whole(gk.shape), whole(tok.shape), whole(msg.shape),
                  whole(vectors.shape), whole(blk.shape), whole(perm.shape), whole(dout.shape),
                  whole(sum_out.shape), whole(sums_mlp.shape), whole(placed.shape)],
        out_specs=(whole((FRAMES, TOK, D)), whole((D // 2, FF + 128)), whole((D // 2, FF + 128))),
        out_shape=(shaped(FRAMES, TOK, D, dtype=WIDE), shaped(D // 2, FF + 128), shaped(D // 2, FF + 128)),
        scratch_shapes=[pltpu.VMEM((ROWS, D), WIDE)],
        compiler_params=pltpu.CompilerParams(vmem_limit_bytes=42 << 20),
        cost_estimate=cost(1),
        name="tokens_back",
    )(dqkv, w_attn, gk, tok, msg, vectors, blk, perm, dout, sum_out, sums_mlp, placed)


ALL = 256


def group_mask(grow_ref, gcol_ref):
    same = gcol_ref[:, 0:1] == grow_ref[0:1, :]

    def mask(s):
        return jnp.where(same, s, -1000000000.0)

    return mask


def msg_fwd_kernel(cls_ref, w_ref, vec_ref, grow_ref, gcol_ref,
                   message_ref, token_ref, min_ref, qkv_ref, mixed_ref, lse_ref, vt_ref, ot_ref):
    message = mm(cls_ref[...], w_ref[:, :D]) + vec(vec_ref, FC_B)
    message_ref[...] = message
    normed, _ = normed_of(message)
    min_ref[...] = narrow(normed * vec(vec_ref, MSG_GAIN) + vec(vec_ref, MSG_SHIFT))
    for n in range(9):
        y = mm(min_ref[...], w_ref[:, D + n * 256 : D + (n + 1) * 256])
        if n < 3:
            y = y + vec_ref[MQ_B : MQ_B + 1, n * 256 : (n + 1) * 256]
        if n >= 6:
            y = y + vec_ref[MV_B : MV_B + 1, (n - 6) * 256 : (n - 5) * 256]
        qkv_ref[:, n * 256 : (n + 1) * 256] = narrow(y)
    vt_ref[...] = qkv_ref[:, 2 * D :].T
    mask = group_mask(grow_ref, gcol_ref)
    lse_ref[...] = jnp.zeros_like(lse_ref)
    for p in range(PAIRS):
        q = qkv_ref[:, p * 128 : (p + 1) * 128]
        k = qkv_ref[:, D + p * 128 : D + (p + 1) * 128]
        vt = vt_ref[p * 128 : (p + 1) * 128, :]
        for h, (o, l) in enumerate(attend_fwd(q, k, vt, None, mask)):
            at = p * 128 + h * HEAD_DIM
            ot_ref[at : at + HEAD_DIM, :] = narrow(o)
            lse_ref[2 * p + h : 2 * p + h + 1, :] = l
    mixed_ref[...] = ot_ref[...].T
    token_ref[...] = message + mm(mixed_ref[...], w_ref[:, 4 * D :]) + vec(vec_ref, MOUT_B)


def msg_fwd(cls, w, vectors, grow, gcol):
    return pl.pallas_call(
        msg_fwd_kernel,
        out_shape=(shaped(ALL, D, dtype=WIDE), shaped(ALL, D, dtype=WIDE), shaped(ALL, D), shaped(ALL, 3 * D),
                   shaped(ALL, D), shaped(16, ALL, dtype=WIDE)),
        scratch_shapes=[pltpu.VMEM((D, ALL), LOW), pltpu.VMEM((D, ALL), LOW)],
        compiler_params=pltpu.CompilerParams(vmem_limit_bytes=20 << 20),
        cost_estimate=cost(1),
        name="message_forward",
    )(cls, w, vectors, grow, gcol)


def msg_bwd_kernel(gm_ref, cls_ref, message_ref, min_ref, qkv_ref, mixed_ref, lse_ref, w_ref, vec_ref,
                   grow_ref, gcol_ref, pick_ref,
                   gcls_ref, dw_ref, sums_ref,
                   gmix_ref, kt_ref, dqt_ref, dqkv_ref):
    gb = gm_ref[...]
    pick = pick_ref[...]
    turned = lambda x: narrow(mm_t(pick, x))
    gmix_ref[...] = narrow(mm_t(gb, w_ref[:, 4 * D :]))
    dw_ref[:, 4 * D :] = mm(turned(mixed_ref[...]), gb)
    kt_ref[...] = qkv_ref[:, D : 2 * D].T
    mask = group_mask(grow_ref, gcol_ref)
    dots = head_sums(gmix_ref[...], mixed_ref[...])
    for p in range(PAIRS):
        cols = lambda part: slice(part * D + p * 128, part * D + (p + 1) * 128)
        q, k, v = (qkv_ref[:, cols(i)] for i in range(3))
        go = gmix_ref[:, cols(0)]
        lse = [lse_ref[2 * p + h : 2 * p + h + 1, :] for h in range(2)]
        dot = [dots[2 * p + h : 2 * p + h + 1, :] for h in range(2)]
        dqt, dk, dv = attend_bwd(q, k, v, kt_ref[cols(0), :], go, lse, dot, mask)
        dqt_ref[cols(0), :] = dqt
        dqkv_ref[:, cols(1)] = dk
        dqkv_ref[:, cols(2)] = dv
    dqkv_ref[:, :D] = dqt_ref[...].T
    dqkv = dqkv_ref[...]
    dw_ref[:, D : 4 * D] = mm(turned(min_ref[...]), dqkv)
    back = mm_t(dqkv, w_ref[:, D : 4 * D])
    normed, inverse = normed_of(message_ref[...])
    gfc = narrow(wide_of(gb) + norm_back(back, normed, inverse, vec(vec_ref, MSG_GAIN)))
    dw_ref[:, :D] = mm(turned(cls_ref[...]), gfc)
    gcls_ref[...] = mm_t(gfc, w_ref[:, :D])
    col = lambda x: jnp.sum(wide_of(x), 0, keepdims=True)
    sums_ref[...] = jnp.concatenate(
        [col(gfc), col(back * normed), col(back), col(gb), col(dqkv[:, :D]), col(dqkv[:, 2 * D :]),
         jnp.zeros((2, D), WIDE)], 0)


def msg_bwd(gm, cls, message, mins, qkv, mixed, lse, w, vectors, grow, gcol, pick):
    return pl.pallas_call(
        msg_bwd_kernel,
        out_shape=(shaped(ALL, D, dtype=WIDE), shaped(16, 5 * D, dtype=WIDE), shaped(8, D, dtype=WIDE)),
        scratch_shapes=[pltpu.VMEM((ALL, D), LOW), pltpu.VMEM((D, ALL), LOW), pltpu.VMEM((D, ALL), LOW),
                        pltpu.VMEM((ALL, 3 * D), LOW)],
        compiler_params=pltpu.CompilerParams(vmem_limit_bytes=48 << 20),
        cost_estimate=cost(1),
        name="message_back",
    )(gm, cls, message, mins, qkv, mixed, lse, w, vectors, grow, gcol, pick)


def frame_of(x_hi, y, z, core):
    return ((x_hi * 4 + y) * 4 + z) * 2 + core


PLACES = list(itertools.product(range(2), range(4), range(4), range(2), range(2)))


def moves(to):
    return [(frame_of(*p[:4]) * 2 + p[4], frame_of(*to(*p)[:4]) * 2 + to(*p)[4]) for p in PLACES]


TO_CORE = moves(lambda x, y, z, c, v: (x, y, z, 1 - c, v))
TO_VIDEO = moves(lambda x, y, z, c, v: (x, y, z, c, 1 - v))
TO_HALF = moves(lambda x, y, z, c, v: (1 - x, y, z, c, v))
TO_BOTH = moves(lambda x, y, z, c, v: (1 - x, y, z, c, 1 - v))
TO_Y = [moves(lambda x, y, z, c, v, k=k: (x, (y + k) % 4, z, c, v)) for k in range(4)]
TO_Z = [moves(lambda x, y, z, c, v, k=k: (x, y, (z + k) % 4, c, v)) for k in range(4)]
ALONG_Y = [[frame_of(x, y, z, c) for y in range(4)] for x in range(2) for z in range(4) for c in range(2)]
ALONG_Z = [[frame_of(x, y, z, c) for z in range(4)] for x in range(2) for y in range(4) for c in range(2)]
PLANE = [[frame_of(x, y, z, c) for y in range(4) for z in range(4)] for x in range(2) for c in range(2)]
def sent(x, pairs):
    return lax.ppermute(x, ("frame", "video"), pairs)


def to_everyone(x):
    return lax.all_to_all(jnp.broadcast_to(x[None], (64, *x.shape)), "frame", 0, 0, tiled=True)


def assemble_y_kernel(place_ref, *refs):
    pieces, out_ref, sems = refs[:8], refs[8], refs[9]
    x, y, _, core = place_parts(place_ref[0])
    span, half = 96, 1536
    copies = []
    for who in range(2):
        col = pl.multiple_of((core if who == 0 else 1 - core) * half, 128)
        for k in range(4):
            for h in range(2):
                row = pl.multiple_of(((x if h == 0 else 1 - x) * 4 + lax.rem(y + 4 - k, 4)) * span, span)
                copies.append(
                    pltpu.make_async_copy(
                        pieces[who * 4 + k].at[h],
                        out_ref.at[pl.ds(row, span), pl.ds(col, half)],
                        sems.at[len(copies)],
                    )
                )
                copies[-1].start()
    for done in copies:
        done.wait()


def assemble_z_kernel(place_ref, *refs):
    pieces, out_ref, held_ref, sems = refs[:-3], refs[-3], refs[-2], refs[-1]
    x, y, z, core = place_parts(place_ref[0])
    each = len(pieces) // 2
    half = pieces[0].shape[-1]
    copies = []
    for n, piece_ref in enumerate(pieces):
        col = pl.multiple_of((core if n < each else 1 - core) * half, 128)
        copies.append(pltpu.make_async_copy(piece_ref, held_ref.at[n % 4, :, pl.ds(col, half)], sems.at[n]))
        copies[-1].start()
    for done in copies:
        done.wait()
    for cols in range(0, 2 * half, D):
        for k in range(4):
            slabs = [
                wide_of(held_ref[lax.rem(z + 4 - to, 4), 48 * k : 48 * k + 48, cols : cols + D])
                for to in range(4)
            ]
            for h in range(2):
                row = pl.multiple_of(((x if h == 0 else 1 - x) * 4 + lax.rem(y + 4 - k, 4)) * 96, 96)
                out_ref[pl.ds(row, 96), cols : cols + D] = narrow(
                    jnp.concatenate([v[24 * h : 24 * h + 24] for v in slabs], 0)
                )


def assembled(kernel, place, pieces, out, scratch):
    anywhere = pl.BlockSpec(memory_space=pltpu.HBM)
    return pl.pallas_call(
        kernel,
        in_specs=[pl.BlockSpec(memory_space=pltpu.SMEM)] + [anywhere] * len(pieces),
        out_shape=out,
        scratch_shapes=scratch,
        compiler_params=pltpu.CompilerParams(vmem_limit_bytes=24 << 20),
        cost_estimate=cost(1),
        name="assemble_weights",
    )(place.reshape(1), *pieces)


def assemble_y(place, pieces):
    return assembled(assemble_y_kernel, place, pieces, shaped(D, FF), [pltpu.SemaphoreType.DMA((16,))])


def assemble_z(place, pieces):
    half = pieces[0].shape[-1]
    scratch = [pltpu.VMEM((4, 192, 2 * half), LOW), pltpu.SemaphoreType.DMA((len(pieces),))]
    return assembled(assemble_z_kernel, place, pieces, shaped(D, 2 * half), scratch)


def pack_kernel(place_ref, qkv_ref, out_ref, fc_ref, mqkv_ref, mout_ref, up_ref, down_ref, mine_ref, give_ref,
                down_mine_ref, down_give_ref):
    def put(which, to_ref, down_to_ref):
        parts = (
            (qkv_ref[:, :1536], fc_ref[...], mqkv_ref[:, :1152], up_ref[:, :1536]),
            (qkv_ref[:, 1536:], out_ref[...], mqkv_ref[:, 1152:], mout_ref[...], up_ref[:, 1536:]),
        )[which]
        to_ref[...] = jnp.concatenate(parts, 1)
        down_to_ref[...] = down_ref[:, which * 384 : which * 384 + 384]

    for core in range(2):

        @pl.when(lax.rem(place_ref[0], 2) == core)
        def _():
            put(core, mine_ref, down_mine_ref)
            put(1 - core, give_ref, down_give_ref)


def packed(place, *shards):
    mine, give, down_mine, down_give = pl.pallas_call(
        pack_kernel,
        in_specs=[pl.BlockSpec(memory_space=pltpu.SMEM)] + [pl.BlockSpec(memory_space=pltpu.VMEM)] * 7,
        out_shape=(shaped(12, 4992), shaped(12, 4992), shaped(48, 384), shaped(48, 384)),
        cost_estimate=cost(1),
        name="pack_weights",
    )(place.reshape(1), *shards)
    return (mine, give), (down_mine, down_give)


def core_pair(place, halves):
    mine, got = halves[0], sent(halves[1], TO_CORE)
    return jnp.where(place % 2 == 0, jnp.concatenate([mine, got], 0), jnp.concatenate([got, mine], 0))


def both_x(pair):
    return jnp.stack([pair, sent(pair, TO_HALF)])


def ring_z(pair):
    return jnp.swapaxes(from_z(jnp.broadcast_to(pair[None], (4, *pair.shape))), 0, 1).reshape(2, -1, pair.shape[2])


def ring_y(pair):
    return jnp.stack([pair, *(sent(pair, TO_Y[k]) for k in range(1, 4))]).reshape(192, -1)


def around(x, moves_by):
    return [x, *(sent(x, moves_by[k]) for k in range(1, 4))]


def from_z(copies):
    return lax.all_to_all(copies, "frame", 0, 0, axis_index_groups=ALONG_Z, tiled=True)


def both_cores(pieces):
    return [*pieces, *(sent(x, TO_CORE) for x in pieces)]


def after(x, *others):
    return lax.optimization_barrier((x, *others))


def row_order(place):
    row = jnp.arange(D, dtype=jnp.int32)
    r, x, z, y, c = row % 12, row // 12 % 2, row // 24 % 4, row // 96 % 4, row // 384
    natural = ((((x * 4 + y) * 4 + z) * 2) + jnp.where(c == 0, place % 2, 1 - place % 2)) * 12 + r
    return (natural[:, None] == row[None, :]).astype(LOW)


def add_pack_kernel(keep_up, got_up, keep_down, got_down, out_ref):
    up = wide_of(keep_up[...]) + wide_of(got_up[...])
    down = wide_of(keep_down[0]) + wide_of(got_down[0])
    for i in range(2):
        out_ref[i, :, :FF] = narrow(up[24 * i : 24 * i + 24])
        slab = jnp.concatenate([down[i, 0], down[i, 1]], 0)
        for q in range(4):
            both = [slab[48 * h + 12 * q : 48 * h + 12 * q + 12] for h in range(2)]
            out_ref[i, :, FF + q * D : FF + (q + 1) * D] = narrow(jnp.concatenate(both, 0))


def add_pack(keep_up, got_up, keep_down, got_down):
    down_spec = pl.BlockSpec((1, 2, 2, 48, D), lambda i: (i // 2, i % 2, 0, 0, 0))
    up_spec = pl.BlockSpec((48, FF), lambda i: (i, 0))
    return pl.pallas_call(
        add_pack_kernel,
        grid=(8,),
        in_specs=[up_spec, up_spec, down_spec, down_spec],
        out_specs=pl.BlockSpec((2, 24, 2 * FF), lambda i: (i, 0, 0)),
        out_shape=shaped(16, 24, 2 * FF),
        compiler_params=pltpu.CompilerParams(vmem_limit_bytes=14 << 20),
        cost_estimate=cost(1),
        name="add_mlp_gradients",
    )(keep_up, got_up, keep_down, got_down)


def ring_sum(parts, groups):
    return lax.psum_scatter(parts, "frame", scatter_dimension=0, axis_index_groups=groups, tiled=True)


def on_plane(parts):
    return lax.all_to_all(parts, "frame", 0, 0, axis_index_groups=PLANE, tiled=True)


def last_kernel(mine_ref, video_ref, half_ref, both_ref, more_ref, *out_refs):
    n = mine_ref.shape[1]
    video = wide_of(video_ref[...])
    total = wide_of(mine_ref[...]) + video[:, :n] + wide_of(half_ref[...]) + wide_of(both_ref[...])
    if video.shape[1] > n:
        total = jnp.concatenate([total, more_ref[...] + video[:, n:]], 1)
    at = 0
    for out_ref in out_refs:
        out_ref[...] = total[:, at : at + out_ref.shape[1]]
        at += out_ref.shape[1]


def last_sums(rows, half, widths, more=None):
    mine, other = (lax.dynamic_slice_in_dim(rows, which * 12, 12, 0) for which in (half, 1 - half))
    give = mine if more is None else jnp.concatenate([mine, narrow(more)], 1)
    if more is None:
        more = jnp.zeros((8, 128), WIDE)
    return pl.pallas_call(
        last_kernel,
        out_shape=tuple(shaped(12, w, dtype=WIDE) for w in widths),
        cost_estimate=cost(1),
        name="last_sums",
    )(mine, sent(give, TO_VIDEO), sent(other, TO_HALF), sent(other, TO_BOTH), more)


def shards(
    tokens_in,
    clip_ids,
    grad_out,
    msg_fc_w,
    msg_fc_b,
    msg_norm_gain,
    msg_norm_shift,
    msg_qkv_w,
    msg_qv_b,
    msg_out_w,
    msg_out_b,
    norm1_gain,
    norm1_shift,
    attn_qkv_w,
    attn_qv_b,
    attn_out_w,
    attn_out_b,
    norm2_gain,
    norm2_shift,
    mlp_in_w,
    mlp_in_b,
    mlp_out_w,
    mlp_out_b,
):
    place = lax.axis_index("frame").astype(jnp.int32)
    core, half = place % 2, place // 32
    tok = tokens_in[0]
    small = jnp.concatenate(
        [
            tok[:, 0, :].reshape(-1),
            msg_fc_b,
            msg_norm_gain,
            msg_norm_shift,
            msg_out_b,
            norm1_gain,
            norm1_shift,
            attn_out_b,
            norm2_gain,
            norm2_shift,
            mlp_out_b,
            msg_qv_b,
            attn_qv_b,
            mlp_in_b,
            clip_ids[0].astype(LOW),
        ]
    )
    small = jnp.pad(small, (0, 4096 - small.shape[0])).reshape(32, 128)
    w_halves, down_halves = packed(
        place, attn_qkv_w, attn_out_w, msg_fc_w, msg_qkv_w, msg_out_w, mlp_in_w, mlp_out_w
    )
    w_pair = core_pair(place, w_halves)
    down_pair = core_pair(place, down_halves).reshape(4, 24, 384).transpose(1, 0, 2).reshape(24, 1536)
    w_x = both_x(jnp.concatenate([w_pair[:, :1536], down_pair, w_pair[:, 1536:]], 1))
    by_y, by_z = ring_z(w_x[:, :, :3072]), ring_y(w_x[:, :, 3072:])
    by_y, by_z, small = after(by_y, by_z, small)
    small_all = to_everyone(small)
    attn = by_y[:, :, :1536]
    attn_last, late_z = after(attn, jnp.broadcast_to(by_z[None, :, 1920:], (4, 192, 1536)))
    msg_all = around(by_z[:, :1920], TO_Z)
    attn_all = [attn, sent(attn_last, TO_Y[1]), sent(attn, TO_Y[2]), sent(attn, TO_Y[3])]
    msg_all, attn_all, small_all, late_y, late_z, grads = after(
        msg_all, attn_all, small_all, by_y[:, :, 1536:], late_z, framed(grad_out[0])
    )
    up_all, down_all = [from_z(late_z)], around(late_y, TO_Y)
    small_all = small_all.reshape(64, 4096)
    cls = small_all[:, :3072].reshape(ALL, D)
    at = 3072
    vectors = small_all[:, at : at + 120].reshape(64, 10, 12).transpose(1, 0, 2).reshape(10, D)
    biases = [small_all[:, at + 120 + a : at + 120 + b].reshape(-1, D) for a, b in ((0, 24), (24, 48), (48, 96))]
    vectors = wide_of(jnp.concatenate([vectors, *biases, jnp.zeros((VECTOR_ROWS - 18, D), LOW)], 0))
    at = at + 216
    groups = wide_of(small_all[:, at : at + 4].reshape(ALL))
    grow = jnp.broadcast_to(groups[None], (8, ALL))
    gcol = jnp.broadcast_to(groups[:, None], (ALL, 128))
    order = row_order(place)
    pick_row = jnp.arange(16, dtype=jnp.int32)[:, None]
    pick_col = jnp.arange(D, dtype=jnp.int32)[None, :]
    pick = ((pick_row < 12) & (pick_col == place * 12 + pick_row)).astype(LOW)

    msg_all, vectors, order, pick, cls, grow, gcol = after(msg_all, vectors, order, pick, cls, grow, gcol)
    w_msg = assemble_z(place, both_cores(msg_all))
    message, token, mins, mqkv, mmixed, mlse = msg_fwd(cls, w_msg, vectors, grow, gcol)
    token, attn_all = after(token, attn_all)
    w_attn = assemble_y(place, both_cores(attn_all))
    msg = lax.dynamic_slice_in_dim(token, place * FRAMES, FRAMES)
    qkv, mixed, kept, lse, blk = attn_fwd(tok, msg, w_attn, vectors)
    kept, up_all, down_all = after(kept, up_all, down_all)
    lay, gk, dup_keep, dup_give, down_keep, down_give, sums_mlp, dub = mlp(
        place, kept, grads, both_cores(up_all), both_cores(down_all), vectors, order
    )
    dup_got, down_got = sent(dup_give, TO_CORE), sent(down_give, TO_CORE)
    gmix, dout, sum_out = out_back(gk, mixed, w_attn, order)
    gmix, dup_got, down_got = after(gmix, dup_got, down_got)
    mlp_parts, gmix = after(add_pack(dup_keep, dup_got, down_keep, down_got), gmix)
    mlp_half = ring_sum(mlp_parts, ALONG_Y)
    dqkv, sums_attn, gmsg = attn_bwd(gmix, mixed, qkv, lse, msg, w_attn, vectors)
    gmsg = jnp.broadcast_to(narrow(gmsg)[None], (64, FRAMES, D))
    gmsg, dqkv = after(gmsg, dqkv)
    gmsg_all = lax.all_to_all(gmsg, "frame", 0, 0, tiled=True).reshape(ALL, D)
    by_place = lambda x, n: x.reshape(64, n, 12).transpose(1, 0, 2).reshape(n, D)
    placed = jnp.concatenate([by_place(sums_attn[:2], 2), by_place(dub[:, 0], 4)], 0)
    grad_tokens, attn_keep, attn_give = tokens_back(dqkv, w_attn, gk, tok, msg, vectors, blk, order, dout, sum_out, sums_mlp, placed)
    attn_keep, attn_give, gmsg_all, mlp_half = after(attn_keep, attn_give, gmsg_all, mlp_half)
    mlp_sum = ring_sum(mlp_half, ALONG_Z).reshape(24, 2 * FF)
    attn_got = sent(attn_give, TO_CORE)
    attn_part = narrow(wide_of(attn_keep) + wide_of(attn_got))
    attn_part, lay, gmsg_all = after(attn_part, lay, gmsg_all)
    attn_all = on_plane(attn_part.reshape(16, 24, FF + 128))
    gcls, dw_msg, sums_msg = msg_bwd(gmsg_all, cls, message, mins, mqkv, mmixed, mlse, w_msg, vectors, grow, gcol, pick)
    gcls = lax.dynamic_slice_in_dim(gcls, place * FRAMES, FRAMES)
    grad_tokens = grad_tokens.at[:, 0, :].add(gcls)
    own = lax.dynamic_slice_in_dim(sums_msg[:4], place * 12, 12, 1).reshape(-1)
    own_qv = lax.dynamic_slice_in_dim(sums_msg[4:6].reshape(-1), place * 24, 24)
    own = jnp.concatenate([own, own_qv])
    msg_rows = dw_msg[:12]
    attn_all, mlp_sum, msg_rows, own, grad_tokens, lay = after(attn_all, mlp_sum, msg_rows, own, grad_tokens, lay)
    mlp_rows, *down_rows, msg_fc, msg_qkv, msg_out = last_sums(
        mlp_sum, half, (FF, D, D, D, D, D, 3 * D, D), msg_rows
    )
    down_rows = jnp.concatenate(down_rows, 0)
    qkv_rows, out_rows, ends = last_sums(narrow(jnp.sum(wide_of(attn_all), 0)), half, (3 * D, D, 128))
    own = own + sent(own, TO_VIDEO)
    fb, mg, ms, mob, mqvb = jnp.split(own, [12, 24, 36, 48])
    ends = ends[:, :12].T
    g1, s1, ob, g2, s2, db = (ends[k] for k in range(6))
    qvb, ub = ends[6:8].reshape(-1), ends[8:12].reshape(-1)
    return (
        lay[None],
        grad_tokens[None],
        msg_fc,
        fb,
        mg,
        ms,
        msg_qkv,
        mqvb,
        msg_out,
        mob,
        g1,
        s1,
        qkv_rows,
        qvb,
        out_rows,
        ob,
        g2,
        s2,
        mlp_rows,
        ub,
        down_rows,
        db,
    )


def solution(mesh):
    in_specs = (
        P("video", "frame", None, None),
        P("video", "frame"),
        P("video", "frame", None, None),
        P("frame", None),
        P("frame"),
        P("frame"),
        P("frame"),
        P("frame", None),
        P("frame"),
        P("frame", None),
        P("frame"),
        P("frame"),
        P("frame"),
        P("frame", None),
        P("frame"),
        P("frame", None),
        P("frame"),
        P("frame"),
        P("frame"),
        P("frame", None),
        P("frame"),
        P("frame", None),
        P("frame"),
    )
    out_specs = (
        P("video", "frame", None, None),
        P("video", "frame", None, None),
        P("frame", None),
        P("frame"),
        P("frame"),
        P("frame"),
        P("frame", None),
        P("frame"),
        P("frame", None),
        P("frame"),
        P("frame"),
        P("frame"),
        P("frame", None),
        P("frame"),
        P("frame", None),
        P("frame"),
        P("frame"),
        P("frame"),
        P("frame", None),
        P("frame"),
        P("frame", None),
        P("frame"),
    )
    return jax.shard_map(shards, mesh=mesh, in_specs=in_specs, out_specs=out_specs, check_vma=False)
```

```python
import functools
import itertools
import jax
import jax.numpy as jnp
from jax import lax
from jax.experimental import pallas as pl
from jax.experimental.pallas import tpu as pltpu
from jax.sharding import PartitionSpec as P

HEAD_DIM = 64
FRAMES = 4
TOK = 197
SPAN = 208
ROWS = FRAMES * SPAN
D = 768
FF = 3072
HEADS = 12
PAIRS = 6
WIDE = jnp.float32
LOW = jnp.bfloat16
SCALE = HEAD_DIM ** (-0.5)
FC_B, MSG_GAIN, MSG_SHIFT, MOUT_B, GAIN1, SHIFT1, OUT_B, GAIN2, SHIFT2, DOWN_B, MQ_B, MV_B, Q_B, V_B, UP_B = range(15)
VECTOR_ROWS = 24


def narrow(x):
    return x.astype(LOW)


def wide_of(x):
    return x.astype(WIDE)


def mm(a, b):
    return lax.dot_general(a, b, (((1,), (0,)), ((), ())), preferred_element_type=WIDE)


def mm_t(a, b):
    return lax.dot_general(a, b, (((1,), (1,)), ((), ())), preferred_element_type=WIDE)


def normed_of(x):
    center = x - jnp.mean(x, -1, keepdims=True)
    inverse = lax.rsqrt(jnp.mean(center * center, -1, keepdims=True) + 1e-05)
    return center * inverse, inverse


def norm_back(grad, normed, inverse, gain):
    scaled = grad * gain
    return inverse * (
        scaled
        - jnp.mean(scaled, -1, keepdims=True)
        - normed * jnp.mean(scaled * normed, -1, keepdims=True)
    )


def own_lanes(x, which):
    lane = lax.broadcasted_iota(jnp.int32, x.shape, 1)
    return jnp.where((lane < HEAD_DIM) == (which == 0), x, jnp.zeros_like(x))


def either(a, b):
    lane = lax.broadcasted_iota(jnp.int32, a.shape, 1)
    return jnp.where(lane < HEAD_DIM, a, b)


def vec(vec_ref, row):
    return vec_ref[row : row + 1, :]


def fill_joined(tok_ref, msg_ref, joined_ref):
    for f in range(FRAMES):
        joined_ref[f * SPAN : f * SPAN + TOK, :] = wide_of(tok_ref[f])
        joined_ref[f * SPAN + TOK : f * SPAN + TOK + 1, :] = msg_ref[f : f + 1, :]
        joined_ref[f * SPAN + TOK + 1 : (f + 1) * SPAN, :] = jnp.zeros((SPAN - TOK - 1, D), WIDE)


def attend_fwd(q, k, vt, valid, mask):
    out = []
    for h in range(2):
        s = mm_t(own_lanes(k, h), q) * SCALE
        s = mask(s)
        peak = jnp.max(s, 0, keepdims=True)
        e = jnp.exp(s - peak)
        total = jnp.sum(e, 0, keepdims=True)
        o = mm(vt[h * HEAD_DIM : (h + 1) * HEAD_DIM], narrow(e)) / total
        out.append((o, peak + jnp.log(total)))
    return out


def attend_bwd(q, k, v, kt, go, lse, dot, mask):
    dqt, dk, dv = [], [], []
    for h in range(2):
        s = mask(mm_t(own_lanes(k, h), q) * SCALE)
        p = jnp.exp(s - lse[h])
        dp = mm_t(own_lanes(v, h), go)
        ds = narrow(p * (dp - dot[h]))
        dv.append(mm(narrow(p), go))
        dk.append(mm(ds, q))
        dqt.append(mm(kt[h * HEAD_DIM : (h + 1) * HEAD_DIM], ds))
    return (
        narrow(jnp.concatenate(dqt, 0) * SCALE),
        narrow(either(*dk) * SCALE),
        narrow(either(*dv)),
    )


def frame_mask(s):
    key = lax.broadcasted_iota(jnp.int32, s.shape, 0)
    return jnp.where(key <= TOK, s, -1e30)


def attn_fwd_kernel(tok_ref, msg_ref, wqkv_ref, wout_ref, vec_ref,
                    qkv_ref, mixed_ref, kept_ref, lse_ref, blk_ref, vt_ref, ot_ref):
    fill_joined(tok_ref, msg_ref, kept_ref)
    for f in range(FRAMES):
        rows = pl.ds(f * SPAN, SPAN)
        normed, _ = normed_of(kept_ref[rows, :])
        blk_ref[rows, :] = narrow(normed * vec(vec_ref, GAIN1) + vec(vec_ref, SHIFT1))
    for n in range(9):
        cols = pl.ds(n * 256, 256)
        y = mm(blk_ref[...], wqkv_ref[:, cols])
        if n < 3:
            y = y + vec_ref[Q_B : Q_B + 1, n * 256 : (n + 1) * 256]
        if n >= 6:
            y = y + vec_ref[V_B : V_B + 1, (n - 6) * 256 : (n - 5) * 256]
        qkv_ref[:, cols] = narrow(y)
    lse_ref[...] = jnp.zeros_like(lse_ref)

    def frame(f, _):
        rows = pl.ds(pl.multiple_of(f * SPAN, SPAN), SPAN)
        vt_ref[...] = qkv_ref[rows, 2 * D :].T
        for p in range(PAIRS):
            q = qkv_ref[rows, p * 128 : (p + 1) * 128]
            k = qkv_ref[rows, D + p * 128 : D + (p + 1) * 128]
            vt = vt_ref[p * 128 : (p + 1) * 128, :]
            for h, (o, l) in enumerate(attend_fwd(q, k, vt, None, frame_mask)):
                at = p * 128 + h * HEAD_DIM
                ot_ref[at : at + HEAD_DIM, :] = narrow(o)
                lse_ref[f, 2 * p + h : 2 * p + h + 1, :] = l
        mixed_ref[rows, :] = ot_ref[...].T
        return 0

    lax.fori_loop(0, FRAMES, frame, 0)
    kept_ref[...] = kept_ref[...] + mm(mixed_ref[...], wout_ref[...]) + vec(vec_ref, OUT_B)


def cost(us):
    return pl.CostEstimate(flops=int(us * 1e6), bytes_accessed=int(us * 1e3), transcendentals=0)


def qkv_out_specs():
    return [pl.BlockSpec((D, 3 * D), lambda *_: (0, 0)), pl.BlockSpec((D, D), lambda *_: (0, 3))]


def whole(shape):
    return pl.BlockSpec(shape, lambda *_: (0,) * len(shape))


def shaped(*shape, dtype=LOW):
    return jax.ShapeDtypeStruct(shape, dtype)


def attn_fwd(tok, msg, w_attn, vectors):
    return pl.pallas_call(
        attn_fwd_kernel,
        grid=(1,),
        in_specs=[whole(tok.shape), whole(msg.shape), *qkv_out_specs(), whole(vectors.shape)],
        out_specs=(whole((ROWS, 3 * D)), whole((ROWS, D)), whole((ROWS, D)), whole((FRAMES, 16, SPAN)), whole((ROWS, D))),
        out_shape=(shaped(ROWS, 3 * D), shaped(ROWS, D), shaped(ROWS, D, dtype=WIDE),
                   shaped(FRAMES, 16, SPAN, dtype=WIDE), shaped(ROWS, D)),
        scratch_shapes=[pltpu.VMEM((D, SPAN), LOW), pltpu.VMEM((D, SPAN), LOW)],
        compiler_params=pltpu.CompilerParams(vmem_limit_bytes=30 << 20),
        cost_estimate=cost(1),
        name="frame_attention",
    )(tok, msg, w_attn, w_attn, vectors)


def framed_kernel(x_ref, out_ref):
    for f in range(FRAMES):
        rows = jnp.concatenate([wide_of(x_ref[f]), jnp.zeros((SPAN - TOK, D), WIDE)], 0)
        out_ref[f * SPAN : (f + 1) * SPAN, :] = narrow(rows)


def framed(x):
    return pl.pallas_call(
        framed_kernel,
        out_shape=shaped(ROWS, D),
        compiler_params=pltpu.CompilerParams(vmem_limit_bytes=10 << 20),
        cost_estimate=cost(1),
        name="framed",
    )(x)


def valid_rows(shape, first=0):
    row = lax.broadcasted_iota(jnp.int32, shape, 0) + first
    return row % SPAN < TOK


def place_parts(place):
    return lax.div(place, 32), lax.rem(lax.div(place, 8), 4), lax.rem(lax.div(place, 2), 4), lax.rem(place, 2)


CHUNK = 768
CHUNKS = FF // CHUNK


def assemble_up(place_ref, held_ref, out_ref, j):
    x, y, _, _ = place_parts(place_ref[0])
    cols = pl.ds(pl.multiple_of(j * CHUNK, CHUNK), CHUNK)
    for k in range(4):
        slabs = [wide_of(held_ref[z, 48 * k : 48 * k + 48, cols]) for z in range(4)]
        for h in range(2):
            row = pl.multiple_of(((x if h == 0 else 1 - x) * 4 + lax.rem(y + 4 - k, 4)) * 96, 96)
            out_ref[pl.ds(row, 96), :] = narrow(jnp.concatenate([v[24 * h : 24 * h + 24] for v in slabs], 0))


def assemble_down(place_ref, held_ref, out_ref, j):
    x, y, _, core = place_parts(place_ref[0])
    side = lax.rem(lax.div(j, 2) + x, 2)
    for who in range(2):
        col = pl.multiple_of((core if who == 0 else 1 - core) * (D // 2), 128)
        for yl in range(2):
            piece = who * 4 + lax.rem(y + 4 - (lax.rem(j, 2) * 2 + yl), 4)
            for pair in range(2):
                slab = wide_of(held_ref[piece, side, 48 * pair : 48 * pair + 48, :])
                parts = [slab[24 * z : 24 * z + 24, q * (D // 2) : (q + 1) * (D // 2)] for z in range(2) for q in range(4)]
                at = yl * 384 + pair * 192
                out_ref[at : at + 192, pl.ds(col, D // 2)] = narrow(jnp.concatenate(parts, 0))


def mlp_kernel(place_ref, kept_ref, g_ref, vec_ref, perm_ref, *refs):
    up_pieces, down_pieces = refs[:2], refs[2:10]
    lay_ref, gk_ref, dup_keep_ref, dup_give_ref, down_keep_ref, down_give_ref, sums_ref, dub_ref = refs[10:18]
    mlp_ref, mlpt_ref, gt_ref, acc_ref, dacc_ref, held_up_ref, held_down_ref, up_ref, down_ref, sems = refs[18:]
    j = pl.program_id(0)
    core_at = lax.rem(place_ref[0], 2)

    def copies():
        for who in range(2):
            col = pl.multiple_of((core_at if who == 0 else 1 - core_at) * (FF // 2), 128)
            yield pltpu.make_async_copy(up_pieces[who], held_up_ref.at[:, :, pl.ds(col, FF // 2)], sems.at[who])
        for n in range(8):
            yield pltpu.make_async_copy(down_pieces[n], held_down_ref.at[n], sems.at[2 + n])

    @pl.when(j == 0)
    def _():
        for copy in copies():
            copy.start()

    @pl.when(j == 0)
    def _():
        for f in range(FRAMES):
            rows = pl.ds(f * SPAN, SPAN)
            normed, _ = normed_of(kept_ref[rows, :])
            mlp_ref[rows, :] = narrow(normed * vec(vec_ref, GAIN2) + vec(vec_ref, SHIFT2))
        mlpt_ref[...] = narrow(mm_t(perm_ref[...], mlp_ref[...]))
        gt_ref[...] = g_ref[...].T
        acc_ref[...] = kept_ref[...] + vec(vec_ref, DOWN_B)
        dacc_ref[...] = jnp.zeros_like(dacc_ref)
        for copy in copies():
            copy.wait()

    assemble_up(place_ref, held_up_ref, up_ref, j)
    assemble_down(place_ref, held_down_ref, down_ref, j)
    mlp = mlp_ref[...]
    g = g_ref[...]
    up = up_ref[...]
    down = down_ref[...]
    hidden = mm(mlp, up) + vec_ref[pl.ds(UP_B + j, 1), :]
    sig = 0.5 * jnp.tanh(0.851 * hidden) + 0.5
    gated = hidden * sig
    act = narrow(gated)
    acc_ref[...] += mm(act, down)
    gact = wide_of(narrow(mm_t(g, down)))
    gh = narrow(gact * (sig + 1.702 * gated * (1.0 - sig)))
    dub_ref[0] = jnp.broadcast_to(jnp.sum(wide_of(gh), 0, keepdims=True), (8, CHUNK))
    dup = narrow(mm(mlpt_ref[...], gh))
    dup_keep_ref[...] = dup[: D // 2]
    dup_give_ref[...] = dup[D // 2 :]
    dacc_ref[...] += mm_t(gh, up)
    ddown = narrow(mm(gt_ref[...], act).T)
    for core in range(2):

        @pl.when(core_at == core)
        def _():
            for yl in range(2):
                for z in range(4):
                    at = (yl * 4 + z) * 2
                    down_keep_ref[yl, z, 0] = ddown[(at + core) * 48 : (at + core + 1) * 48]
                    down_give_ref[yl, z, 0] = ddown[(at + 1 - core) * 48 : (at + 2 - core) * 48]

    @pl.when(j == CHUNKS - 1)
    def _():
        for f in range(FRAMES):
            lay_ref[f] = narrow(acc_ref[f * SPAN : f * SPAN + TOK, :])
        dg = jnp.zeros((1, D), WIDE)
        dsh = jnp.zeros((1, D), WIDE)
        db = jnp.zeros((1, D), WIDE)
        for f in range(FRAMES):
            rows = pl.ds(f * SPAN, SPAN)
            normed, inverse = normed_of(kept_ref[rows, :])
            gm = dacc_ref[rows, :]
            gw = wide_of(g_ref[rows, :])
            dg += jnp.sum(gm * normed, 0, keepdims=True)
            dsh += jnp.sum(gm, 0, keepdims=True)
            db += jnp.sum(gw, 0, keepdims=True)
            gk = gw + norm_back(gm, normed, inverse, vec(vec_ref, GAIN2))
            gk_ref[rows, :] = jnp.where(valid_rows(gk.shape), gk, 0.0)
        sums_ref[...] = jnp.concatenate([dg, dsh, db, jnp.zeros((5, D), WIDE)], 0)


def once(shape):
    return pl.BlockSpec(shape, lambda *_: (0,) * len(shape), pipeline_mode=pl.Buffered(1))


def mlp(place, kept, grads, up, down, vectors, perm):
    down_spec = pl.BlockSpec((2, 4, 1, 48, D), lambda j: (j % 2, 0, j // 2, 0, 0))
    up_spec = pl.BlockSpec((D // 2, CHUNK), lambda j: (0, j))
    anywhere = pl.BlockSpec(memory_space=pltpu.HBM)
    return pl.pallas_call(
        mlp_kernel,
        grid=(CHUNKS,),
        in_specs=[pl.BlockSpec(memory_space=pltpu.SMEM), once((ROWS, D)), once((ROWS, D)),
                  once((VECTOR_ROWS, D)), once((D, D))] + [anywhere] * 10,
        out_specs=[once((FRAMES, TOK, D)), once((ROWS, D)),
                   up_spec, up_spec, down_spec, down_spec,
                   once((8, D)), pl.BlockSpec((1, 8, CHUNK), lambda j: (j, 0, 0))],
        out_shape=(shaped(FRAMES, TOK, D), shaped(ROWS, D, dtype=WIDE), shaped(D // 2, FF), shaped(D // 2, FF),
                   shaped(4, 4, 2, 48, D), shaped(4, 4, 2, 48, D), shaped(8, D, dtype=WIDE),
                   shaped(CHUNKS, 8, CHUNK, dtype=WIDE)),
        scratch_shapes=[pltpu.VMEM((ROWS, D), LOW), pltpu.VMEM((D, ROWS), LOW), pltpu.VMEM((D, ROWS), LOW),
                        pltpu.VMEM((ROWS, D), WIDE), pltpu.VMEM((ROWS, D), WIDE),
                        pltpu.VMEM((4, 192, FF), LOW), pltpu.VMEM((8, 2, 96, 1536), LOW),
                        pltpu.VMEM((D, CHUNK), LOW), pltpu.VMEM((CHUNK, D), LOW), pltpu.SemaphoreType.DMA((10,))],
        compiler_params=pltpu.CompilerParams(vmem_limit_bytes=52 << 20),
        cost_estimate=cost(1),
        name="mlp_both_ways",
    )(place.reshape(1), kept, grads, vectors, perm, *up, *down)


def head_sums(go, o):
    t = wide_of(go) * wide_of(o)
    high = narrow(t)
    rest = narrow(t - wide_of(high))
    head = lax.broadcasted_iota(jnp.int32, (16, D), 0)
    lane = lax.broadcasted_iota(jnp.int32, (16, D), 1)
    pick = jnp.where((lane // HEAD_DIM) == head, 1.0, 0.0).astype(LOW)
    return mm_t(pick, high) + mm_t(pick, rest)


def out_back_kernel(gk_ref, mixed_ref, wout_ref, perm_ref, gmix_ref, dout_ref, sum_ref):
    gb = narrow(gk_ref[...])
    gmix_ref[...] = narrow(mm_t(gb, wout_ref[...]))
    turned = narrow(mm_t(perm_ref[...], mixed_ref[...]))
    dout_ref[...] = narrow(mm(turned, gb))
    sum_ref[...] = jnp.broadcast_to(jnp.sum(wide_of(gb), 0, keepdims=True), (8, D))


def out_back(gk, mixed, w_attn, perm):
    return pl.pallas_call(
        out_back_kernel,
        grid=(1,),
        in_specs=[whole(gk.shape), whole(mixed.shape), qkv_out_specs()[1], whole(perm.shape)],
        out_specs=(whole((ROWS, D)), whole((D, D)), whole((8, D))),
        out_shape=(shaped(ROWS, D), shaped(D, D), shaped(8, D, dtype=WIDE)),
        compiler_params=pltpu.CompilerParams(vmem_limit_bytes=20 << 20),
        cost_estimate=cost(1),
        name="attention_out_back",
    )(gk, mixed, w_attn, perm)


def attn_bwd_kernel(gmix_ref, mixed_ref, qkv_ref, lse_ref, msg_ref, wqkv_ref, vec_ref,
                    dqkv_ref, sums_ref, gmsg_ref,
                    kt_ref, dqt_ref, rows_ref):
    def frame(f, _):
        rows = pl.ds(pl.multiple_of(f * SPAN, SPAN), SPAN)
        kt_ref[...] = qkv_ref[rows, D : 2 * D].T
        dots = head_sums(gmix_ref[rows, :], mixed_ref[rows, :])
        for p in range(PAIRS):
            cols = lambda part: slice(part * D + p * 128, part * D + (p + 1) * 128)
            q, k, v = (qkv_ref[rows, cols(i)] for i in range(3))
            go = gmix_ref[rows, cols(0)]
            lse = [lse_ref[f, 2 * p + h : 2 * p + h + 1, :] for h in range(2)]
            dot = [dots[2 * p + h : 2 * p + h + 1, :] for h in range(2)]
            dqt, dk, dv = attend_bwd(q, k, v, kt_ref[cols(0), :], go, lse, dot, frame_mask)
            dqt_ref[cols(0), :] = dqt
            dqkv_ref[rows, cols(1)] = dk
            dqkv_ref[rows, cols(2)] = dv
        dqkv_ref[rows, :D] = dqt_ref[...].T
        return 0

    lax.fori_loop(0, FRAMES, frame, 0)
    dqb = jnp.zeros((1, D), WIDE)
    dvb = jnp.zeros((1, D), WIDE)
    for f in range(FRAMES):
        rows = pl.ds(f * SPAN, SPAN)
        dqb += jnp.sum(wide_of(dqkv_ref[rows, :D]), 0, keepdims=True)
        dvb += jnp.sum(wide_of(dqkv_ref[rows, 2 * D :]), 0, keepdims=True)
        tile = wide_of(dqkv_ref[f * SPAN + 192 : f * SPAN + 208, :])
        rows_ref[f : f + 1, :] = tile[TOK - 192 : TOK - 191, :]
    rows_ref[FRAMES:, :] = jnp.zeros((8 - FRAMES, 3 * D), WIDE)
    sums_ref[...] = jnp.concatenate([dqb, dvb, jnp.zeros((6, D), WIDE)], 0)
    back = mm_t(narrow(rows_ref[...]), wqkv_ref[...])
    normed, inverse = normed_of(msg_ref[...])
    gmsg_ref[...] = norm_back(back[:FRAMES], normed, inverse, vec(vec_ref, GAIN1))


def attn_bwd(gmix, mixed, qkv, lse, msg, w_attn, vectors):
    return pl.pallas_call(
        attn_bwd_kernel,
        grid=(1,),
        in_specs=[whole(gmix.shape), whole(mixed.shape), whole(qkv.shape), whole(lse.shape), whole(msg.shape),
                  qkv_out_specs()[0], whole(vectors.shape)],
        out_specs=(whole((ROWS, 3 * D)), whole((8, D)), whole((FRAMES, D))),
        out_shape=(shaped(ROWS, 3 * D), shaped(8, D, dtype=WIDE), shaped(FRAMES, D, dtype=WIDE)),
        scratch_shapes=[pltpu.VMEM((D, SPAN), LOW), pltpu.VMEM((D, SPAN), LOW), pltpu.VMEM((8, 3 * D), WIDE)],
        compiler_params=pltpu.CompilerParams(vmem_limit_bytes=44 << 20),
        cost_estimate=cost(1),
        name="frame_attention_back",
    )(gmix, mixed, qkv, lse, msg, w_attn, vectors)


def tokens_back_kernel(dqkv_ref, wqkv_ref, gk_ref, tok_ref, msg_ref, vec_ref, blk_ref, perm_ref, dout_ref,
                       sum_out_ref, sums_mlp_ref, placed_ref, out_ref, keep_ref, give_ref, joined_ref):
    turned = narrow(mm_t(perm_ref[...], blk_ref[...]))
    for n in range(3):
        cols = slice(n * D, (n + 1) * D)
        dw = narrow(mm(turned, dqkv_ref[:, cols]))
        keep_ref[:, cols] = dw[: D // 2]
        give_ref[:, cols] = dw[D // 2 :]
    keep_ref[:, 3 * D : FF] = dout_ref[: D // 2]
    give_ref[:, 3 * D : FF] = dout_ref[D // 2 :]
    fill_joined(tok_ref, msg_ref, joined_ref)
    dg = jnp.zeros((1, D), WIDE)
    dsh = jnp.zeros((1, D), WIDE)
    back_all = mm_t(dqkv_ref[...], wqkv_ref[...])
    for f in range(FRAMES):
        rows = pl.ds(f * SPAN, SPAN)
        back = back_all[f * SPAN : (f + 1) * SPAN]
        normed, inverse = normed_of(joined_ref[rows, :])
        dg += jnp.sum(back * normed, 0, keepdims=True)
        dsh += jnp.sum(back, 0, keepdims=True)
        full = gk_ref[rows, :] + norm_back(back, normed, inverse, vec(vec_ref, GAIN1))
        out_ref[f] = full[:TOK]
    sums = jnp.concatenate(
        [dg, dsh, sum_out_ref[:1, :], sums_mlp_ref[:3, :], placed_ref[...], jnp.zeros((116, D), WIDE)], 0
    )
    turned = narrow(mm_t(perm_ref[...], narrow(sums)))
    keep_ref[:, FF:] = turned[: D // 2]
    give_ref[:, FF:] = turned[D // 2 :]


def tokens_back(dqkv, w_attn, gk, tok, msg, vectors, blk, perm, dout, sum_out, sums_mlp, placed):
    return pl.pallas_call(
        tokens_back_kernel,
        grid=(1,),
        in_specs=[whole(dqkv.shape), qkv_out_specs()[0], whole(gk.shape), whole(tok.shape), whole(msg.shape),
                  whole(vectors.shape), whole(blk.shape), whole(perm.shape), whole(dout.shape),
                  whole(sum_out.shape), whole(sums_mlp.shape), whole(placed.shape)],
        out_specs=(whole((FRAMES, TOK, D)), whole((D // 2, FF + 128)), whole((D // 2, FF + 128))),
        out_shape=(shaped(FRAMES, TOK, D, dtype=WIDE), shaped(D // 2, FF + 128), shaped(D // 2, FF + 128)),
        scratch_shapes=[pltpu.VMEM((ROWS, D), WIDE)],
        compiler_params=pltpu.CompilerParams(vmem_limit_bytes=42 << 20),
        cost_estimate=cost(1),
        name="tokens_back",
    )(dqkv, w_attn, gk, tok, msg, vectors, blk, perm, dout, sum_out, sums_mlp, placed)


ALL = 256


def group_mask(grow_ref, gcol_ref):
    same = gcol_ref[:, 0:1] == grow_ref[0:1, :]

    def mask(s):
        return jnp.where(same, s, -1000000000.0)

    return mask


def msg_fwd_kernel(cls_ref, w_ref, vec_ref, grow_ref, gcol_ref,
                   message_ref, token_ref, min_ref, qkv_ref, mixed_ref, lse_ref, vt_ref, ot_ref):
    message = mm(cls_ref[...], w_ref[:, :D]) + vec(vec_ref, FC_B)
    message_ref[...] = message
    normed, _ = normed_of(message)
    min_ref[...] = narrow(normed * vec(vec_ref, MSG_GAIN) + vec(vec_ref, MSG_SHIFT))
    for n in range(9):
        y = mm(min_ref[...], w_ref[:, D + n * 256 : D + (n + 1) * 256])
        if n < 3:
            y = y + vec_ref[MQ_B : MQ_B + 1, n * 256 : (n + 1) * 256]
        if n >= 6:
            y = y + vec_ref[MV_B : MV_B + 1, (n - 6) * 256 : (n - 5) * 256]
        qkv_ref[:, n * 256 : (n + 1) * 256] = narrow(y)
    vt_ref[...] = qkv_ref[:, 2 * D :].T
    mask = group_mask(grow_ref, gcol_ref)
    lse_ref[...] = jnp.zeros_like(lse_ref)
    for p in range(PAIRS):
        q = qkv_ref[:, p * 128 : (p + 1) * 128]
        k = qkv_ref[:, D + p * 128 : D + (p + 1) * 128]
        vt = vt_ref[p * 128 : (p + 1) * 128, :]
        for h, (o, l) in enumerate(attend_fwd(q, k, vt, None, mask)):
            at = p * 128 + h * HEAD_DIM
            ot_ref[at : at + HEAD_DIM, :] = narrow(o)
            lse_ref[2 * p + h : 2 * p + h + 1, :] = l
    mixed_ref[...] = ot_ref[...].T
    token_ref[...] = message + mm(mixed_ref[...], w_ref[:, 4 * D :]) + vec(vec_ref, MOUT_B)


def msg_fwd(cls, w, vectors, grow, gcol):
    return pl.pallas_call(
        msg_fwd_kernel,
        out_shape=(shaped(ALL, D, dtype=WIDE), shaped(ALL, D, dtype=WIDE), shaped(ALL, D), shaped(ALL, 3 * D),
                   shaped(ALL, D), shaped(16, ALL, dtype=WIDE)),
        scratch_shapes=[pltpu.VMEM((D, ALL), LOW), pltpu.VMEM((D, ALL), LOW)],
        compiler_params=pltpu.CompilerParams(vmem_limit_bytes=20 << 20),
        cost_estimate=cost(1),
        name="message_forward",
    )(cls, w, vectors, grow, gcol)


def msg_bwd_kernel(gm_ref, cls_ref, message_ref, min_ref, qkv_ref, mixed_ref, lse_ref, w_ref, vec_ref,
                   grow_ref, gcol_ref, pick_ref,
                   gcls_ref, dw_ref, sums_ref,
                   gmix_ref, kt_ref, dqt_ref, dqkv_ref):
    gb = gm_ref[...]
    pick = pick_ref[...]
    turned = lambda x: narrow(mm_t(pick, x))
    gmix_ref[...] = narrow(mm_t(gb, w_ref[:, 4 * D :]))
    dw_ref[:, 4 * D :] = mm(turned(mixed_ref[...]), gb)
    kt_ref[...] = qkv_ref[:, D : 2 * D].T
    mask = group_mask(grow_ref, gcol_ref)
    dots = head_sums(gmix_ref[...], mixed_ref[...])
    for p in range(PAIRS):
        cols = lambda part: slice(part * D + p * 128, part * D + (p + 1) * 128)
        q, k, v = (qkv_ref[:, cols(i)] for i in range(3))
        go = gmix_ref[:, cols(0)]
        lse = [lse_ref[2 * p + h : 2 * p + h + 1, :] for h in range(2)]
        dot = [dots[2 * p + h : 2 * p + h + 1, :] for h in range(2)]
        dqt, dk, dv = attend_bwd(q, k, v, kt_ref[cols(0), :], go, lse, dot, mask)
        dqt_ref[cols(0), :] = dqt
        dqkv_ref[:, cols(1)] = dk
        dqkv_ref[:, cols(2)] = dv
    dqkv_ref[:, :D] = dqt_ref[...].T
    dqkv = dqkv_ref[...]
    dw_ref[:, D : 4 * D] = mm(turned(min_ref[...]), dqkv)
    back = mm_t(dqkv, w_ref[:, D : 4 * D])
    normed, inverse = normed_of(message_ref[...])
    gfc = narrow(wide_of(gb) + norm_back(back, normed, inverse, vec(vec_ref, MSG_GAIN)))
    dw_ref[:, :D] = mm(turned(cls_ref[...]), gfc)
    gcls_ref[...] = mm_t(gfc, w_ref[:, :D])
    col = lambda x: jnp.sum(wide_of(x), 0, keepdims=True)
    sums_ref[...] = jnp.concatenate(
        [col(gfc), col(back * normed), col(back), col(gb), col(dqkv[:, :D]), col(dqkv[:, 2 * D :]),
         jnp.zeros((2, D), WIDE)], 0)


def msg_bwd(gm, cls, message, mins, qkv, mixed, lse, w, vectors, grow, gcol, pick):
    return pl.pallas_call(
        msg_bwd_kernel,
        out_shape=(shaped(ALL, D, dtype=WIDE), shaped(16, 5 * D, dtype=WIDE), shaped(8, D, dtype=WIDE)),
        scratch_shapes=[pltpu.VMEM((ALL, D), LOW), pltpu.VMEM((D, ALL), LOW), pltpu.VMEM((D, ALL), LOW),
                        pltpu.VMEM((ALL, 3 * D), LOW)],
        compiler_params=pltpu.CompilerParams(vmem_limit_bytes=48 << 20),
        cost_estimate=cost(1),
        name="message_back",
    )(gm, cls, message, mins, qkv, mixed, lse, w, vectors, grow, gcol, pick)


def frame_of(x_hi, y, z, core):
    return ((x_hi * 4 + y) * 4 + z) * 2 + core


PLACES = list(itertools.product(range(2), range(4), range(4), range(2), range(2)))


def moves(to):
    return [(frame_of(*p[:4]) * 2 + p[4], frame_of(*to(*p)[:4]) * 2 + to(*p)[4]) for p in PLACES]


TO_CORE = moves(lambda x, y, z, c, v: (x, y, z, 1 - c, v))
TO_VIDEO = moves(lambda x, y, z, c, v: (x, y, z, c, 1 - v))
TO_HALF = moves(lambda x, y, z, c, v: (1 - x, y, z, c, v))
TO_BOTH = moves(lambda x, y, z, c, v: (1 - x, y, z, c, 1 - v))
TO_Y = [moves(lambda x, y, z, c, v, k=k: (x, (y + k) % 4, z, c, v)) for k in range(4)]
TO_Z = [moves(lambda x, y, z, c, v, k=k: (x, y, (z + k) % 4, c, v)) for k in range(4)]
ALONG_Y = [[frame_of(x, y, z, c) for y in range(4)] for x in range(2) for z in range(4) for c in range(2)]
ALONG_Z = [[frame_of(x, y, z, c) for z in range(4)] for x in range(2) for y in range(4) for c in range(2)]
PLANE = [[frame_of(x, y, z, c) for y in range(4) for z in range(4)] for x in range(2) for c in range(2)]
def sent(x, pairs):
    return lax.ppermute(x, ("frame", "video"), pairs)


def to_everyone(x):
    return lax.all_to_all(jnp.broadcast_to(x[None], (64, *x.shape)), "frame", 0, 0, tiled=True)


def assemble_y_kernel(place_ref, *refs):
    pieces, out_ref, sems = refs[:8], refs[8], refs[9]
    x, y, _, core = place_parts(place_ref[0])
    span, half = 96, 1536
    copies = []
    for who in range(2):
        col = pl.multiple_of((core if who == 0 else 1 - core) * half, 128)
        for k in range(4):
            for h in range(2):
                row = pl.multiple_of(((x if h == 0 else 1 - x) * 4 + lax.rem(y + 4 - k, 4)) * span, span)
                copies.append(
                    pltpu.make_async_copy(
                        pieces[who * 4 + k].at[h],
                        out_ref.at[pl.ds(row, span), pl.ds(col, half)],
                        sems.at[len(copies)],
                    )
                )
                copies[-1].start()
    for done in copies:
        done.wait()


def assemble_z_kernel(place_ref, *refs):
    pieces, out_ref, held_ref, sems = refs[:-3], refs[-3], refs[-2], refs[-1]
    x, y, z, core = place_parts(place_ref[0])
    each = len(pieces) // 2
    half = pieces[0].shape[-1]
    copies = []
    for n, piece_ref in enumerate(pieces):
        col = pl.multiple_of((core if n < each else 1 - core) * half, 128)
        copies.append(pltpu.make_async_copy(piece_ref, held_ref.at[n % 4, :, pl.ds(col, half)], sems.at[n]))
        copies[-1].start()
    for done in copies:
        done.wait()
    for cols in range(0, 2 * half, D):
        for k in range(4):
            slabs = [
                wide_of(held_ref[lax.rem(z + 4 - to, 4), 48 * k : 48 * k + 48, cols : cols + D])
                for to in range(4)
            ]
            for h in range(2):
                row = pl.multiple_of(((x if h == 0 else 1 - x) * 4 + lax.rem(y + 4 - k, 4)) * 96, 96)
                out_ref[pl.ds(row, 96), cols : cols + D] = narrow(
                    jnp.concatenate([v[24 * h : 24 * h + 24] for v in slabs], 0)
                )


def assembled(kernel, place, pieces, out, scratch):
    anywhere = pl.BlockSpec(memory_space=pltpu.HBM)
    return pl.pallas_call(
        kernel,
        in_specs=[pl.BlockSpec(memory_space=pltpu.SMEM)] + [anywhere] * len(pieces),
        out_shape=out,
        scratch_shapes=scratch,
        compiler_params=pltpu.CompilerParams(vmem_limit_bytes=24 << 20),
        cost_estimate=cost(1),
        name="assemble_weights",
    )(place.reshape(1), *pieces)


def assemble_y(place, pieces):
    return assembled(assemble_y_kernel, place, pieces, shaped(D, FF), [pltpu.SemaphoreType.DMA((16,))])


def assemble_z(place, pieces):
    half = pieces[0].shape[-1]
    scratch = [pltpu.VMEM((4, 192, 2 * half), LOW), pltpu.SemaphoreType.DMA((len(pieces),))]
    return assembled(assemble_z_kernel, place, pieces, shaped(D, 2 * half), scratch)


def pack_kernel(place_ref, qkv_ref, out_ref, fc_ref, mqkv_ref, mout_ref, up_ref, down_ref, mine_ref, give_ref,
                down_mine_ref, down_give_ref):
    def put(which, to_ref, down_to_ref):
        parts = (
            (qkv_ref[:, :1536], fc_ref[...], mqkv_ref[:, :1152], up_ref[:, :1536]),
            (qkv_ref[:, 1536:], out_ref[...], mqkv_ref[:, 1152:], mout_ref[...], up_ref[:, 1536:]),
        )[which]
        to_ref[...] = jnp.concatenate(parts, 1)
        down_to_ref[...] = down_ref[:, which * 384 : which * 384 + 384]

    for core in range(2):

        @pl.when(lax.rem(place_ref[0], 2) == core)
        def _():
            put(core, mine_ref, down_mine_ref)
            put(1 - core, give_ref, down_give_ref)


def packed(place, *shards):
    mine, give, down_mine, down_give = pl.pallas_call(
        pack_kernel,
        in_specs=[pl.BlockSpec(memory_space=pltpu.SMEM)] + [pl.BlockSpec(memory_space=pltpu.VMEM)] * 7,
        out_shape=(shaped(12, 4992), shaped(12, 4992), shaped(48, 384), shaped(48, 384)),
        cost_estimate=cost(1),
        name="pack_weights",
    )(place.reshape(1), *shards)
    return (mine, give), (down_mine, down_give)


def core_pair(place, halves):
    mine, got = halves[0], sent(halves[1], TO_CORE)
    return jnp.where(place % 2 == 0, jnp.concatenate([mine, got], 0), jnp.concatenate([got, mine], 0))


def both_x(pair):
    return jnp.stack([pair, sent(pair, TO_HALF)])


def ring_z(pair):
    return jnp.swapaxes(from_z(jnp.broadcast_to(pair[None], (4, *pair.shape))), 0, 1).reshape(2, -1, pair.shape[2])


def ring_y(pair):
    return jnp.stack([pair, *(sent(pair, TO_Y[k]) for k in range(1, 4))]).reshape(192, -1)


def around(x, moves_by):
    return [x, *(sent(x, moves_by[k]) for k in range(1, 4))]


def from_z(copies):
    return lax.all_to_all(copies, "frame", 0, 0, axis_index_groups=ALONG_Z, tiled=True)


def both_cores(pieces):
    return [*pieces, *(sent(x, TO_CORE) for x in pieces)]


def after(x, *others):
    return lax.optimization_barrier((x, *others))


def row_order(place):
    row = jnp.arange(D, dtype=jnp.int32)
    r, x, z, y, c = row % 12, row // 12 % 2, row // 24 % 4, row // 96 % 4, row // 384
    natural = ((((x * 4 + y) * 4 + z) * 2) + jnp.where(c == 0, place % 2, 1 - place % 2)) * 12 + r
    return (natural[:, None] == row[None, :]).astype(LOW)


def add_pack_kernel(keep_up, got_up, keep_down, got_down, out_ref):
    up = wide_of(keep_up[...]) + wide_of(got_up[...])
    down = wide_of(keep_down[0]) + wide_of(got_down[0])
    for i in range(2):
        out_ref[i, :, :FF] = narrow(up[24 * i : 24 * i + 24])
        slab = jnp.concatenate([down[i, 0], down[i, 1]], 0)
        for q in range(4):
            both = [slab[48 * h + 12 * q : 48 * h + 12 * q + 12] for h in range(2)]
            out_ref[i, :, FF + q * D : FF + (q + 1) * D] = narrow(jnp.concatenate(both, 0))


def add_pack(keep_up, got_up, keep_down, got_down):
    down_spec = pl.BlockSpec((1, 2, 2, 48, D), lambda i: (i // 2, i % 2, 0, 0, 0))
    up_spec = pl.BlockSpec((48, FF), lambda i: (i, 0))
    return pl.pallas_call(
        add_pack_kernel,
        grid=(8,),
        in_specs=[up_spec, up_spec, down_spec, down_spec],
        out_specs=pl.BlockSpec((2, 24, 2 * FF), lambda i: (i, 0, 0)),
        out_shape=shaped(16, 24, 2 * FF),
        compiler_params=pltpu.CompilerParams(vmem_limit_bytes=14 << 20),
        cost_estimate=cost(1),
        name="add_mlp_gradients",
    )(keep_up, got_up, keep_down, got_down)


def ring_sum(parts, groups):
    return lax.psum_scatter(parts, "frame", scatter_dimension=0, axis_index_groups=groups, tiled=True)


def plane_sum(parts):
    got = lax.all_to_all(parts, "frame", 0, 0, axis_index_groups=PLANE, tiled=True)
    return narrow(jnp.sum(wide_of(got), 0))


def last_kernel(mine_ref, video_ref, half_ref, both_ref, *out_refs):
    total = wide_of(mine_ref[...]) + wide_of(video_ref[...]) + wide_of(half_ref[...]) + wide_of(both_ref[...])
    at = 0
    for out_ref in out_refs:
        out_ref[...] = total[:, at : at + out_ref.shape[1]]
        at += out_ref.shape[1]


def last_sums(rows, half, widths):
    mine, other = (lax.dynamic_slice_in_dim(rows, which * 12, 12, 0) for which in (half, 1 - half))
    return pl.pallas_call(
        last_kernel,
        out_shape=tuple(shaped(12, w, dtype=WIDE) for w in widths),
        cost_estimate=cost(1),
        name="last_sums",
    )(mine, sent(mine, TO_VIDEO), sent(other, TO_HALF), sent(other, TO_BOTH))


def shards(
    tokens_in,
    clip_ids,
    grad_out,
    msg_fc_w,
    msg_fc_b,
    msg_norm_gain,
    msg_norm_shift,
    msg_qkv_w,
    msg_qv_b,
    msg_out_w,
    msg_out_b,
    norm1_gain,
    norm1_shift,
    attn_qkv_w,
    attn_qv_b,
    attn_out_w,
    attn_out_b,
    norm2_gain,
    norm2_shift,
    mlp_in_w,
    mlp_in_b,
    mlp_out_w,
    mlp_out_b,
):
    place = lax.axis_index("frame").astype(jnp.int32)
    core, half = place % 2, place // 32
    tok = tokens_in[0]
    small = jnp.concatenate(
        [
            tok[:, 0, :].reshape(-1),
            msg_fc_b,
            msg_norm_gain,
            msg_norm_shift,
            msg_out_b,
            norm1_gain,
            norm1_shift,
            attn_out_b,
            norm2_gain,
            norm2_shift,
            mlp_out_b,
            msg_qv_b,
            attn_qv_b,
            mlp_in_b,
            clip_ids[0].astype(LOW),
        ]
    )
    small = jnp.pad(small, (0, 4096 - small.shape[0])).reshape(32, 128)
    w_halves, down_halves = packed(
        place, attn_qkv_w, attn_out_w, msg_fc_w, msg_qkv_w, msg_out_w, mlp_in_w, mlp_out_w
    )
    w_pair = core_pair(place, w_halves)
    down_pair = core_pair(place, down_halves).reshape(4, 24, 384).transpose(1, 0, 2).reshape(24, 1536)
    w_x = both_x(jnp.concatenate([w_pair[:, :1536], down_pair, w_pair[:, 1536:]], 1))
    by_y, by_z = ring_z(w_x[:, :, :3072]), ring_y(w_x[:, :, 3072:])
    by_y, by_z, small = after(by_y, by_z, small)
    small_all = to_everyone(small)
    attn = by_y[:, :, :1536]
    attn_last, late_z = after(attn, jnp.broadcast_to(by_z[None, :, 1920:], (4, 192, 1536)))
    msg_all = around(by_z[:, :1920], TO_Z)
    attn_all = [attn, sent(attn_last, TO_Y[1]), sent(attn, TO_Y[2]), sent(attn, TO_Y[3])]
    msg_all, attn_all, small_all, late_y, late_z, grads = after(
        msg_all, attn_all, small_all, by_y[:, :, 1536:], late_z, framed(grad_out[0])
    )
    up_all, down_all = [from_z(late_z)], around(late_y, TO_Y)
    small_all = small_all.reshape(64, 4096)
    cls = small_all[:, :3072].reshape(ALL, D)
    at = 3072
    vectors = small_all[:, at : at + 120].reshape(64, 10, 12).transpose(1, 0, 2).reshape(10, D)
    biases = [small_all[:, at + 120 + a : at + 120 + b].reshape(-1, D) for a, b in ((0, 24), (24, 48), (48, 96))]
    vectors = wide_of(jnp.concatenate([vectors, *biases, jnp.zeros((VECTOR_ROWS - 18, D), LOW)], 0))
    at = at + 216
    groups = wide_of(small_all[:, at : at + 4].reshape(ALL))
    grow = jnp.broadcast_to(groups[None], (8, ALL))
    gcol = jnp.broadcast_to(groups[:, None], (ALL, 128))
    order = row_order(place)
    pick_row = jnp.arange(16, dtype=jnp.int32)[:, None]
    pick_col = jnp.arange(D, dtype=jnp.int32)[None, :]
    pick = ((pick_row < 12) & (pick_col == place * 12 + pick_row)).astype(LOW)

    msg_all, vectors, order, pick, cls, grow, gcol = after(msg_all, vectors, order, pick, cls, grow, gcol)
    w_msg = assemble_z(place, both_cores(msg_all))
    message, token, mins, mqkv, mmixed, mlse = msg_fwd(cls, w_msg, vectors, grow, gcol)
    token, attn_all = after(token, attn_all)
    w_attn = assemble_y(place, both_cores(attn_all))
    msg = lax.dynamic_slice_in_dim(token, place * FRAMES, FRAMES)
    qkv, mixed, kept, lse, blk = attn_fwd(tok, msg, w_attn, vectors)
    kept, up_all, down_all = after(kept, up_all, down_all)
    lay, gk, dup_keep, dup_give, down_keep, down_give, sums_mlp, dub = mlp(
        place, kept, grads, both_cores(up_all), both_cores(down_all), vectors, order
    )
    dup_got, down_got = sent(dup_give, TO_CORE), sent(down_give, TO_CORE)
    gmix, dout, sum_out = out_back(gk, mixed, w_attn, order)
    gmix, dup_got, down_got = after(gmix, dup_got, down_got)
    mlp_parts, gmix = after(add_pack(dup_keep, dup_got, down_keep, down_got), gmix)
    mlp_half = ring_sum(mlp_parts, ALONG_Y)
    dqkv, sums_attn, gmsg = attn_bwd(gmix, mixed, qkv, lse, msg, w_attn, vectors)
    gmsg = jnp.broadcast_to(narrow(gmsg)[None], (64, FRAMES, D))
    gmsg, dqkv = after(gmsg, dqkv)
    gmsg_all = lax.all_to_all(gmsg, "frame", 0, 0, tiled=True).reshape(ALL, D)
    by_place = lambda x, n: x.reshape(64, n, 12).transpose(1, 0, 2).reshape(n, D)
    placed = jnp.concatenate([by_place(sums_attn[:2], 2), by_place(dub[:, 0], 4)], 0)
    grad_tokens, attn_keep, attn_give = tokens_back(dqkv, w_attn, gk, tok, msg, vectors, blk, order, dout, sum_out, sums_mlp, placed)
    attn_keep, attn_give, gmsg_all, mlp_half = after(attn_keep, attn_give, gmsg_all, mlp_half)
    mlp_sum = ring_sum(mlp_half, ALONG_Z).reshape(24, 2 * FF)
    attn_got = sent(attn_give, TO_CORE)
    gcls, dw_msg, sums_msg = msg_bwd(gmsg_all, cls, message, mins, mqkv, mmixed, mlse, w_msg, vectors, grow, gcol, pick)
    attn_got, gcls, dw_msg, sums_msg = after(attn_got, gcls, dw_msg, sums_msg)
    attn_part = narrow(wide_of(attn_keep) + wide_of(attn_got))
    attn_part, lay = after(attn_part, lay)
    attn_part, gcls, dw_msg, sums_msg = after(attn_part, gcls, dw_msg, sums_msg)
    attn_sum = plane_sum(attn_part.reshape(16, 24, FF + 128))
    gcls = lax.dynamic_slice_in_dim(gcls, place * FRAMES, FRAMES)
    grad_tokens = grad_tokens.at[:, 0, :].add(gcls)
    own = lax.dynamic_slice_in_dim(sums_msg[:4], place * 12, 12, 1).reshape(-1)
    own_qv = lax.dynamic_slice_in_dim(sums_msg[4:6].reshape(-1), place * 24, 24)
    own = jnp.concatenate([own, own_qv])
    own = own + sent(own, TO_VIDEO)
    fb, mg, ms, mob, mqvb = jnp.split(own, [12, 24, 36, 48])
    msg_rows = dw_msg[:12]
    msg_rows = msg_rows + wide_of(sent(narrow(msg_rows), TO_VIDEO))
    mlp_sum, msg_rows = after(mlp_sum, msg_rows)
    mlp_rows, *down_rows = last_sums(mlp_sum, half, (FF, D, D, D, D))
    down_rows = jnp.concatenate(down_rows, 0)
    attn_sum, mlp_rows, down_rows = after(attn_sum, mlp_rows, down_rows)
    qkv_rows, out_rows, ends = last_sums(attn_sum, half, (3 * D, D, 128))
    ends = ends[:, :12].T
    g1, s1, ob, g2, s2, db = (ends[k] for k in range(6))
    qvb, ub = ends[6:8].reshape(-1), ends[8:12].reshape(-1)
    return (
        lay[None],
        grad_tokens[None],
        msg_rows[:, :D],
        fb,
        mg,
        ms,
        msg_rows[:, D : 4 * D],
        mqvb,
        msg_rows[:, 4 * D :],
        mob,
        g1,
        s1,
        qkv_rows,
        qvb,
        out_rows,
        ob,
        g2,
        s2,
        mlp_rows,
        ub,
        down_rows,
        db,
    )


def solution(mesh):
    in_specs = (
        P("video", "frame", None, None),
        P("video", "frame"),
        P("video", "frame", None, None),
        P("frame", None),
        P("frame"),
        P("frame"),
        P("frame"),
        P("frame", None),
        P("frame"),
        P("frame", None),
        P("frame"),
        P("frame"),
        P("frame"),
        P("frame", None),
        P("frame"),
        P("frame", None),
        P("frame"),
        P("frame"),
        P("frame"),
        P("frame", None),
        P("frame"),
        P("frame", None),
        P("frame"),
    )
    out_specs = (
        P("video", "frame", None, None),
        P("video", "frame", None, None),
        P("frame", None),
        P("frame"),
        P("frame"),
        P("frame"),
        P("frame", None),
        P("frame"),
        P("frame", None),
        P("frame"),
        P("frame"),
        P("frame"),
        P("frame", None),
        P("frame"),
        P("frame", None),
        P("frame"),
        P("frame"),
        P("frame"),
        P("frame", None),
        P("frame"),
        P("frame", None),
        P("frame"),
    )
    return jax.shard_map(shards, mesh=mesh, in_specs=in_specs, out_specs=out_specs, check_vma=False)
```
